32 devices in a mesh: scen: 8 (over y, x, core), arc: 4 (over z).
Axes of the slice: x: 2, y: 2, z: 4, core: 2. Of those that a mesh axis runs over, the one named last changes fastest.
Arguments:
- coupling: bfloat16 [512, 2048], P(None, 'arc'), may hold values from -0.125 to 0.125
- incidence: int32 [4, 16], P(None, 'arc'), may hold values 0 or 1
- arc_cost: float32 [2048], P('arc'), may hold values from -6 to 6
- capacity: float32 [2048], P('arc'), may hold values from 0.5 to 2
- demand: float32 [8, 512], P('scen'), may hold values from -4 to 4
- weights: int32 [8], P('scen'), may hold values from 8 to 1408, as said below
- fleet_slots: int32 [512], P('arc'), may hold values from 0 to 511, as said below
Outputs:
- flows: float32 [8, 2048], P('scen', 'arc')
- duals: float32 [8, 512], P('scen', 'arc')
- multipliers: float32 [8, 512], P('scen', 'arc')
- consensus: float32 [512], P('arc')
- spread: float32 [2], replicated
The draws below stay inside these ranges and needn't reach their ends.
Inputs may be any that keep to these rules, and one draw needn't show every extreme that they name: `weights`: weight s is (8 + 2 s) times a power of two from 1 to 64. `fleet_slots`: within each aligned block of 128 entries (one arc block) the values are distinct positions inside that arc block.
All inputs are finite; a program needn't handle non-finite values. No bound on the sum of `incidence` on one device may be relied on, other than what follows from the above.
Results may differ from the reference program's by a relative error of at most 0.012.
Values may be sent and summed in bfloat16 or wider, within the bound.
No kernel may reach another device: no remote copies, remote signals or barrier semaphores. Data moves between devices by JAX's collectives and lax.ppermute only.
A program may use at most 64 MiB of HBM per device.

```python
import jax
import jax.numpy as jnp
from jax import lax

A_DEV = 512
TILE = 128
ITERS = 4
ROUNDS = 2
F_DEV = 128
SCEN = 8
NA = 2048
ROWS = 512
NF = 512


def draw_weights(key, part):
    index = jnp.arange(SCEN, dtype=jnp.int32)
    powers = jax.random.randint(key, (SCEN,), 0, 7, dtype=jnp.int32)
    powers = jnp.where(index == 0, 0, jnp.where(index == SCEN - 1, 6, powers)).astype(jnp.int32)
    factor = jnp.left_shift(jnp.ones((SCEN,), jnp.int32), powers)
    return ((SCEN + 2 * index) * factor).astype(jnp.int32)


def draw_fleet_slots(key, part):

    def one_block(block_key):
        first_key, second_key = jax.random.split(block_key)
        inner = jax.random.permutation(first_key, A_DEV - 2)[:F_DEV - 2].astype(jnp.int32) + 1
        values = jnp.concatenate([jnp.array([0, A_DEV - 1], jnp.int32), inner])
        order = jax.random.permutation(second_key, F_DEV).astype(jnp.int32)
        return values[order]
    block_keys = jax.random.split(key, NF // F_DEV)
    return jax.vmap(one_block)(block_keys).reshape(-1).astype(jnp.int32)


def with_ends(drawn, rng, least, largest):
    longest = drawn.shape.index(max(drawn.shape))
    spots = []
    for shift in (0, 1):
        where = [jax.random.randint(jax.random.fold_in(rng, axis), (), 0, length) for axis, length in enumerate(drawn.shape)]
        where[longest] = (where[longest] + shift) % drawn.shape[longest]
        spots.append(tuple(where))
    return drawn.at[spots[0]].set(least).at[spots[1]].set(largest)


def levels(own_key, shape, pieces, least, largest):
    def one(position, shards_of):
        heights = jax.random.uniform(jax.random.fold_in(jax.random.fold_in(own_key, 6), position), (shards_of,), jnp.float32, least / len(pieces), largest / len(pieces))
        return jnp.repeat(jnp.exp(heights), shape[position] // shards_of).reshape((-1,) + (1,) * (len(shape) - position - 1))

    gain = one(*pieces[0])
    for cut in pieces[1:]:
        gain = gain * one(*cut)
    return gain


def noise(own_key, shape, scale, reach, pieces=(), kind=jnp.bfloat16):
    result = jax.random.normal(own_key, shape, jnp.float32) * scale
    if len(pieces) > 0:
        result = levels(own_key, shape, pieces, -0.22, 0.18) * result
    return jnp.clip(result, min=-reach, max=reach).astype(kind)


def setup_inputs(seed: int = 0) -> dict:
    keys = jax.random.split(jax.random.key(seed), 8)
    return {
        "coupling": noise(keys[0], (ROWS, NA), NA ** -0.5, 0.125, ((1, 4),)),
        "incidence": with_ends((jax.random.randint(keys[1], (ROWS // TILE, NA // TILE), 0, 2) < 1).astype(jnp.int32), jax.random.fold_in(keys[1], 1), 0, 1),
        "arc_cost": noise(keys[2], (NA,), 1.0, 6.0, ((0, 4),), jnp.float32),
        "capacity": jnp.clip(0.5 + 1.5 * jax.random.uniform(keys[3], (NA,), jnp.float32) ** levels(keys[3], (NA,), ((0, 4),), -0.2, 0.2), 0.5, 2.0),
        "demand": noise(keys[4], (SCEN, ROWS), 0.5, 4.0, ((0, 8),), jnp.float32),
        "weights": draw_weights(jax.random.fold_in(keys[7], 71), 0),
        "fleet_slots": draw_fleet_slots(jax.random.fold_in(keys[7], 71), 0),
    }


primal_step = 0.9
dual_step = 0.9
penalty = 1.0

def reference(coupling, incidence, arc_cost, capacity, demand, weights, fleet_slots):
    total_rows, total_arcs = coupling.shape
    masked = (coupling.reshape(total_rows // TILE, TILE, total_arcs // TILE, TILE) * incidence.astype(jnp.bfloat16)[:, None, :, None]).reshape(total_rows, total_arcs)
    block_owner = jnp.arange(NF, dtype=jnp.int32) // F_DEV
    slot_index = (fleet_slots + block_owner * A_DEV).astype(jnp.int32)
    shares = weights.astype(jnp.float32)
    weight_sum = jnp.sum(shares)
    flows = jnp.zeros((SCEN, NA), jnp.float32)
    duals = jnp.zeros((SCEN, ROWS), jnp.float32)
    multipliers = jnp.zeros((SCEN, NF), jnp.float32)
    consensus = jnp.zeros((NF,), jnp.float32)
    spreads = []
    for round_index in range(ROUNDS):
        for step_index in range(ITERS):
            dual_pull = jnp.dot(duals.astype(jnp.bfloat16), masked, preferred_element_type=jnp.float32)
            fleet_push = multipliers + penalty * (flows[:, slot_index] - consensus[None, :])
            gradient = (arc_cost[None, :] + dual_pull).at[:, slot_index].add(fleet_push)
            flows_next = jnp.clip(flows - primal_step * gradient, 0.0, capacity[None, :])
            flows_bar = (2.0 * flows_next - flows).astype(jnp.bfloat16)
            row_load = jnp.dot(flows_bar, masked.T, preferred_element_type=jnp.float32)
            duals = jnp.maximum(duals + dual_step * (row_load - demand), 0.0)
            flows = flows_next
        fleet_flow = flows[:, slot_index]
        consensus = lax.optimization_barrier(jnp.sum(shares[:, None] * fleet_flow, axis=0)) / weight_sum
        deviation = fleet_flow - consensus[None, :]
        spreads.append(jnp.sqrt(jnp.sum(shares[:, None] * deviation * deviation) / (weight_sum * NF) + 1e-06))
        multipliers = multipliers + penalty * deviation
    return (flows, duals, multipliers, consensus, jnp.stack(spreads))
```

```python
import functools

import jax
import jax.numpy as jnp
from jax import lax
from jax.experimental import pallas as pl
from jax.experimental.pallas import tpu as pltpu
from jax.sharding import PartitionSpec as P

TILE = 128
ITERS = 4
ROUNDS = 2
EXTRA = 16

primal_step = 0.9
dual_step = 0.9
penalty = 1.0

VMEM = pl.BlockSpec(memory_space=pltpu.VMEM)
SMEM = pl.BlockSpec(memory_space=pltpu.SMEM)
ANY = pl.BlockSpec(memory_space=pl.ANY)


def pieces(value):
    high = value.astype(jnp.bfloat16)
    rest = value - high.astype(jnp.float32)
    middle = rest.astype(jnp.bfloat16)
    low = (rest - middle.astype(jnp.float32)).astype(jnp.bfloat16)
    return high, middle, low


def one_hot(slots, block_arcs):
    arcs = lax.broadcasted_iota(jnp.int32, (block_arcs, slots.shape[1]), 0)
    return jnp.where(arcs == slots, 1.0, 0.0).astype(jnp.bfloat16)


def fleet_mask(slots, block_arcs):
    ones = jnp.ones((8, slots.shape[1]), jnp.bfloat16)
    hits = lax.dot_general(ones, one_hot(slots, block_arcs), (((1,), (1,)), ((), ())),
                           preferred_element_type=jnp.float32)
    return hits[:1]


def own_row(value, scen):
    rows = lax.broadcasted_iota(jnp.int32, value.shape, 0)
    return jnp.sum(jnp.where(rows == scen, value, 0.0), axis=0, keepdims=True)


def pack_kernel(coupling, incidence, arc_cost, capacity, demand, weights, slots,
                near, across, beyond, extra, rows_in, sems):
    total_rows, block_arcs = rows_in.shape
    half = TILE // 2
    scen = lax.axis_index("scen")
    chip, core = scen // 2, lax.rem(scen, 2)
    chips = total_rows // TILE
    copies = []
    for part in range(chips):
        first = pl.multiple_of(jnp.bitwise_xor(chip, part) * TILE, TILE)
        copies.append(pltpu.make_async_copy(
            coupling.at[pl.ds(first, TILE)], rows_in.at[pl.ds(part * TILE, TILE)], sems.at[part]))
    for copy in copies:
        copy.start()
    share = jnp.broadcast_to(weights[...].astype(jnp.float32), (1, 128))
    share = jnp.concatenate([*pieces(share), jnp.zeros((1, 128), jnp.bfloat16)], axis=1)
    mask = fleet_mask(slots[...], block_arcs)
    touch = []
    for part in range(chips):
        owner = jnp.bitwise_xor(chip, part)
        touch.append(jnp.concatenate(
            [jnp.full((1, TILE), incidence[owner, tile].astype(jnp.float32))
             for tile in range(block_arcs // TILE)], axis=1))
    lines = [*pieces(arc_cost[...]), *pieces(capacity[...]), mask, *pieces(demand[...]), share, *touch]
    lines = [line.astype(jnp.float32) for line in lines]
    lines += [jnp.zeros((1, block_arcs), jnp.float32)] * (EXTRA - len(lines))
    lines = jnp.concatenate(lines, axis=0).astype(jnp.bfloat16)
    extra[...] = lines
    across[TILE:, :] = lines
    beyond[half:, :] = lines
    for part in range(chips):
        copies[part].wait()
        rows = slice(part * TILE, (part + 1) * TILE)
        near[rows, :] = rows_in[rows, :] * touch[part].astype(jnp.bfloat16)
    across[:TILE, :] = near[(chips - 1) * TILE:, :]
    beyond[:half, :] = near[pl.ds(pl.multiple_of(core * half, half), half), :]


def rounds(masked, blocks, cost, cap, mask, demand, share, fleet_count, spread_out,
           flows, duals, prices, centre, shifted):
    scenarios, total_rows = demand.shape
    block_arcs = cost.shape[1] // blocks
    weight_sum = jnp.sum(share[:, :1])
    for round_index in range(ROUNDS):
        for step_index in range(ITERS):
            first = round_index == 0 and step_index == 0
            load = jnp.zeros((scenarios, total_rows), jnp.float32)
            if not first:
                duals_low = duals[...].astype(jnp.bfloat16)
            for block in range(blocks):
                cols = slice(block * block_arcs, (block + 1) * block_arcs)
                if first:
                    gradient = jnp.broadcast_to(cost[:, cols], (scenarios, block_arcs))
                    old = jnp.zeros((scenarios, block_arcs), jnp.float32)
                else:
                    old = flows[:, cols]
                    pull = jnp.dot(duals_low, masked(block), preferred_element_type=jnp.float32)
                    push = penalty * mask[:, cols] * old
                    if round_index > 0:
                        push = push + shifted[:, cols]
                    gradient = cost[:, cols] + pull + push
                new = jnp.clip(old - primal_step * gradient, 0.0, cap[:, cols])
                flows[:, cols] = new
                bar = (2.0 * new - old).astype(jnp.bfloat16)
                load = load + lax.dot_general(bar, masked(block), (((1,), (1,)), ((), ())),
                                              preferred_element_type=jnp.float32)
            step = dual_step * (load - demand[...])
            duals[...] = jnp.maximum(step if first else duals[...] + step, 0.0)
        squares = jnp.float32(0.0)
        for block in range(blocks):
            cols = slice(block * block_arcs, (block + 1) * block_arcs)
            fleet = flows[:, cols] * mask[:, cols]
            share_col = share[:, :1]
            mean = jnp.sum(share_col * fleet, axis=0, keepdims=True) / weight_sum
            gap = fleet - mean
            squares = squares + jnp.sum(share_col * gap * gap)
            total = penalty * gap if round_index == 0 else prices[:, cols] + penalty * gap
            prices[:, cols] = total
            centre[:, cols] = mean
            shifted[:, cols] = total - penalty * mean
        spread_out[round_index] = jnp.sqrt(squares / (weight_sum * fleet_count) + 1e-06)


def pick_fleet(price, mean, slots):
    picked = [line.astype(jnp.float32) for line in (*pieces(price), *pieces(mean))]
    picked += [jnp.zeros_like(price)] * 2
    picked = jnp.dot(jnp.concatenate(picked, axis=0).astype(jnp.bfloat16),
                     one_hot(slots, price.shape[1]), preferred_element_type=jnp.float32)
    return picked[0:1] + picked[1:2] + picked[2:3], picked[3:4] + picked[4:5] + picked[5:6]


def plain_kernel(masked, cost, cap, mask, demand, share, slots, flows_out, duals_out, mult_out, cons_out,
                 spread_out, flows, duals, prices, centre, shifted):
    blocks, total_rows, block_arcs = masked.shape
    rounds(lambda block: masked[block], blocks, cost, cap, mask, demand, share, slots.shape[1] * blocks,
           spread_out, flows, duals, prices, centre, shifted)
    scen, arc = lax.axis_index("scen"), lax.axis_index("arc")
    own = pl.ds(pl.multiple_of(arc * block_arcs, block_arcs), block_arcs)
    share_rows = total_rows // blocks
    own_rows = pl.ds(pl.multiple_of(arc * share_rows, share_rows), share_rows)
    flows_out[...] = own_row(flows[:, own], scen)
    duals_out[...] = own_row(duals[:, own_rows], scen)
    mult_out[...], cons_out[...] = pick_fleet(own_row(prices[:, own], scen), centre[:, own], slots[...])


def whole_kernel(near, *refs):
    lines, others = refs[:5], refs[5:10]
    (slots, flows_out, duals_out, mult_out, cons_out, spread_out,
     blocks_in, cost, cap, mask, demand_in, demand, share, flows, duals, prices, centre, shifted) = refs[10:]
    total_rows, block_arcs = near.shape
    scen, arc = lax.axis_index("scen"), lax.axis_index("arc")
    chip, core = scen // 2, lax.rem(scen, 2)
    chips = total_rows // TILE
    half = TILE // 2
    tails = [lines[0][TILE + half:, :], lines[3][TILE:, :], others[3][TILE:, :], lines[4][half:, :]]
    touch = []
    for block, tail in enumerate(tails):
        cols = slice(block * block_arcs, (block + 1) * block_arcs)
        tail = tail.astype(jnp.float32)
        cost[:, cols] = tail[0:1] + tail[1:2] + tail[2:3]
        cap[:, cols] = tail[3:4] + tail[4:5] + tail[5:6]
        mask[:, cols] = tail[6:7]
        touch.append(tail[11:11 + chips].astype(jnp.bfloat16))
    for row in range(2 * chips):
        part, source = row // 2, others if row % 2 else lines
        tail = source[part][TILE + half:, :] if part < chips - 1 else source[chips][half:, :]
        tail = tail.astype(jnp.float32)
        demand_in[row:row + 1, :] = tail[7:8] + tail[8:9] + tail[9:10]
        share[row:row + 1, :] = tail[10:11, :128] + tail[10:11, 128:256] + tail[10:11, 256:384]
    for part in range(chips):
        owner = jnp.bitwise_xor(chip, part)
        rows = slice(part * TILE, (part + 1) * TILE)
        demand[:, rows] = demand_in[:, pl.ds(pl.multiple_of(owner * TILE, TILE), TILE)]
        for side, source in enumerate((lines, others)):
            place = jnp.where(core == side, 0, half)
            place = pl.ds(pl.multiple_of(part * TILE + place, half), half)
            if part < chips - 1:
                blocks_in[side, rows, :] = source[part][:TILE, :] * touch[1 + side][part:part + 1]
                on = touch[3][chips - 1 - part:chips - part]
                blocks_in[2, place, :] = source[part][TILE:TILE + half, :] * on
            else:
                blocks_in[side, rows, :] = source[chips - 1][:TILE, :]
                blocks_in[2, place, :] = source[chips][:half, :]

    def masked(block):
        return near[...] if block == 0 else blocks_in[block - 1]

    rounds(masked, len(tails), cost, cap, mask, demand, share, slots.shape[1] * len(tails),
           spread_out, flows, duals, prices, centre, shifted)
    flows_out[...] = flows[0:1, :block_arcs]
    first = pl.multiple_of(jnp.bitwise_xor(chip, arc) * TILE, TILE)
    duals_out[...] = duals[:, pl.ds(first, TILE)][0:1]
    mult_out[...], cons_out[...] = pick_fleet(prices[0:1, :block_arcs], centre[:, :block_arcs], slots[...])


def swap(value, partner):
    scenarios, blocks = lax.axis_size("scen"), lax.axis_size("arc")
    pairs = []
    for scen in range(scenarios):
        for arc in range(blocks):
            other_scen, other_arc = partner(scen, arc)
            pairs.append((scen * blocks + arc, other_scen * blocks + other_arc))
    return lax.ppermute(value, ("scen", "arc"), pairs)


def bring(coupling, across, beyond, extra):
    scen = lax.axis_index("scen")
    half = TILE // 2
    wide = lax.dynamic_slice_in_dim(coupling, lax.shift_right_logical(scen, 1) * TILE, TILE, 0)
    wide = lax.optimization_barrier(wide)
    narrow = lax.dynamic_slice_in_dim(wide, (scen & 1) * half, half, 0)
    wide = swap(wide, lambda scen, arc: (scen, arc ^ (1 + scen % 2)))
    narrow = swap(narrow, lambda scen, arc: (scen, arc ^ 3))
    beyond = swap(beyond, lambda scen, arc: (scen ^ 6, arc ^ 3))
    line = jnp.concatenate([wide, narrow, extra], axis=0)
    line, across = lax.optimization_barrier((line, across))
    side = swap(line, lambda scen, arc: (scen ^ 2, arc))
    front = swap(line, lambda scen, arc: (scen ^ 4, arc))
    across = swap(across, lambda scen, arc: (scen, arc ^ (1 + scen % 2)))
    brought = [line, side, front, across, beyond]
    return brought + [swap(value, lambda scen, arc: (scen ^ 1, arc)) for value in brought]


def body(coupling, incidence, arc_cost, capacity, demand, weights, fleet_slots):
    total_rows, block_arcs = coupling.shape
    scenarios, blocks = lax.axis_size("scen"), lax.axis_size("arc")
    arcs = blocks * block_arcs
    fleet_block = fleet_slots.shape[0]
    row = lambda value: value.reshape(1, -1)
    slots = row(fleet_slots)
    out_shape = (
        jax.ShapeDtypeStruct((1, block_arcs), jnp.float32),
        jax.ShapeDtypeStruct((1, total_rows // blocks), jnp.float32),
        jax.ShapeDtypeStruct((1, fleet_block), jnp.float32),
        jax.ShapeDtypeStruct((1, fleet_block), jnp.float32),
        jax.ShapeDtypeStruct((ROUNDS,), jnp.float32),
    )
    out_specs = (VMEM, VMEM, VMEM, VMEM, SMEM)
    state = [
        pltpu.VMEM((scenarios, arcs), jnp.float32),
        pltpu.VMEM((scenarios, total_rows), jnp.float32),
        pltpu.VMEM((scenarios, arcs), jnp.float32),
        pltpu.VMEM((1, arcs), jnp.float32),
        pltpu.VMEM((scenarios, arcs), jnp.float32),
    ]
    limit = lambda mib: pltpu.CompilerParams(vmem_limit_bytes=mib * 1024 * 1024)
    cost = pl.CostEstimate(
        flops=4 * ROUNDS * ITERS * scenarios * total_rows * arcs,
        bytes_accessed=2 * total_rows * arcs,
        transcendentals=0,
    )
    fits = (scenarios, blocks) == (8, 4)
    if fits and total_rows == TILE * 4:
        like = lambda rows: jax.ShapeDtypeStruct((rows, block_arcs), jnp.bfloat16)
        near, across, beyond, extra = pl.pallas_call(
            pack_kernel,
            out_shape=(like(total_rows), like(TILE + EXTRA), like(TILE // 2 + EXTRA), like(EXTRA)),
            in_specs=[ANY, SMEM, VMEM, VMEM, VMEM, VMEM, VMEM],
            out_specs=(VMEM,) * 4,
            scratch_shapes=[
                pltpu.VMEM((total_rows, block_arcs), jnp.bfloat16),
                pltpu.SemaphoreType.DMA((total_rows // TILE,)),
            ],
            compiler_params=limit(8),
            name="pack",
        )(coupling, incidence, row(arc_cost), row(capacity), demand, weights.reshape(1, 1), slots)
        brought = bring(coupling, across, beyond, extra)
        outs = pl.pallas_call(
            whole_kernel,
            out_shape=out_shape,
            in_specs=[VMEM] * (len(brought) + 2),
            out_specs=out_specs,
            scratch_shapes=[
                pltpu.VMEM((blocks - 1, total_rows, block_arcs), jnp.bfloat16),
                pltpu.VMEM((1, arcs), jnp.float32),
                pltpu.VMEM((1, arcs), jnp.float32),
                pltpu.VMEM((1, arcs), jnp.float32),
                pltpu.VMEM((scenarios, total_rows), jnp.float32),
                pltpu.VMEM((scenarios, total_rows), jnp.float32),
                pltpu.VMEM((scenarios, 128), jnp.float32),
                *state,
            ],
            compiler_params=limit(16),
            cost_estimate=cost,
            name="whole",
        )(near, *brought, slots)
    else:
        masked = (
            coupling.reshape(total_rows // TILE, TILE, block_arcs // TILE, TILE)
            * incidence.astype(jnp.bfloat16)[:, None, :, None]
        ).reshape(total_rows, block_arcs)
        masked = lax.all_gather(masked, "arc")
        own_mask = jnp.zeros((block_arcs,), jnp.float32).at[fleet_slots].set(1.0)
        per_arc = lax.all_gather(jnp.stack([arc_cost, capacity, own_mask]), "arc", axis=1, tiled=True)
        shares = jnp.broadcast_to(weights.astype(jnp.float32)[:, None], (1, 128))
        per_scen = lax.all_gather(jnp.concatenate([demand, shares], axis=1), "scen", tiled=True)
        outs = pl.pallas_call(
            plain_kernel,
            out_shape=out_shape,
            in_specs=[VMEM] * 7,
            out_specs=out_specs,
            scratch_shapes=state,
            compiler_params=limit(48),
            cost_estimate=cost,
            name="whole",
        )(masked, per_arc[0:1], per_arc[1:2], per_arc[2:3], per_scen[:, :total_rows],
          per_scen[:, total_rows:], slots)
    flows, duals, multipliers, consensus, spread = outs
    return flows, duals, multipliers, consensus.reshape(-1), spread


def solution(mesh):
    in_specs = (
        P(None, "arc"),
        P(None, "arc"),
        P("arc"),
        P("arc"),
        P("scen", None),
        P("scen"),
        P("arc"),
    )
    out_specs = (P("scen", "arc"), P("scen", "arc"), P("scen", "arc"), P("arc"), P())
    return jax.shard_map(body, mesh=mesh, in_specs=in_specs, out_specs=out_specs, check_vma=False)
```

```python
import functools

import jax
import jax.numpy as jnp
from jax import lax
from jax.experimental import pallas as pl
from jax.experimental.pallas import tpu as pltpu
from jax.sharding import PartitionSpec as P

TILE = 128
ITERS = 4
ROUNDS = 2
EXTRA = 16

primal_step = 0.9
dual_step = 0.9
penalty = 1.0

VMEM = pl.BlockSpec(memory_space=pltpu.VMEM)
SMEM = pl.BlockSpec(memory_space=pltpu.SMEM)
ANY = pl.BlockSpec(memory_space=pl.ANY)


def pieces(value):
    high = value.astype(jnp.bfloat16)
    rest = value - high.astype(jnp.float32)
    middle = rest.astype(jnp.bfloat16)
    low = (rest - middle.astype(jnp.float32)).astype(jnp.bfloat16)
    return high, middle, low


def one_hot(slots, block_arcs):
    arcs = lax.broadcasted_iota(jnp.int32, (block_arcs, slots.shape[1]), 0)
    return jnp.where(arcs == slots, 1.0, 0.0).astype(jnp.bfloat16)


def fleet_mask(slots, block_arcs):
    ones = jnp.ones((8, slots.shape[1]), jnp.bfloat16)
    hits = lax.dot_general(ones, one_hot(slots, block_arcs), (((1,), (1,)), ((), ())),
                           preferred_element_type=jnp.float32)
    return hits[:1]


def own_row(value, scen):
    rows = lax.broadcasted_iota(jnp.int32, value.shape, 0)
    return jnp.sum(jnp.where(rows == scen, value, 0.0), axis=0, keepdims=True)


def pack_kernel(coupling, incidence, arc_cost, capacity, demand, weights, slots,
                near, across, beyond, extra, rows_in, sems):
    total_rows, block_arcs = rows_in.shape
    half = TILE // 2
    scen = lax.axis_index("scen")
    chip, core = scen // 2, lax.rem(scen, 2)
    chips = total_rows // TILE
    copies = []
    for part in range(chips):
        first = pl.multiple_of(jnp.bitwise_xor(chip, part) * TILE, TILE)
        copies.append(pltpu.make_async_copy(
            coupling.at[pl.ds(first, TILE)], rows_in.at[pl.ds(part * TILE, TILE)], sems.at[part]))
    for copy in copies:
        copy.start()
    share = jnp.broadcast_to(weights[...].astype(jnp.float32), (1, 128))
    share = jnp.concatenate([*pieces(share), jnp.zeros((1, 128), jnp.bfloat16)], axis=1)
    mask = fleet_mask(slots[...], block_arcs)
    touch = []
    for part in range(chips):
        owner = jnp.bitwise_xor(chip, part)
        touch.append(jnp.concatenate(
            [jnp.full((1, TILE), incidence[owner, tile].astype(jnp.float32))
             for tile in range(block_arcs // TILE)], axis=1))
    lines = [*pieces(arc_cost[...]), *pieces(capacity[...]), mask, *pieces(demand[...]), share, *touch]
    lines = [line.astype(jnp.float32) for line in lines]
    lines += [jnp.zeros((1, block_arcs), jnp.float32)] * (EXTRA - len(lines))
    lines = jnp.concatenate(lines, axis=0).astype(jnp.bfloat16)
    extra[...] = lines
    across[TILE:, :] = lines
    beyond[half:, :] = lines
    for part in range(chips):
        copies[part].wait()
        rows = slice(part * TILE, (part + 1) * TILE)
        near[rows, :] = rows_in[rows, :] * touch[part].astype(jnp.bfloat16)
    across[:TILE, :] = near[(chips - 1) * TILE:, :]
    beyond[:half, :] = near[pl.ds(pl.multiple_of(core * half, half), half), :]


def rounds(masked, blocks, cost, cap, mask, demand, share, fleet_count, spread_out,
           flows, duals, prices, centre, shifted):
    scenarios, total_rows = demand.shape
    block_arcs = cost.shape[1] // blocks
    weight_sum = jnp.sum(share[:, :1])
    for round_index in range(ROUNDS):
        for step_index in range(ITERS):
            first = round_index == 0 and step_index == 0
            load = jnp.zeros((scenarios, total_rows), jnp.float32)
            if not first:
                duals_low = duals[...].astype(jnp.bfloat16)
            for block in range(blocks):
                cols = slice(block * block_arcs, (block + 1) * block_arcs)
                if first:
                    gradient = jnp.broadcast_to(cost[:, cols], (scenarios, block_arcs))
                    old = jnp.zeros((scenarios, block_arcs), jnp.float32)
                else:
                    old = flows[:, cols]
                    pull = jnp.dot(duals_low, masked(block), preferred_element_type=jnp.float32)
                    push = penalty * mask[:, cols] * old
                    if round_index > 0:
                        push = push + shifted[:, cols]
                    gradient = cost[:, cols] + pull + push
                new = jnp.clip(old - primal_step * gradient, 0.0, cap[:, cols])
                flows[:, cols] = new
                bar = (2.0 * new - old).astype(jnp.bfloat16)
                load = load + lax.dot_general(bar, masked(block), (((1,), (1,)), ((), ())),
                                              preferred_element_type=jnp.float32)
            step = dual_step * (load - demand[...])
            duals[...] = jnp.maximum(step if first else duals[...] + step, 0.0)
        squares = jnp.float32(0.0)
        for block in range(blocks):
            cols = slice(block * block_arcs, (block + 1) * block_arcs)
            fleet = flows[:, cols] * mask[:, cols]
            share_col = share[:, :1]
            mean = jnp.sum(share_col * fleet, axis=0, keepdims=True) / weight_sum
            gap = fleet - mean
            squares = squares + jnp.sum(share_col * gap * gap)
            total = penalty * gap if round_index == 0 else prices[:, cols] + penalty * gap
            prices[:, cols] = total
            centre[:, cols] = mean
            shifted[:, cols] = total - penalty * mean
        spread_out[round_index] = jnp.sqrt(squares / (weight_sum * fleet_count) + 1e-06)


def pick_fleet(price, mean, slots):
    picked = [line.astype(jnp.float32) for line in (*pieces(price), *pieces(mean))]
    picked += [jnp.zeros_like(price)] * 2
    picked = jnp.dot(jnp.concatenate(picked, axis=0).astype(jnp.bfloat16),
                     one_hot(slots, price.shape[1]), preferred_element_type=jnp.float32)
    return picked[0:1] + picked[1:2] + picked[2:3], picked[3:4] + picked[4:5] + picked[5:6]


def plain_kernel(masked, cost, cap, mask, demand, share, slots, flows_out, duals_out, mult_out, cons_out,
                 spread_out, flows, duals, prices, centre, shifted):
    blocks, total_rows, block_arcs = masked.shape
    rounds(lambda block: masked[block], blocks, cost, cap, mask, demand, share, slots.shape[1] * blocks,
           spread_out, flows, duals, prices, centre, shifted)
    scen, arc = lax.axis_index("scen"), lax.axis_index("arc")
    own = pl.ds(pl.multiple_of(arc * block_arcs, block_arcs), block_arcs)
    share_rows = total_rows // blocks
    own_rows = pl.ds(pl.multiple_of(arc * share_rows, share_rows), share_rows)
    flows_out[...] = own_row(flows[:, own], scen)
    duals_out[...] = own_row(duals[:, own_rows], scen)
    mult_out[...], cons_out[...] = pick_fleet(own_row(prices[:, own], scen), centre[:, own], slots[...])


def whole_kernel(near, *refs):
    lines, (early, late) = refs[:5], refs[5:7]
    others, first = [None] * 5, {id(early): 0, id(late): 0}
    for index, packed in ((0, early), (1, early), (4, early), (2, late), (3, late)):
        size = lines[index].shape[0]
        others[index] = packed.at[pl.ds(first[id(packed)], size)]
        first[id(packed)] += size
    (slots, flows_out, duals_out, mult_out, cons_out, spread_out,
     blocks_in, cost, cap, mask, demand_in, demand, share, flows, duals, prices, centre, shifted) = refs[7:]
    total_rows, block_arcs = near.shape
    scen, arc = lax.axis_index("scen"), lax.axis_index("arc")
    chip, core = scen // 2, lax.rem(scen, 2)
    chips = total_rows // TILE
    half = TILE // 2
    tails = [lines[0][TILE + half:, :], lines[3][TILE:, :], others[3][TILE:, :], lines[4][half:, :]]
    touch = []
    for block, tail in enumerate(tails):
        cols = slice(block * block_arcs, (block + 1) * block_arcs)
        tail = tail.astype(jnp.float32)
        cost[:, cols] = tail[0:1] + tail[1:2] + tail[2:3]
        cap[:, cols] = tail[3:4] + tail[4:5] + tail[5:6]
        mask[:, cols] = tail[6:7]
        touch.append(tail[11:11 + chips].astype(jnp.bfloat16))
    for row in range(2 * chips):
        part, source = row // 2, others if row % 2 else lines
        tail = source[part][TILE + half:, :] if part < chips - 1 else source[chips][half:, :]
        tail = tail.astype(jnp.float32)
        demand_in[row:row + 1, :] = tail[7:8] + tail[8:9] + tail[9:10]
        share[row:row + 1, :] = tail[10:11, :128] + tail[10:11, 128:256] + tail[10:11, 256:384]
    for part in range(chips):
        owner = jnp.bitwise_xor(chip, part)
        rows = slice(part * TILE, (part + 1) * TILE)
        demand[:, rows] = demand_in[:, pl.ds(pl.multiple_of(owner * TILE, TILE), TILE)]
        for side, source in enumerate((lines, others)):
            place = jnp.where(core == side, 0, half)
            place = pl.ds(pl.multiple_of(part * TILE + place, half), half)
            if part < chips - 1:
                blocks_in[side, rows, :] = source[part][:TILE, :] * touch[1 + side][part:part + 1]
                on = touch[3][chips - 1 - part:chips - part]
                blocks_in[2, place, :] = source[part][TILE:TILE + half, :] * on
            else:
                blocks_in[side, rows, :] = source[chips - 1][:TILE, :]
                blocks_in[2, place, :] = source[chips][:half, :]

    def masked(block):
        return near[...] if block == 0 else blocks_in[block - 1]

    rounds(masked, len(tails), cost, cap, mask, demand, share, slots.shape[1] * len(tails),
           spread_out, flows, duals, prices, centre, shifted)
    flows_out[...] = flows[0:1, :block_arcs]
    first = pl.multiple_of(jnp.bitwise_xor(chip, arc) * TILE, TILE)
    duals_out[...] = duals[:, pl.ds(first, TILE)][0:1]
    mult_out[...], cons_out[...] = pick_fleet(prices[0:1, :block_arcs], centre[:, :block_arcs], slots[...])


def swap(value, partner):
    scenarios, blocks = lax.axis_size("scen"), lax.axis_size("arc")
    pairs = []
    for scen in range(scenarios):
        for arc in range(blocks):
            other_scen, other_arc = partner(scen, arc)
            pairs.append((scen * blocks + arc, other_scen * blocks + other_arc))
    return lax.ppermute(value, ("scen", "arc"), pairs)


def bring(coupling, across, beyond, extra):
    scen = lax.axis_index("scen")
    half = TILE // 2
    wide = lax.dynamic_slice_in_dim(coupling, lax.shift_right_logical(scen, 1) * TILE, TILE, 0)
    wide = lax.optimization_barrier(wide)
    narrow = lax.dynamic_slice_in_dim(wide, (scen & 1) * half, half, 0)
    wide = swap(wide, lambda scen, arc: (scen, arc ^ (1 + scen % 2)))
    narrow = swap(narrow, lambda scen, arc: (scen, arc ^ 3))
    beyond = swap(beyond, lambda scen, arc: (scen ^ 6, arc ^ 3))
    line = jnp.concatenate([wide, narrow, extra], axis=0)
    line, across = lax.optimization_barrier((line, across))
    side = swap(line, lambda scen, arc: (scen ^ 2, arc))
    front = swap(line, lambda scen, arc: (scen ^ 4, arc))
    across = swap(across, lambda scen, arc: (scen, arc ^ (1 + scen % 2)))
    early = jnp.concatenate([line, side, beyond], axis=0)
    late = jnp.concatenate([front, across], axis=0)
    other = lambda scen, arc: (scen ^ 1, arc)
    return [line, side, front, across, beyond, swap(early, other), swap(late, other)]


def body(coupling, incidence, arc_cost, capacity, demand, weights, fleet_slots):
    total_rows, block_arcs = coupling.shape
    scenarios, blocks = lax.axis_size("scen"), lax.axis_size("arc")
    arcs = blocks * block_arcs
    fleet_block = fleet_slots.shape[0]
    row = lambda value: value.reshape(1, -1)
    slots = row(fleet_slots)
    out_shape = (
        jax.ShapeDtypeStruct((1, block_arcs), jnp.float32),
        jax.ShapeDtypeStruct((1, total_rows // blocks), jnp.float32),
        jax.ShapeDtypeStruct((1, fleet_block), jnp.float32),
        jax.ShapeDtypeStruct((1, fleet_block), jnp.float32),
        jax.ShapeDtypeStruct((ROUNDS,), jnp.float32),
    )
    out_specs = (VMEM, VMEM, VMEM, VMEM, SMEM)
    state = [
        pltpu.VMEM((scenarios, arcs), jnp.float32),
        pltpu.VMEM((scenarios, total_rows), jnp.float32),
        pltpu.VMEM((scenarios, arcs), jnp.float32),
        pltpu.VMEM((1, arcs), jnp.float32),
        pltpu.VMEM((scenarios, arcs), jnp.float32),
    ]
    limit = lambda mib: pltpu.CompilerParams(vmem_limit_bytes=mib * 1024 * 1024)
    cost = pl.CostEstimate(
        flops=4 * ROUNDS * ITERS * scenarios * total_rows * arcs,
        bytes_accessed=2 * total_rows * arcs,
        transcendentals=0,
    )
    fits = (scenarios, blocks) == (8, 4)
    if fits and total_rows == TILE * 4:
        like = lambda rows: jax.ShapeDtypeStruct((rows, block_arcs), jnp.bfloat16)
        near, across, beyond, extra = pl.pallas_call(
            pack_kernel,
            out_shape=(like(total_rows), like(TILE + EXTRA), like(TILE // 2 + EXTRA), like(EXTRA)),
            in_specs=[ANY, SMEM, VMEM, VMEM, VMEM, VMEM, VMEM],
            out_specs=(VMEM,) * 4,
            scratch_shapes=[
                pltpu.VMEM((total_rows, block_arcs), jnp.bfloat16),
                pltpu.SemaphoreType.DMA((total_rows // TILE,)),
            ],
            compiler_params=limit(8),
            name="pack",
        )(coupling, incidence, row(arc_cost), row(capacity), demand, weights.reshape(1, 1), slots)
        brought = bring(coupling, across, beyond, extra)
        outs = pl.pallas_call(
            whole_kernel,
            out_shape=out_shape,
            in_specs=[VMEM] * (len(brought) + 2),
            out_specs=out_specs,
            scratch_shapes=[
                pltpu.VMEM((blocks - 1, total_rows, block_arcs), jnp.bfloat16),
                pltpu.VMEM((1, arcs), jnp.float32),
                pltpu.VMEM((1, arcs), jnp.float32),
                pltpu.VMEM((1, arcs), jnp.float32),
                pltpu.VMEM((scenarios, total_rows), jnp.float32),
                pltpu.VMEM((scenarios, total_rows), jnp.float32),
                pltpu.VMEM((scenarios, 128), jnp.float32),
                *state,
            ],
            compiler_params=limit(16),
            cost_estimate=cost,
            name="whole",
        )(near, *brought, slots)
    else:
        masked = (
            coupling.reshape(total_rows // TILE, TILE, block_arcs // TILE, TILE)
            * incidence.astype(jnp.bfloat16)[:, None, :, None]
        ).reshape(total_rows, block_arcs)
        masked = lax.all_gather(masked, "arc")
        own_mask = jnp.zeros((block_arcs,), jnp.float32).at[fleet_slots].set(1.0)
        per_arc = lax.all_gather(jnp.stack([arc_cost, capacity, own_mask]), "arc", axis=1, tiled=True)
        shares = jnp.broadcast_to(weights.astype(jnp.float32)[:, None], (1, 128))
        per_scen = lax.all_gather(jnp.concatenate([demand, shares], axis=1), "scen", tiled=True)
        outs = pl.pallas_call(
            plain_kernel,
            out_shape=out_shape,
            in_specs=[VMEM] * 7,
            out_specs=out_specs,
            scratch_shapes=state,
            compiler_params=limit(48),
            cost_estimate=cost,
            name="whole",
        )(masked, per_arc[0:1], per_arc[1:2], per_arc[2:3], per_scen[:, :total_rows],
          per_scen[:, total_rows:], slots)
    flows, duals, multipliers, consensus, spread = outs
    return flows, duals, multipliers, consensus.reshape(-1), spread


def solution(mesh):
    in_specs = (
        P(None, "arc"),
        P(None, "arc"),
        P("arc"),
        P("arc"),
        P("scen", None),
        P("scen"),
        P("arc"),
    )
    out_specs = (P("scen", "arc"), P("scen", "arc"), P("scen", "arc"), P("arc"), P())
    return jax.shard_map(body, mesh=mesh, in_specs=in_specs, out_specs=out_specs, check_vma=False)
```

```python
import functools

import jax
import jax.numpy as jnp
from jax import lax
from jax.experimental import pallas as pl
from jax.experimental.pallas import tpu as pltpu
from jax.sharding import PartitionSpec as P

TILE = 128
ITERS = 4
ROUNDS = 2
EXTRA = 16

primal_step = 0.9
dual_step = 0.9
penalty = 1.0

VMEM = pl.BlockSpec(memory_space=pltpu.VMEM)
SMEM = pl.BlockSpec(memory_space=pltpu.SMEM)
ANY = pl.BlockSpec(memory_space=pl.ANY)


def pieces(value):
    high = value.astype(jnp.bfloat16)
    rest = value - high.astype(jnp.float32)
    middle = rest.astype(jnp.bfloat16)
    low = (rest - middle.astype(jnp.float32)).astype(jnp.bfloat16)
    return high, middle, low


def one_hot(slots, block_arcs):
    arcs = lax.broadcasted_iota(jnp.int32, (block_arcs, slots.shape[1]), 0)
    return jnp.where(arcs == slots, 1.0, 0.0).astype(jnp.bfloat16)


def fleet_mask(slots, block_arcs):
    ones = jnp.ones((8, slots.shape[1]), jnp.bfloat16)
    hits = lax.dot_general(ones, one_hot(slots, block_arcs), (((1,), (1,)), ((), ())),
                           preferred_element_type=jnp.float32)
    return hits[:1]


def own_row(value, scen):
    rows = lax.broadcasted_iota(jnp.int32, value.shape, 0)
    return jnp.sum(jnp.where(rows == scen, value, 0.0), axis=0, keepdims=True)


def pack_kernel(coupling, incidence, arc_cost, capacity, demand, weights, slots,
                near, across, extra, rows_in, sems):
    total_rows, block_arcs = rows_in.shape
    chip = lax.axis_index("scen") // 2
    chips = total_rows // TILE
    copies = []
    for part in range(chips):
        first = pl.multiple_of(jnp.bitwise_xor(chip, part) * TILE, TILE)
        copies.append(pltpu.make_async_copy(
            coupling.at[pl.ds(first, TILE)], rows_in.at[pl.ds(part * TILE, TILE)], sems.at[part]))
    for copy in copies:
        copy.start()
    share = jnp.broadcast_to(weights[...].astype(jnp.float32), (1, 128))
    share = jnp.concatenate([*pieces(share), jnp.zeros((1, 128), jnp.bfloat16)], axis=1)
    mask = fleet_mask(slots[...], block_arcs)
    touch = []
    for part in range(chips):
        owner = jnp.bitwise_xor(chip, part)
        touch.append(jnp.concatenate(
            [jnp.full((1, TILE), incidence[owner, tile].astype(jnp.float32))
             for tile in range(block_arcs // TILE)], axis=1))
    lines = [*pieces(arc_cost[...]), *pieces(capacity[...]), mask, *pieces(demand[...]), share, *touch]
    lines = [line.astype(jnp.float32) for line in lines]
    lines += [jnp.zeros((1, block_arcs), jnp.float32)] * (EXTRA - len(lines))
    lines = jnp.concatenate(lines, axis=0).astype(jnp.bfloat16)
    extra[...] = lines
    across[TILE:, :] = lines
    for part in range(chips):
        copies[part].wait()
        rows = slice(part * TILE, (part + 1) * TILE)
        near[rows, :] = rows_in[rows, :] * touch[part].astype(jnp.bfloat16)
    across[:TILE, :] = near[(chips - 1) * TILE:, :]


def rounds(masked, blocks, cost, cap, mask, demand, share, fleet_count, spread_out,
           flows, duals, prices, centre, shifted):
    scenarios, total_rows = demand.shape
    block_arcs = cost.shape[1] // blocks
    weight_sum = jnp.sum(share[:, :1])
    for round_index in range(ROUNDS):
        for step_index in range(ITERS):
            first = round_index == 0 and step_index == 0
            load = jnp.zeros((scenarios, total_rows), jnp.float32)
            if not first:
                duals_low = duals[...].astype(jnp.bfloat16)
            for block in range(blocks):
                cols = slice(block * block_arcs, (block + 1) * block_arcs)
                if first:
                    gradient = jnp.broadcast_to(cost[:, cols], (scenarios, block_arcs))
                    old = jnp.zeros((scenarios, block_arcs), jnp.float32)
                else:
                    old = flows[:, cols]
                    pull = jnp.dot(duals_low, masked(block), preferred_element_type=jnp.float32)
                    push = penalty * mask[:, cols] * old
                    if round_index > 0:
                        push = push + shifted[:, cols]
                    gradient = cost[:, cols] + pull + push
                new = jnp.clip(old - primal_step * gradient, 0.0, cap[:, cols])
                flows[:, cols] = new
                bar = (2.0 * new - old).astype(jnp.bfloat16)
                load = load + lax.dot_general(bar, masked(block), (((1,), (1,)), ((), ())),
                                              preferred_element_type=jnp.float32)
            step = dual_step * (load - demand[...])
            duals[...] = jnp.maximum(step if first else duals[...] + step, 0.0)
        squares = jnp.float32(0.0)
        for block in range(blocks):
            cols = slice(block * block_arcs, (block + 1) * block_arcs)
            fleet = flows[:, cols] * mask[:, cols]
            share_col = share[:, :1]
            mean = jnp.sum(share_col * fleet, axis=0, keepdims=True) / weight_sum
            gap = fleet - mean
            squares = squares + jnp.sum(share_col * gap * gap)
            total = penalty * gap if round_index == 0 else prices[:, cols] + penalty * gap
            prices[:, cols] = total
            centre[:, cols] = mean
            shifted[:, cols] = total - penalty * mean
        spread_out[round_index] = jnp.sqrt(squares / (weight_sum * fleet_count) + 1e-06)


def pick_fleet(price, mean, slots):
    picked = [line.astype(jnp.float32) for line in (*pieces(price), *pieces(mean))]
    picked += [jnp.zeros_like(price)] * 2
    picked = jnp.dot(jnp.concatenate(picked, axis=0).astype(jnp.bfloat16),
                     one_hot(slots, price.shape[1]), preferred_element_type=jnp.float32)
    return picked[0:1] + picked[1:2] + picked[2:3], picked[3:4] + picked[4:5] + picked[5:6]


def plain_kernel(masked, cost, cap, mask, demand, share, slots, flows_out, duals_out, mult_out, cons_out,
                 spread_out, flows, duals, prices, centre, shifted):
    blocks, total_rows, block_arcs = masked.shape
    rounds(lambda block: masked[block], blocks, cost, cap, mask, demand, share, slots.shape[1] * blocks,
           spread_out, flows, duals, prices, centre, shifted)
    scen, arc = lax.axis_index("scen"), lax.axis_index("arc")
    own = pl.ds(pl.multiple_of(arc * block_arcs, block_arcs), block_arcs)
    share_rows = total_rows // blocks
    own_rows = pl.ds(pl.multiple_of(arc * share_rows, share_rows), share_rows)
    flows_out[...] = own_row(flows[:, own], scen)
    duals_out[...] = own_row(duals[:, own_rows], scen)
    mult_out[...], cons_out[...] = pick_fleet(own_row(prices[:, own], scen), centre[:, own], slots[...])


def whole_kernel(near, *refs):
    lines, others = refs[:6], [None] * 6
    for packed, parts in ((refs[6], (0, 1, 4)), (refs[7], (2, 3, 5))):
        first = 0
        for part in parts:
            rows = lines[part].shape[0]
            others[part] = packed.at[pl.ds(first, rows)]
            first += rows
    (slots, flows_out, duals_out, mult_out, cons_out, spread_out,
     blocks_in, cost, cap, mask, demand_in, demand, share, flows, duals, prices, centre, shifted) = refs[8:]
    total_rows, block_arcs = near.shape
    scen, arc = lax.axis_index("scen"), lax.axis_index("arc")
    chip, core = scen // 2, lax.rem(scen, 2)
    chips = total_rows // TILE
    half = TILE // 2
    tails = [lines[0][TILE + half:, :], lines[3][TILE:, :], others[3][TILE:, :], lines[5][...]]
    touch = []
    for block, tail in enumerate(tails):
        cols = slice(block * block_arcs, (block + 1) * block_arcs)
        tail = tail.astype(jnp.float32)
        cost[:, cols] = tail[0:1] + tail[1:2] + tail[2:3]
        cap[:, cols] = tail[3:4] + tail[4:5] + tail[5:6]
        mask[:, cols] = tail[6:7]
        touch.append(tail[11:11 + chips].astype(jnp.bfloat16))
    for row in range(2 * chips):
        part, source = row // 2, others if row % 2 else lines
        tail = source[part][TILE + half:, :] if part < chips - 1 else source[5][...]
        tail = tail.astype(jnp.float32)
        demand_in[row:row + 1, :] = tail[7:8] + tail[8:9] + tail[9:10]
        share[row:row + 1, :] = tail[10:11, :128] + tail[10:11, 128:256] + tail[10:11, 256:384]
    for part in range(chips):
        owner = jnp.bitwise_xor(chip, part)
        rows = slice(part * TILE, (part + 1) * TILE)
        demand[:, rows] = demand_in[:, pl.ds(pl.multiple_of(owner * TILE, TILE), TILE)]
        for side, source in enumerate((lines, others)):
            place = jnp.where(core == side, 0, half)
            place = pl.ds(pl.multiple_of(part * TILE + place, half), half)
            on = touch[3][chips - 1 - part:chips - part]
            if part < chips - 1:
                blocks_in[side, rows, :] = source[part][:TILE, :] * touch[1 + side][part:part + 1]
                blocks_in[2, place, :] = source[part][TILE:TILE + half, :] * on
            else:
                blocks_in[side, rows, :] = source[3][:TILE, :]
                blocks_in[2, place, :] = source[4][...] * on

    def masked(block):
        return near[...] if block == 0 else blocks_in[block - 1]

    rounds(masked, len(tails), cost, cap, mask, demand, share, slots.shape[1] * len(tails),
           spread_out, flows, duals, prices, centre, shifted)
    flows_out[...] = flows[0:1, :block_arcs]
    first = pl.multiple_of(jnp.bitwise_xor(chip, arc) * TILE, TILE)
    duals_out[...] = duals[:, pl.ds(first, TILE)][0:1]
    mult_out[...], cons_out[...] = pick_fleet(prices[0:1, :block_arcs], centre[:, :block_arcs], slots[...])


def swap(value, partner):
    scenarios, blocks = lax.axis_size("scen"), lax.axis_size("arc")
    pairs = []
    for scen in range(scenarios):
        for arc in range(blocks):
            other_scen, other_arc = partner(scen, arc)
            pairs.append((scen * blocks + arc, other_scen * blocks + other_arc))
    return lax.ppermute(value, ("scen", "arc"), pairs)


def bring(coupling, across, extra):
    scen = lax.axis_index("scen")
    half = TILE // 2
    wide = lax.dynamic_slice_in_dim(coupling, lax.shift_right_logical(scen, 1) * TILE, TILE, 0)
    wide = lax.optimization_barrier(wide)
    narrow = lax.dynamic_slice_in_dim(wide, (scen & 1) * half, half, 0)
    wide = swap(wide, lambda scen, arc: (scen, arc ^ (1 + scen % 2)))
    narrow = swap(narrow, lambda scen, arc: (scen, arc ^ 3))
    line = jnp.concatenate([wide, narrow, extra], axis=0)
    line, across = lax.optimization_barrier((line, across))
    side = swap(line, lambda scen, arc: (scen ^ 2, arc))
    front = swap(line, lambda scen, arc: (scen ^ 4, arc))
    across = swap(across, lambda scen, arc: (scen, arc ^ (1 + scen % 2)))
    beyond = swap(narrow, lambda scen, arc: (scen ^ 6, arc))
    extra = swap(extra, lambda scen, arc: (scen ^ 6, arc ^ 3))
    early = jnp.concatenate([line, side, beyond], axis=0)
    late = jnp.concatenate([front, across, extra], axis=0)
    other = lambda scen, arc: (scen ^ 1, arc)
    return [line, side, front, across, beyond, extra, swap(early, other), swap(late, other)]


def body(coupling, incidence, arc_cost, capacity, demand, weights, fleet_slots):
    total_rows, block_arcs = coupling.shape
    scenarios, blocks = lax.axis_size("scen"), lax.axis_size("arc")
    arcs = blocks * block_arcs
    fleet_block = fleet_slots.shape[0]
    row = lambda value: value.reshape(1, -1)
    slots = row(fleet_slots)
    out_shape = (
        jax.ShapeDtypeStruct((1, block_arcs), jnp.float32),
        jax.ShapeDtypeStruct((1, total_rows // blocks), jnp.float32),
        jax.ShapeDtypeStruct((1, fleet_block), jnp.float32),
        jax.ShapeDtypeStruct((1, fleet_block), jnp.float32),
        jax.ShapeDtypeStruct((ROUNDS,), jnp.float32),
    )
    out_specs = (VMEM, VMEM, VMEM, VMEM, SMEM)
    state = [
        pltpu.VMEM((scenarios, arcs), jnp.float32),
        pltpu.VMEM((scenarios, total_rows), jnp.float32),
        pltpu.VMEM((scenarios, arcs), jnp.float32),
        pltpu.VMEM((1, arcs), jnp.float32),
        pltpu.VMEM((scenarios, arcs), jnp.float32),
    ]
    limit = lambda mib: pltpu.CompilerParams(vmem_limit_bytes=mib * 1024 * 1024)
    cost = pl.CostEstimate(
        flops=4 * ROUNDS * ITERS * scenarios * total_rows * arcs,
        bytes_accessed=2 * total_rows * arcs,
        transcendentals=0,
    )
    fits = (scenarios, blocks) == (8, 4)
    if fits and total_rows == TILE * 4:
        like = lambda rows: jax.ShapeDtypeStruct((rows, block_arcs), jnp.bfloat16)
        near, across, extra = pl.pallas_call(
            pack_kernel,
            out_shape=(like(total_rows), like(TILE + EXTRA), like(EXTRA)),
            in_specs=[ANY, SMEM, VMEM, VMEM, VMEM, VMEM, VMEM],
            out_specs=(VMEM,) * 3,
            scratch_shapes=[
                pltpu.VMEM((total_rows, block_arcs), jnp.bfloat16),
                pltpu.SemaphoreType.DMA((total_rows // TILE,)),
            ],
            compiler_params=limit(8),
            name="pack",
        )(coupling, incidence, row(arc_cost), row(capacity), demand, weights.reshape(1, 1), slots)
        brought = bring(coupling, across, extra)
        outs = pl.pallas_call(
            whole_kernel,
            out_shape=out_shape,
            in_specs=[VMEM] * (len(brought) + 2),
            out_specs=out_specs,
            scratch_shapes=[
                pltpu.VMEM((blocks - 1, total_rows, block_arcs), jnp.bfloat16),
                pltpu.VMEM((1, arcs), jnp.float32),
                pltpu.VMEM((1, arcs), jnp.float32),
                pltpu.VMEM((1, arcs), jnp.float32),
                pltpu.VMEM((scenarios, total_rows), jnp.float32),
                pltpu.VMEM((scenarios, total_rows), jnp.float32),
                pltpu.VMEM((scenarios, 128), jnp.float32),
                *state,
            ],
            compiler_params=limit(16),
            cost_estimate=cost,
            name="whole",
        )(near, *brought, slots)
    else:
        masked = (
            coupling.reshape(total_rows // TILE, TILE, block_arcs // TILE, TILE)
            * incidence.astype(jnp.bfloat16)[:, None, :, None]
        ).reshape(total_rows, block_arcs)
        masked = lax.all_gather(masked, "arc")
        own_mask = jnp.zeros((block_arcs,), jnp.float32).at[fleet_slots].set(1.0)
        per_arc = lax.all_gather(jnp.stack([arc_cost, capacity, own_mask]), "arc", axis=1, tiled=True)
        shares = jnp.broadcast_to(weights.astype(jnp.float32)[:, None], (1, 128))
        per_scen = lax.all_gather(jnp.concatenate([demand, shares], axis=1), "scen", tiled=True)
        outs = pl.pallas_call(
            plain_kernel,
            out_shape=out_shape,
            in_specs=[VMEM] * 7,
            out_specs=out_specs,
            scratch_shapes=state,
            compiler_params=limit(48),
            cost_estimate=cost,
            name="whole",
        )(masked, per_arc[0:1], per_arc[1:2], per_arc[2:3], per_scen[:, :total_rows],
          per_scen[:, total_rows:], slots)
    flows, duals, multipliers, consensus, spread = outs
    return flows, duals, multipliers, consensus.reshape(-1), spread


def solution(mesh):
    in_specs = (
        P(None, "arc"),
        P(None, "arc"),
        P("arc"),
        P("arc"),
        P("scen", None),
        P("scen"),
        P("arc"),
    )
    out_specs = (P("scen", "arc"), P("scen", "arc"), P("scen", "arc"), P("arc"), P())
    return jax.shard_map(body, mesh=mesh, in_specs=in_specs, out_specs=out_specs, check_vma=False)
```

```python
import functools

import jax
import jax.numpy as jnp
from jax import lax
from jax.experimental import pallas as pl
from jax.experimental.pallas import tpu as pltpu
from jax.sharding import PartitionSpec as P

TILE = 128
ITERS = 4
ROUNDS = 2
EXTRA = 16

primal_step = 0.9
dual_step = 0.9
penalty = 1.0

VMEM = pl.BlockSpec(memory_space=pltpu.VMEM)
SMEM = pl.BlockSpec(memory_space=pltpu.SMEM)
ANY = pl.BlockSpec(memory_space=pl.ANY)


def pieces(value):
    high = value.astype(jnp.bfloat16)
    rest = value - high.astype(jnp.float32)
    middle = rest.astype(jnp.bfloat16)
    low = (rest - middle.astype(jnp.float32)).astype(jnp.bfloat16)
    return high, middle, low


def one_hot(slots, block_arcs):
    arcs = lax.broadcasted_iota(jnp.int32, (block_arcs, slots.shape[1]), 0)
    return jnp.where(arcs == slots, 1.0, 0.0).astype(jnp.bfloat16)


def fleet_mask(slots, block_arcs):
    ones = jnp.ones((8, slots.shape[1]), jnp.bfloat16)
    hits = lax.dot_general(ones, one_hot(slots, block_arcs), (((1,), (1,)), ((), ())),
                           preferred_element_type=jnp.float32)
    return hits[:1]


def own_row(value, scen):
    rows = lax.broadcasted_iota(jnp.int32, value.shape, 0)
    return jnp.sum(jnp.where(rows == scen, value, 0.0), axis=0, keepdims=True)


def pack_kernel(coupling, incidence, arc_cost, capacity, demand, weights, slots,
                near, across, extra, rows_in, sems):
    total_rows, block_arcs = rows_in.shape
    chip = lax.axis_index("scen") // 2
    chips = total_rows // TILE
    copies = []
    for part in range(chips):
        first = pl.multiple_of(jnp.bitwise_xor(chip, part) * TILE, TILE)
        copies.append(pltpu.make_async_copy(
            coupling.at[pl.ds(first, TILE)], rows_in.at[pl.ds(part * TILE, TILE)], sems.at[part]))
    for copy in copies:
        copy.start()
    share = jnp.broadcast_to(weights[...].astype(jnp.float32), (1, 128))
    share = jnp.concatenate([*pieces(share), jnp.zeros((1, 128), jnp.bfloat16)], axis=1)
    mask = fleet_mask(slots[...], block_arcs)
    touch = []
    for part in range(chips):
        owner = jnp.bitwise_xor(chip, part)
        touch.append(jnp.concatenate(
            [jnp.full((1, TILE), incidence[owner, tile].astype(jnp.float32))
             for tile in range(block_arcs // TILE)], axis=1))
    lines = [*pieces(arc_cost[...]), *pieces(capacity[...]), mask, *pieces(demand[...]), share, *touch]
    lines = [line.astype(jnp.float32) for line in lines]
    lines += [jnp.zeros((1, block_arcs), jnp.float32)] * (EXTRA - len(lines))
    lines = jnp.concatenate(lines, axis=0).astype(jnp.bfloat16)
    extra[...] = lines
    across[TILE:, :] = lines
    for part in range(chips):
        copies[part].wait()
        rows = slice(part * TILE, (part + 1) * TILE)
        near[rows, :] = rows_in[rows, :] * touch[part].astype(jnp.bfloat16)
    across[:TILE, :] = near[(chips - 1) * TILE:, :]


def rounds(masked, turned, blocks, cost, cap, mask, demand, share, fleet_count, spread_out,
           flows, duals, prices, centre, shifted):
    scenarios, total_rows = demand.shape
    block_arcs = cost.shape[1] // blocks
    weight_sum = jnp.sum(share[:, :1])
    for round_index in range(ROUNDS):
        for step_index in range(ITERS):
            first = round_index == 0 and step_index == 0
            load = jnp.zeros((scenarios, total_rows), jnp.float32)
            if not first:
                duals_low = duals[...].astype(jnp.bfloat16)
            for block in range(blocks):
                cols = slice(block * block_arcs, (block + 1) * block_arcs)
                if first:
                    gradient = jnp.broadcast_to(cost[:, cols], (scenarios, block_arcs))
                    old = jnp.zeros((scenarios, block_arcs), jnp.float32)
                else:
                    old = flows[:, cols]
                    pull = jnp.dot(duals_low, masked(block), preferred_element_type=jnp.float32)
                    push = penalty * mask[:, cols] * old
                    if round_index > 0:
                        push = push + shifted[:, cols]
                    gradient = cost[:, cols] + pull + push
                new = jnp.clip(old - primal_step * gradient, 0.0, cap[:, cols])
                flows[:, cols] = new
                bar = (2.0 * new - old).astype(jnp.bfloat16)
                load = load + jnp.dot(bar, turned(block), preferred_element_type=jnp.float32)
            step = dual_step * (load - demand[...])
            duals[...] = jnp.maximum(step if first else duals[...] + step, 0.0)
        squares = jnp.float32(0.0)
        for block in range(blocks):
            cols = slice(block * block_arcs, (block + 1) * block_arcs)
            fleet = flows[:, cols] * mask[:, cols]
            share_col = share[:, :1]
            mean = jnp.sum(share_col * fleet, axis=0, keepdims=True) / weight_sum
            gap = fleet - mean
            squares = squares + jnp.sum(share_col * gap * gap)
            total = penalty * gap if round_index == 0 else prices[:, cols] + penalty * gap
            prices[:, cols] = total
            centre[:, cols] = mean
            shifted[:, cols] = total - penalty * mean
        spread_out[round_index] = jnp.sqrt(squares / (weight_sum * fleet_count) + 1e-06)


def pick_fleet(price, mean, slots):
    picked = [line.astype(jnp.float32) for line in (*pieces(price), *pieces(mean))]
    picked += [jnp.zeros_like(price)] * 2
    picked = jnp.dot(jnp.concatenate(picked, axis=0).astype(jnp.bfloat16),
                     one_hot(slots, price.shape[1]), preferred_element_type=jnp.float32)
    return picked[0:1] + picked[1:2] + picked[2:3], picked[3:4] + picked[4:5] + picked[5:6]


def plain_kernel(masked, cost, cap, mask, demand, share, slots, flows_out, duals_out, mult_out, cons_out,
                 spread_out, flows, duals, prices, centre, shifted):
    blocks, total_rows, block_arcs = masked.shape
    rounds(lambda block: masked[block], lambda block: masked[block].T, blocks, cost, cap, mask, demand, share, slots.shape[1] * blocks,
           spread_out, flows, duals, prices, centre, shifted)
    scen, arc = lax.axis_index("scen"), lax.axis_index("arc")
    own = pl.ds(pl.multiple_of(arc * block_arcs, block_arcs), block_arcs)
    share_rows = total_rows // blocks
    own_rows = pl.ds(pl.multiple_of(arc * share_rows, share_rows), share_rows)
    flows_out[...] = own_row(flows[:, own], scen)
    duals_out[...] = own_row(duals[:, own_rows], scen)
    mult_out[...], cons_out[...] = pick_fleet(own_row(prices[:, own], scen), centre[:, own], slots[...])


def whole_kernel(near, *refs):
    lines, others = refs[:5], [None] * 5
    for packed, parts in ((refs[6], (0, 1, 4)), (refs[7], (2, 3))):
        first = 0
        for part in parts:
            rows = lines[part].shape[0]
            others[part] = packed.at[pl.ds(first, rows)]
            first += rows
    (slots, flows_out, duals_out, mult_out, cons_out, spread_out,
     blocks_in, turned, cost, cap, mask, demand_in, demand, share, flows, duals, prices, centre, shifted) = refs[8:]
    total_rows, block_arcs = near.shape
    scen, arc = lax.axis_index("scen"), lax.axis_index("arc")
    chip, core = scen // 2, lax.rem(scen, 2)
    chips = total_rows // TILE
    half = TILE // 2
    tails = [lines[0][TILE + half:, :], lines[3][TILE:, :], others[3][TILE:, :], refs[5][...]]
    touch = []
    for block, tail in enumerate(tails):
        cols = slice(block * block_arcs, (block + 1) * block_arcs)
        tail = tail.astype(jnp.float32)
        cost[:, cols] = tail[0:1] + tail[1:2] + tail[2:3]
        cap[:, cols] = tail[3:4] + tail[4:5] + tail[5:6]
        mask[:, cols] = tail[6:7]
        touch.append(tail[11:11 + chips].astype(jnp.bfloat16))
    for row in range(2 * chips):
        part, source = row // 2, others if row % 2 else lines
        tail = source[part][TILE + half:, :] if part < chips - 1 else source[4][half:, :]
        tail = tail.astype(jnp.float32)
        demand_in[row:row + 1, :] = tail[7:8] + tail[8:9] + tail[9:10]
        share[row:row + 1, :] = tail[10:11, :128] + tail[10:11, 128:256] + tail[10:11, 256:384]
    for part in range(chips):
        owner = jnp.bitwise_xor(chip, part)
        rows = slice(part * TILE, (part + 1) * TILE)
        demand[:, rows] = demand_in[:, pl.ds(pl.multiple_of(owner * TILE, TILE), TILE)]
        for side, source in enumerate((lines, others)):
            place = jnp.where(core == side, 0, half)
            place = pl.ds(pl.multiple_of(part * TILE + place, half), half)
            on = touch[3][part:part + 1]
            if part < chips - 1:
                blocks_in[side, rows, :] = source[part][:TILE, :] * touch[1 + side][part:part + 1]
                blocks_in[2, place, :] = source[part][TILE:TILE + half, :] * on
            else:
                blocks_in[side, rows, :] = source[3][:TILE, :]
                blocks_in[2, place, :] = source[4][:half, :] * on

    def masked(block):
        return near[...] if block == 0 else blocks_in[block - 1]

    for block in range(len(tails)):
        turned[block] = masked(block).T
    rounds(masked, lambda block: turned[block], len(tails), cost, cap, mask, demand, share, slots.shape[1] * len(tails),
           spread_out, flows, duals, prices, centre, shifted)
    flows_out[...] = flows[0:1, :block_arcs]
    first = pl.multiple_of(jnp.bitwise_xor(chip, arc) * TILE, TILE)
    duals_out[...] = duals[:, pl.ds(first, TILE)][0:1]
    mult_out[...], cons_out[...] = pick_fleet(prices[0:1, :block_arcs], centre[:, :block_arcs], slots[...])


def swap(value, partner):
    scenarios, blocks = lax.axis_size("scen"), lax.axis_size("arc")
    pairs = []
    for scen in range(scenarios):
        for arc in range(blocks):
            other_scen, other_arc = partner(scen, arc)
            pairs.append((scen * blocks + arc, other_scen * blocks + other_arc))
    return lax.ppermute(value, ("scen", "arc"), pairs)


def bring(coupling, across, extra):
    scen = lax.axis_index("scen")
    half = TILE // 2
    wide = lax.dynamic_slice_in_dim(coupling, lax.shift_right_logical(scen, 1) * TILE, TILE, 0)
    wide = lax.optimization_barrier(wide)
    narrow = lax.dynamic_slice_in_dim(wide, (scen & 1) * half, half, 0)
    wide = swap(wide, lambda scen, arc: (scen, arc ^ (1 + scen % 2)))
    narrow = swap(narrow, lambda scen, arc: (scen, arc ^ 3))
    line = jnp.concatenate([wide, narrow, extra], axis=0)
    line, across = lax.optimization_barrier((line, across))
    side = swap(line, lambda scen, arc: (scen ^ 2, arc))
    front = swap(line, lambda scen, arc: (scen ^ 4, arc))
    across = swap(across, lambda scen, arc: (scen, arc ^ (1 + scen % 2)))
    beyond = swap(jnp.concatenate([narrow, extra], axis=0), lambda scen, arc: (scen ^ 6, arc))
    extra = swap(extra, lambda scen, arc: (scen, arc ^ 3))
    early = jnp.concatenate([line, side, beyond, extra], axis=0)
    late = jnp.concatenate([front, across], axis=0)
    other = lambda scen, arc: (scen ^ 1, arc)
    return [line, side, front, across, beyond, extra, swap(early, other), swap(late, other)]


def body(coupling, incidence, arc_cost, capacity, demand, weights, fleet_slots):
    total_rows, block_arcs = coupling.shape
    scenarios, blocks = lax.axis_size("scen"), lax.axis_size("arc")
    arcs = blocks * block_arcs
    fleet_block = fleet_slots.shape[0]
    row = lambda value: value.reshape(1, -1)
    slots = row(fleet_slots)
    out_shape = (
        jax.ShapeDtypeStruct((1, block_arcs), jnp.float32),
        jax.ShapeDtypeStruct((1, total_rows // blocks), jnp.float32),
        jax.ShapeDtypeStruct((1, fleet_block), jnp.float32),
        jax.ShapeDtypeStruct((1, fleet_block), jnp.float32),
        jax.ShapeDtypeStruct((ROUNDS,), jnp.float32),
    )
    out_specs = (VMEM, VMEM, VMEM, VMEM, SMEM)
    state = [
        pltpu.VMEM((scenarios, arcs), jnp.float32),
        pltpu.VMEM((scenarios, total_rows), jnp.float32),
        pltpu.VMEM((scenarios, arcs), jnp.float32),
        pltpu.VMEM((1, arcs), jnp.float32),
        pltpu.VMEM((scenarios, arcs), jnp.float32),
    ]
    limit = lambda mib: pltpu.CompilerParams(vmem_limit_bytes=mib * 1024 * 1024)
    cost = pl.CostEstimate(
        flops=4 * ROUNDS * ITERS * scenarios * total_rows * arcs,
        bytes_accessed=2 * total_rows * arcs,
        transcendentals=0,
    )
    fits = (scenarios, blocks) == (8, 4)
    if fits and total_rows == TILE * 4:
        like = lambda rows: jax.ShapeDtypeStruct((rows, block_arcs), jnp.bfloat16)
        near, across, extra = pl.pallas_call(
            pack_kernel,
            out_shape=(like(total_rows), like(TILE + EXTRA), like(EXTRA)),
            in_specs=[ANY, SMEM, VMEM, VMEM, VMEM, VMEM, VMEM],
            out_specs=(VMEM,) * 3,
            scratch_shapes=[
                pltpu.VMEM((total_rows, block_arcs), jnp.bfloat16),
                pltpu.SemaphoreType.DMA((total_rows // TILE,)),
            ],
            compiler_params=limit(8),
            name="pack",
        )(coupling, incidence, row(arc_cost), row(capacity), demand, weights.reshape(1, 1), slots)
        brought = bring(coupling, across, extra)
        outs = pl.pallas_call(
            whole_kernel,
            out_shape=out_shape,
            in_specs=[VMEM] * (len(brought) + 2),
            out_specs=out_specs,
            scratch_shapes=[
                pltpu.VMEM((blocks - 1, total_rows, block_arcs), jnp.bfloat16),
                pltpu.VMEM((blocks, block_arcs, total_rows), jnp.bfloat16),
                pltpu.VMEM((1, arcs), jnp.float32),
                pltpu.VMEM((1, arcs), jnp.float32),
                pltpu.VMEM((1, arcs), jnp.float32),
                pltpu.VMEM((scenarios, total_rows), jnp.float32),
                pltpu.VMEM((scenarios, total_rows), jnp.float32),
                pltpu.VMEM((scenarios, 128), jnp.float32),
                *state,
            ],
            compiler_params=limit(16),
            cost_estimate=cost,
            name="whole",
        )(near, *brought, slots)
    else:
        masked = (
            coupling.reshape(total_rows // TILE, TILE, block_arcs // TILE, TILE)
            * incidence.astype(jnp.bfloat16)[:, None, :, None]
        ).reshape(total_rows, block_arcs)
        masked = lax.all_gather(masked, "arc")
        own_mask = jnp.zeros((block_arcs,), jnp.float32).at[fleet_slots].set(1.0)
        per_arc = lax.all_gather(jnp.stack([arc_cost, capacity, own_mask]), "arc", axis=1, tiled=True)
        shares = jnp.broadcast_to(weights.astype(jnp.float32)[:, None], (1, 128))
        per_scen = lax.all_gather(jnp.concatenate([demand, shares], axis=1), "scen", tiled=True)
        outs = pl.pallas_call(
            plain_kernel,
            out_shape=out_shape,
            in_specs=[VMEM] * 7,
            out_specs=out_specs,
            scratch_shapes=state,
            compiler_params=limit(48),
            cost_estimate=cost,
            name="whole",
        )(masked, per_arc[0:1], per_arc[1:2], per_arc[2:3], per_scen[:, :total_rows],
          per_scen[:, total_rows:], slots)
    flows, duals, multipliers, consensus, spread = outs
    return flows, duals, multipliers, consensus.reshape(-1), spread


def solution(mesh):
    in_specs = (
        P(None, "arc"),
        P(None, "arc"),
        P("arc"),
        P("arc"),
        P("scen", None),
        P("scen"),
        P("arc"),
    )
    out_specs = (P("scen", "arc"), P("scen", "arc"), P("scen", "arc"), P("arc"), P())
    return jax.shard_map(body, mesh=mesh, in_specs=in_specs, out_specs=out_specs, check_vma=False)
```

```python
import functools

import jax
import jax.numpy as jnp
from jax import lax
from jax.experimental import pallas as pl
from jax.experimental.pallas import tpu as pltpu
from jax.sharding import PartitionSpec as P

TILE = 128
ITERS = 4
ROUNDS = 2
EXTRA = 16
GROUPS = ((0, 1, 2, 3, 4, 5, 6, 7),)

primal_step = 0.9
dual_step = 0.9
penalty = 1.0

VMEM = pl.BlockSpec(memory_space=pltpu.VMEM)
SMEM = pl.BlockSpec(memory_space=pltpu.SMEM)
ANY = pl.BlockSpec(memory_space=pl.ANY)


def pieces(value):
    high = value.astype(jnp.bfloat16)
    rest = value - high.astype(jnp.float32)
    middle = rest.astype(jnp.bfloat16)
    low = (rest - middle.astype(jnp.float32)).astype(jnp.bfloat16)
    return high, middle, low


def one_hot(slots, block_arcs):
    arcs = lax.broadcasted_iota(jnp.int32, (block_arcs, slots.shape[1]), 0)
    return jnp.where(arcs == slots, 1.0, 0.0).astype(jnp.bfloat16)


def fleet_mask(slots, block_arcs):
    ones = jnp.ones((8, slots.shape[1]), jnp.bfloat16)
    hits = lax.dot_general(ones, one_hot(slots, block_arcs), (((1,), (1,)), ((), ())),
                           preferred_element_type=jnp.float32)
    return hits[:1]


def own_row(value, scen):
    rows = lax.broadcasted_iota(jnp.int32, value.shape, 0)
    return jnp.sum(jnp.where(rows == scen, value, 0.0), axis=0, keepdims=True)


def narrow_kernel(coupling, incidence, arc_cost, capacity, demand, weights, slots, out, weight, sems):
    half = out.shape[0] - EXTRA
    block_arcs = out.shape[1]
    scen = lax.axis_index("scen")
    chip = scen // 2
    first = pl.multiple_of(scen * half, half)
    copies = [
        pltpu.make_async_copy(weights, weight, sems.at[0]),
        pltpu.make_async_copy(coupling.at[pl.ds(first, half)], out.at[pl.ds(0, half)], sems.at[1]),
    ]
    for copy in copies:
        copy.start()
    mask = fleet_mask(slots[...], block_arcs)
    touch = []
    for part in range(incidence.shape[0]):
        owner = jnp.bitwise_xor(chip, part)
        touch.append(jnp.concatenate(
            [jnp.full((1, TILE), incidence[owner, tile].astype(jnp.float32))
             for tile in range(block_arcs // TILE)], axis=1))
    copies[0].wait()
    share = jnp.full((1, 128), weight[0].astype(jnp.float32))
    share = jnp.concatenate([*pieces(share), jnp.zeros((1, 128), jnp.bfloat16)], axis=1)
    lines = [*pieces(arc_cost[...]), *pieces(capacity[...]), mask, *pieces(demand[...]), share, *touch]
    lines = [line.astype(jnp.float32) for line in lines]
    lines += [jnp.zeros((1, block_arcs), jnp.float32)] * (EXTRA - len(lines))
    out[half:, :] = jnp.concatenate(lines, axis=0).astype(jnp.bfloat16)
    copies[1].wait()


def pack_kernel(coupling, narrow, near, across, rows_in, sems):
    half = TILE // 2
    chip = lax.axis_index("scen") // 2
    chips = rows_in.shape[0] // TILE
    copies = []
    for part in range(chips):
        first = pl.multiple_of(jnp.bitwise_xor(chip, part) * TILE, TILE)
        copies.append(pltpu.make_async_copy(
            coupling.at[pl.ds(first, TILE)], rows_in.at[pl.ds(part * TILE, TILE)], sems.at[part]))
    for copy in copies:
        copy.start()
    extra = narrow[half:, :]
    across[TILE:, :] = extra
    touch = extra.astype(jnp.float32)[11:11 + chips].astype(jnp.bfloat16)
    for part in range(chips):
        copies[part].wait()
        rows = slice(part * TILE, (part + 1) * TILE)
        near[rows, :] = rows_in[rows, :] * touch[part:part + 1]
    across[:TILE, :] = near[(chips - 1) * TILE:, :]


def rounds(masked, turned, blocks, cost, cap, mask, demand, share, fleet_count, spread_out,
           flows, duals, prices, centre, shifted):
    scenarios, total_rows = demand.shape
    block_arcs = cost.shape[1] // blocks
    weight_sum = jnp.sum(share[:, :1])
    for round_index in range(ROUNDS):
        for step_index in range(ITERS):
            first = round_index == 0 and step_index == 0
            load = jnp.zeros((scenarios, total_rows), jnp.float32)
            if not first:
                duals_low = duals[...].astype(jnp.bfloat16)
            for block in range(blocks):
                cols = slice(block * block_arcs, (block + 1) * block_arcs)
                if first:
                    gradient = jnp.broadcast_to(cost[:, cols], (scenarios, block_arcs))
                    old = jnp.zeros((scenarios, block_arcs), jnp.float32)
                else:
                    old = flows[:, cols]
                    pull = jnp.dot(duals_low, masked(block), preferred_element_type=jnp.float32)
                    push = penalty * mask[:, cols] * old
                    if round_index > 0:
                        push = push + shifted[:, cols]
                    gradient = cost[:, cols] + pull + push
                new = jnp.clip(old - primal_step * gradient, 0.0, cap[:, cols])
                flows[:, cols] = new
                bar = (2.0 * new - old).astype(jnp.bfloat16)
                load = load + jnp.dot(bar, turned(block), preferred_element_type=jnp.float32)
            step = dual_step * (load - demand[...])
            duals[...] = jnp.maximum(step if first else duals[...] + step, 0.0)
        squares = jnp.float32(0.0)
        for block in range(blocks):
            cols = slice(block * block_arcs, (block + 1) * block_arcs)
            fleet = flows[:, cols] * mask[:, cols]
            share_col = share[:, :1]
            mean = jnp.sum(share_col * fleet, axis=0, keepdims=True) / weight_sum
            gap = fleet - mean
            squares = squares + jnp.sum(share_col * gap * gap)
            total = penalty * gap if round_index == 0 else prices[:, cols] + penalty * gap
            prices[:, cols] = total
            centre[:, cols] = mean
            shifted[:, cols] = total - penalty * mean
        spread_out[round_index] = jnp.sqrt(squares / (weight_sum * fleet_count) + 1e-06)


def pick_fleet(price, mean, slots):
    picked = [line.astype(jnp.float32) for line in (*pieces(price), *pieces(mean))]
    picked += [jnp.zeros_like(price)] * 2
    picked = jnp.dot(jnp.concatenate(picked, axis=0).astype(jnp.bfloat16),
                     one_hot(slots, price.shape[1]), preferred_element_type=jnp.float32)
    return picked[0:1] + picked[1:2] + picked[2:3], picked[3:4] + picked[4:5] + picked[5:6]


def plain_kernel(masked, cost, cap, mask, demand, share, slots, flows_out, duals_out, mult_out, cons_out,
                 spread_out, flows, duals, prices, centre, shifted):
    blocks, total_rows, block_arcs = masked.shape
    rounds(lambda block: masked[block], lambda block: masked[block].T, blocks, cost, cap, mask, demand, share, slots.shape[1] * blocks,
           spread_out, flows, duals, prices, centre, shifted)
    scen, arc = lax.axis_index("scen"), lax.axis_index("arc")
    own = pl.ds(pl.multiple_of(arc * block_arcs, block_arcs), block_arcs)
    share_rows = total_rows // blocks
    own_rows = pl.ds(pl.multiple_of(arc * share_rows, share_rows), share_rows)
    flows_out[...] = own_row(flows[:, own], scen)
    duals_out[...] = own_row(duals[:, own_rows], scen)
    mult_out[...], cons_out[...] = pick_fleet(own_row(prices[:, own], scen), centre[:, own], slots[...])


def whole_kernel(near, own, *refs):
    brought, others = refs[:8], [None] * 8
    for group, joined in zip(GROUPS, refs[8:]):
        first = 0
        for part in group:
            rows = brought[part].shape[0]
            others[part] = joined.at[pl.ds(first, rows)]
            first += rows
    wides, narrows = (brought[:4], others[:4]), (brought[4:], others[4:])
    (slots, flows_out, duals_out, mult_out, cons_out, spread_out,
     blocks_in, turned, cost, cap, mask, demand_in, demand, share, flows, duals, prices, centre, shifted) = refs[8 + len(GROUPS):]
    total_rows, block_arcs = near.shape
    scen, arc = lax.axis_index("scen"), lax.axis_index("arc")
    chip, core = scen // 2, lax.rem(scen, 2)
    chips = total_rows // TILE
    half = TILE // 2
    tails = [own[TILE:, :], wides[0][3][TILE:, :], wides[1][3][TILE:, :], narrows[0][0][half:, :]]
    touch = []
    for block, tail in enumerate(tails):
        cols = slice(block * block_arcs, (block + 1) * block_arcs)
        tail = tail.astype(jnp.float32)
        cost[:, cols] = tail[0:1] + tail[1:2] + tail[2:3]
        cap[:, cols] = tail[3:4] + tail[4:5] + tail[5:6]
        mask[:, cols] = tail[6:7]
        touch.append(tail[11:11 + chips].astype(jnp.bfloat16))
    for row in range(2 * chips):
        tail = narrows[row % 2][row // 2][half:, :].astype(jnp.float32)
        demand_in[row:row + 1, :] = tail[7:8] + tail[8:9] + tail[9:10]
        share[row:row + 1, :] = tail[10:11, :128] + tail[10:11, 128:256] + tail[10:11, 256:384]
    for part in range(chips):
        owner = jnp.bitwise_xor(chip, part)
        rows = slice(part * TILE, (part + 1) * TILE)
        demand[:, rows] = demand_in[:, pl.ds(pl.multiple_of(owner * TILE, TILE), TILE)]
        for side in range(2):
            wide = wides[side][part][:TILE, :]
            if part < chips - 1:
                wide = wide * touch[1 + side][part:part + 1]
            blocks_in[side, rows, :] = wide
            place = jnp.where(core == side, 0, half)
            place = pl.ds(pl.multiple_of(part * TILE + place, half), half)
            blocks_in[2, place, :] = narrows[side][part][:half, :] * touch[3][part:part + 1]

    def masked(block):
        return near[...] if block == 0 else blocks_in[block - 1]

    for block in range(len(tails)):
        turned[block] = masked(block).T
    rounds(masked, lambda block: turned[block], len(tails), cost, cap, mask, demand, share, slots.shape[1] * len(tails),
           spread_out, flows, duals, prices, centre, shifted)
    flows_out[...] = flows[0:1, :block_arcs]
    first = pl.multiple_of(jnp.bitwise_xor(chip, arc) * TILE, TILE)
    duals_out[...] = duals[:, pl.ds(first, TILE)][0:1]
    mult_out[...], cons_out[...] = pick_fleet(prices[0:1, :block_arcs], centre[:, :block_arcs], slots[...])


def swap(value, partner):
    scenarios, blocks = lax.axis_size("scen"), lax.axis_size("arc")
    pairs = []
    for scen in range(scenarios):
        for arc in range(blocks):
            other_scen, other_arc = partner(scen, arc)
            pairs.append((scen * blocks + arc, other_scen * blocks + other_arc))
    return lax.ppermute(value, ("scen", "arc"), pairs)


def bring(coupling, narrow, across):
    scen = lax.axis_index("scen")
    wide = lax.dynamic_slice_in_dim(coupling, lax.shift_right_logical(scen, 1) * TILE, TILE, 0)
    wide = swap(wide, lambda scen, arc: (scen, arc ^ (1 + scen % 2)))
    line = swap(narrow, lambda scen, arc: (scen, arc ^ 3))
    side, front = (lambda scen, arc: (scen ^ 2, arc)), (lambda scen, arc: (scen ^ 4, arc))
    wides = [wide, swap(wide, side), swap(wide, front)]
    wides.append(swap(across, lambda scen, arc: (scen, arc ^ (1 + scen % 2))))
    narrows = [line, swap(line, side), swap(line, front), swap(line, lambda scen, arc: (scen ^ 6, arc))]
    other = lambda scen, arc: (scen ^ 1, arc)
    brought = wides + narrows
    joined = [jnp.concatenate([brought[part] for part in group], axis=0) for group in GROUPS]
    return brought + [swap(parts, other) for parts in joined]


def body(coupling, incidence, arc_cost, capacity, demand, weights, fleet_slots):
    total_rows, block_arcs = coupling.shape
    scenarios, blocks = lax.axis_size("scen"), lax.axis_size("arc")
    arcs = blocks * block_arcs
    fleet_block = fleet_slots.shape[0]
    row = lambda value: value.reshape(1, -1)
    slots = row(fleet_slots)
    out_shape = (
        jax.ShapeDtypeStruct((1, block_arcs), jnp.float32),
        jax.ShapeDtypeStruct((1, total_rows // blocks), jnp.float32),
        jax.ShapeDtypeStruct((1, fleet_block), jnp.float32),
        jax.ShapeDtypeStruct((1, fleet_block), jnp.float32),
        jax.ShapeDtypeStruct((ROUNDS,), jnp.float32),
    )
    out_specs = (VMEM, VMEM, VMEM, VMEM, SMEM)
    state = [
        pltpu.VMEM((scenarios, arcs), jnp.float32),
        pltpu.VMEM((scenarios, total_rows), jnp.float32),
        pltpu.VMEM((scenarios, arcs), jnp.float32),
        pltpu.VMEM((1, arcs), jnp.float32),
        pltpu.VMEM((scenarios, arcs), jnp.float32),
    ]
    limit = lambda mib: pltpu.CompilerParams(vmem_limit_bytes=mib * 1024 * 1024)
    cost = pl.CostEstimate(
        flops=4 * ROUNDS * ITERS * scenarios * total_rows * arcs,
        bytes_accessed=2 * total_rows * arcs,
        transcendentals=0,
    )
    fits = (scenarios, blocks) == (8, 4)
    if fits and total_rows == TILE * 4:
        like = lambda rows: jax.ShapeDtypeStruct((rows, block_arcs), jnp.bfloat16)
        narrow = pl.pallas_call(
            narrow_kernel,
            out_shape=like(TILE // 2 + EXTRA),
            in_specs=[ANY, SMEM, VMEM, VMEM, VMEM, ANY, VMEM],
            out_specs=VMEM,
            scratch_shapes=[pltpu.SMEM((1,), jnp.int32), pltpu.SemaphoreType.DMA((2,))],
            compiler_params=limit(56),
            name="narrow",
        )(coupling, incidence, row(arc_cost), row(capacity), demand, weights, slots)
        near, across = pl.pallas_call(
            pack_kernel,
            out_shape=(like(total_rows), like(TILE + EXTRA)),
            in_specs=[ANY, VMEM],
            out_specs=(VMEM,) * 2,
            scratch_shapes=[
                pltpu.VMEM((total_rows, block_arcs), jnp.bfloat16),
                pltpu.SemaphoreType.DMA((total_rows // TILE,)),
            ],
            compiler_params=limit(8),
            name="pack",
        )(coupling, narrow)
        brought = bring(coupling, narrow, across)
        outs = pl.pallas_call(
            whole_kernel,
            out_shape=out_shape,
            in_specs=[VMEM] * (len(brought) + 3),
            out_specs=out_specs,
            scratch_shapes=[
                pltpu.VMEM((blocks - 1, total_rows, block_arcs), jnp.bfloat16),
                pltpu.VMEM((blocks, block_arcs, total_rows), jnp.bfloat16),
                pltpu.VMEM((1, arcs), jnp.float32),
                pltpu.VMEM((1, arcs), jnp.float32),
                pltpu.VMEM((1, arcs), jnp.float32),
                pltpu.VMEM((scenarios, total_rows), jnp.float32),
                pltpu.VMEM((scenarios, total_rows), jnp.float32),
                pltpu.VMEM((scenarios, 128), jnp.float32),
                *state,
            ],
            compiler_params=limit(16),
            cost_estimate=cost,
            name="whole",
        )(near, across, *brought, slots)
    else:
        masked = (
            coupling.reshape(total_rows // TILE, TILE, block_arcs // TILE, TILE)
            * incidence.astype(jnp.bfloat16)[:, None, :, None]
        ).reshape(total_rows, block_arcs)
        masked = lax.all_gather(masked, "arc")
        own_mask = jnp.zeros((block_arcs,), jnp.float32).at[fleet_slots].set(1.0)
        per_arc = lax.all_gather(jnp.stack([arc_cost, capacity, own_mask]), "arc", axis=1, tiled=True)
        shares = jnp.broadcast_to(weights.astype(jnp.float32)[:, None], (1, 128))
        per_scen = lax.all_gather(jnp.concatenate([demand, shares], axis=1), "scen", tiled=True)
        outs = pl.pallas_call(
            plain_kernel,
            out_shape=out_shape,
            in_specs=[VMEM] * 7,
            out_specs=out_specs,
            scratch_shapes=state,
            compiler_params=limit(48),
            cost_estimate=cost,
            name="whole",
        )(masked, per_arc[0:1], per_arc[1:2], per_arc[2:3], per_scen[:, :total_rows],
          per_scen[:, total_rows:], slots)
    flows, duals, multipliers, consensus, spread = outs
    return flows, duals, multipliers, consensus.reshape(-1), spread


def solution(mesh):
    in_specs = (
        P(None, "arc"),
        P(None, "arc"),
        P("arc"),
        P("arc"),
        P("scen", None),
        P("scen"),
        P("arc"),
    )
    out_specs = (P("scen", "arc"), P("scen", "arc"), P("scen", "arc"), P("arc"), P())
    return jax.shard_map(body, mesh=mesh, in_specs=in_specs, out_specs=out_specs, check_vma=False)
```

```python
import functools

import jax
import jax.numpy as jnp
from jax import lax
from jax.experimental import pallas as pl
from jax.experimental.pallas import tpu as pltpu
from jax.sharding import PartitionSpec as P

TILE = 128
ITERS = 4
ROUNDS = 2
EXTRA = 16
GROUPS = ((0, 3, 4, 5), (1, 2))

primal_step = 0.9
dual_step = 0.9
penalty = 1.0

VMEM = pl.BlockSpec(memory_space=pltpu.VMEM)
SMEM = pl.BlockSpec(memory_space=pltpu.SMEM)
ANY = pl.BlockSpec(memory_space=pl.ANY)


def pieces(value):
    high = value.astype(jnp.bfloat16)
    rest = value - high.astype(jnp.float32)
    middle = rest.astype(jnp.bfloat16)
    low = (rest - middle.astype(jnp.float32)).astype(jnp.bfloat16)
    return high, middle, low


def one_hot(slots, block_arcs):
    arcs = lax.broadcasted_iota(jnp.int32, (block_arcs, slots.shape[1]), 0)
    return jnp.where(arcs == slots, 1.0, 0.0).astype(jnp.bfloat16)


def fleet_mask(slots, block_arcs):
    ones = jnp.ones((8, slots.shape[1]), jnp.bfloat16)
    hits = lax.dot_general(ones, one_hot(slots, block_arcs), (((1,), (1,)), ((), ())),
                           preferred_element_type=jnp.float32)
    return hits[:1]


def own_row(value, scen):
    rows = lax.broadcasted_iota(jnp.int32, value.shape, 0)
    return jnp.sum(jnp.where(rows == scen, value, 0.0), axis=0, keepdims=True)


def pack_kernel(coupling, incidence, arc_cost, capacity, demand, weights, slots,
                near, across, extra, rows_in, sems):
    total_rows, block_arcs = rows_in.shape
    chip = lax.axis_index("scen") // 2
    chips = total_rows // TILE
    copies = []
    for part in range(chips):
        first = pl.multiple_of(jnp.bitwise_xor(chip, part) * TILE, TILE)
        copies.append(pltpu.make_async_copy(
            coupling.at[pl.ds(first, TILE)], rows_in.at[pl.ds(part * TILE, TILE)], sems.at[part]))
    for copy in copies:
        copy.start()
    share = jnp.broadcast_to(weights[...].astype(jnp.float32), (1, 128))
    share = jnp.concatenate([*pieces(share), jnp.zeros((1, 128), jnp.bfloat16)], axis=1)
    mask = fleet_mask(slots[...], block_arcs)
    touch = []
    for part in range(chips):
        owner = jnp.bitwise_xor(chip, part)
        touch.append(jnp.concatenate(
            [jnp.full((1, TILE), incidence[owner, tile].astype(jnp.float32))
             for tile in range(block_arcs // TILE)], axis=1))
    lines = [*pieces(arc_cost[...]), *pieces(capacity[...]), mask, *pieces(demand[...]), share, *touch]
    lines = [line.astype(jnp.float32) for line in lines]
    lines += [jnp.zeros((1, block_arcs), jnp.float32)] * (EXTRA - len(lines))
    lines = jnp.concatenate(lines, axis=0).astype(jnp.bfloat16)
    extra[...] = lines
    across[TILE:, :] = lines
    for part in range(chips):
        copies[part].wait()
        rows = slice(part * TILE, (part + 1) * TILE)
        near[rows, :] = rows_in[rows, :] * touch[part].astype(jnp.bfloat16)
    across[:TILE, :] = near[(chips - 1) * TILE:, :]


def rounds(masked, turned, blocks, cost, cap, mask, demand, share, fleet_count, spread_out,
           flows, duals, prices, centre, shifted):
    scenarios, total_rows = demand.shape
    block_arcs = cost.shape[1] // blocks
    weight_sum = jnp.sum(share[:, :1])
    for round_index in range(ROUNDS):
        for step_index in range(ITERS):
            first = round_index == 0 and step_index == 0
            load = jnp.zeros((scenarios, total_rows), jnp.float32)
            if not first:
                duals_low = duals[...].astype(jnp.bfloat16)
            for block in range(blocks):
                cols = slice(block * block_arcs, (block + 1) * block_arcs)
                if first:
                    gradient = jnp.broadcast_to(cost[:, cols], (scenarios, block_arcs))
                    old = jnp.zeros((scenarios, block_arcs), jnp.float32)
                else:
                    old = flows[:, cols]
                    pull = jnp.dot(duals_low, masked(block), preferred_element_type=jnp.float32)
                    push = penalty * mask[:, cols] * old
                    if round_index > 0:
                        push = push + shifted[:, cols]
                    gradient = cost[:, cols] + pull + push
                new = jnp.clip(old - primal_step * gradient, 0.0, cap[:, cols])
                flows[:, cols] = new
                bar = (2.0 * new - old).astype(jnp.bfloat16)
                load = load + jnp.dot(bar, turned(block), preferred_element_type=jnp.float32)
            step = dual_step * (load - demand[...])
            duals[...] = jnp.maximum(step if first else duals[...] + step, 0.0)
        squares = jnp.float32(0.0)
        for block in range(blocks):
            cols = slice(block * block_arcs, (block + 1) * block_arcs)
            fleet = flows[:, cols] * mask[:, cols]
            share_col = share[:, :1]
            mean = jnp.sum(share_col * fleet, axis=0, keepdims=True) / weight_sum
            gap = fleet - mean
            squares = squares + jnp.sum(share_col * gap * gap)
            total = penalty * gap if round_index == 0 else prices[:, cols] + penalty * gap
            prices[:, cols] = total
            centre[:, cols] = mean
            shifted[:, cols] = total - penalty * mean
        spread_out[round_index] = jnp.sqrt(squares / (weight_sum * fleet_count) + 1e-06)


def pick_fleet(price, mean, slots):
    picked = [line.astype(jnp.float32) for line in (*pieces(price), *pieces(mean))]
    picked += [jnp.zeros_like(price)] * 2
    picked = jnp.dot(jnp.concatenate(picked, axis=0).astype(jnp.bfloat16),
                     one_hot(slots, price.shape[1]), preferred_element_type=jnp.float32)
    return picked[0:1] + picked[1:2] + picked[2:3], picked[3:4] + picked[4:5] + picked[5:6]


def plain_kernel(masked, cost, cap, mask, demand, share, slots, flows_out, duals_out, mult_out, cons_out,
                 spread_out, flows, duals, prices, centre, shifted):
    blocks, total_rows, block_arcs = masked.shape
    rounds(lambda block: masked[block], lambda block: masked[block].T, blocks, cost, cap, mask, demand, share, slots.shape[1] * blocks,
           spread_out, flows, duals, prices, centre, shifted)
    scen, arc = lax.axis_index("scen"), lax.axis_index("arc")
    own = pl.ds(pl.multiple_of(arc * block_arcs, block_arcs), block_arcs)
    share_rows = total_rows // blocks
    own_rows = pl.ds(pl.multiple_of(arc * share_rows, share_rows), share_rows)
    flows_out[...] = own_row(flows[:, own], scen)
    duals_out[...] = own_row(duals[:, own_rows], scen)
    mult_out[...], cons_out[...] = pick_fleet(own_row(prices[:, own], scen), centre[:, own], slots[...])


def whole_kernel(near, *refs):
    lines, others = refs[:6], [None] * 6
    for group, joined in zip(GROUPS, refs[6:]):
        first = 0
        for part in group:
            rows = lines[part].shape[0]
            others[part] = joined.at[pl.ds(first, rows)]
            first += rows
    (slots, flows_out, duals_out, mult_out, cons_out, spread_out,
     blocks_in, turned, cost, cap, mask, demand_in, demand, share, flows, duals, prices, centre, shifted) = refs[6 + len(GROUPS):]
    total_rows, block_arcs = near.shape
    scen, arc = lax.axis_index("scen"), lax.axis_index("arc")
    chip, core = scen // 2, lax.rem(scen, 2)
    chips = total_rows // TILE
    half = TILE // 2
    tails = [lines[0][TILE + half:, :], lines[3][TILE:, :], others[3][TILE:, :], refs[5][...]]
    touch = []
    for block, tail in enumerate(tails):
        cols = slice(block * block_arcs, (block + 1) * block_arcs)
        tail = tail.astype(jnp.float32)
        cost[:, cols] = tail[0:1] + tail[1:2] + tail[2:3]
        cap[:, cols] = tail[3:4] + tail[4:5] + tail[5:6]
        mask[:, cols] = tail[6:7]
        touch.append(tail[11:11 + chips].astype(jnp.bfloat16))
    for row in range(2 * chips):
        part, source = row // 2, others if row % 2 else lines
        tail = source[part][TILE + half:, :] if part < chips - 1 else source[4][half:, :]
        tail = tail.astype(jnp.float32)
        demand_in[row:row + 1, :] = tail[7:8] + tail[8:9] + tail[9:10]
        share[row:row + 1, :] = tail[10:11, :128] + tail[10:11, 128:256] + tail[10:11, 256:384]
    for part in range(chips):
        owner = jnp.bitwise_xor(chip, part)
        rows = slice(part * TILE, (part + 1) * TILE)
        demand[:, rows] = demand_in[:, pl.ds(pl.multiple_of(owner * TILE, TILE), TILE)]
        for side, source in enumerate((lines, others)):
            place = jnp.where(core == side, 0, half)
            place = pl.ds(pl.multiple_of(part * TILE + place, half), half)
            on = touch[3][part:part + 1]
            if part < chips - 1:
                blocks_in[side, rows, :] = source[part][:TILE, :] * touch[1 + side][part:part + 1]
                blocks_in[2, place, :] = source[part][TILE:TILE + half, :] * on
            else:
                blocks_in[side, rows, :] = source[3][:TILE, :]
                blocks_in[2, place, :] = source[4][:half, :] * on

    def masked(block):
        return near[...] if block == 0 else blocks_in[block - 1]

    for block in range(len(tails)):
        turned[block] = masked(block).T
    rounds(masked, lambda block: turned[block], len(tails), cost, cap, mask, demand, share, slots.shape[1] * len(tails),
           spread_out, flows, duals, prices, centre, shifted)
    flows_out[...] = flows[0:1, :block_arcs]
    first = pl.multiple_of(jnp.bitwise_xor(chip, arc) * TILE, TILE)
    duals_out[...] = duals[:, pl.ds(first, TILE)][0:1]
    mult_out[...], cons_out[...] = pick_fleet(prices[0:1, :block_arcs], centre[:, :block_arcs], slots[...])


def swap(value, partner):
    scenarios, blocks = lax.axis_size("scen"), lax.axis_size("arc")
    pairs = []
    for scen in range(scenarios):
        for arc in range(blocks):
            other_scen, other_arc = partner(scen, arc)
            pairs.append((scen * blocks + arc, other_scen * blocks + other_arc))
    return lax.ppermute(value, ("scen", "arc"), pairs)


def bring(coupling, across, extra):
    scen = lax.axis_index("scen")
    half = TILE // 2
    wide = lax.dynamic_slice_in_dim(coupling, lax.shift_right_logical(scen, 1) * TILE, TILE, 0)
    wide = lax.optimization_barrier(wide)
    narrow = lax.dynamic_slice_in_dim(wide, (scen & 1) * half, half, 0)
    wide = swap(wide, lambda scen, arc: (scen, arc ^ (1 + scen % 2)))
    narrow = swap(narrow, lambda scen, arc: (scen, arc ^ 3))
    line = jnp.concatenate([wide, narrow, extra], axis=0)
    line, across = lax.optimization_barrier((line, across))
    side = swap(line, lambda scen, arc: (scen ^ 2, arc))
    front = swap(line, lambda scen, arc: (scen ^ 4, arc))
    across = swap(across, lambda scen, arc: (scen, arc ^ (1 + scen % 2)))
    beyond = swap(jnp.concatenate([narrow, extra], axis=0), lambda scen, arc: (scen ^ 6, arc))
    extra = swap(extra, lambda scen, arc: (scen, arc ^ 3))
    brought = [line, side, front, across, beyond, extra]
    joined = [jnp.concatenate([brought[part] for part in group], axis=0) for group in GROUPS]
    return brought + [swap(parts, lambda scen, arc: (scen ^ 1, arc)) for parts in joined]


def body(coupling, incidence, arc_cost, capacity, demand, weights, fleet_slots):
    total_rows, block_arcs = coupling.shape
    scenarios, blocks = lax.axis_size("scen"), lax.axis_size("arc")
    arcs = blocks * block_arcs
    fleet_block = fleet_slots.shape[0]
    row = lambda value: value.reshape(1, -1)
    slots = row(fleet_slots)
    out_shape = (
        jax.ShapeDtypeStruct((1, block_arcs), jnp.float32),
        jax.ShapeDtypeStruct((1, total_rows // blocks), jnp.float32),
        jax.ShapeDtypeStruct((1, fleet_block), jnp.float32),
        jax.ShapeDtypeStruct((1, fleet_block), jnp.float32),
        jax.ShapeDtypeStruct((ROUNDS,), jnp.float32),
    )
    out_specs = (VMEM, VMEM, VMEM, VMEM, SMEM)
    state = [
        pltpu.VMEM((scenarios, arcs), jnp.float32),
        pltpu.VMEM((scenarios, total_rows), jnp.float32),
        pltpu.VMEM((scenarios, arcs), jnp.float32),
        pltpu.VMEM((1, arcs), jnp.float32),
        pltpu.VMEM((scenarios, arcs), jnp.float32),
    ]
    limit = lambda mib: pltpu.CompilerParams(vmem_limit_bytes=mib * 1024 * 1024)
    cost = pl.CostEstimate(
        flops=4 * ROUNDS * ITERS * scenarios * total_rows * arcs,
        bytes_accessed=2 * total_rows * arcs,
        transcendentals=0,
    )
    fits = (scenarios, blocks) == (8, 4)
    if fits and total_rows == TILE * 4:
        like = lambda rows: jax.ShapeDtypeStruct((rows, block_arcs), jnp.bfloat16)
        near, across, extra = pl.pallas_call(
            pack_kernel,
            out_shape=(like(total_rows), like(TILE + EXTRA), like(EXTRA)),
            in_specs=[ANY, SMEM, VMEM, VMEM, VMEM, VMEM, VMEM],
            out_specs=(VMEM,) * 3,
            scratch_shapes=[
                pltpu.VMEM((total_rows, block_arcs), jnp.bfloat16),
                pltpu.SemaphoreType.DMA((total_rows // TILE,)),
            ],
            compiler_params=limit(8),
            name="pack",
        )(coupling, incidence, row(arc_cost), row(capacity), demand, weights.reshape(1, 1), slots)
        brought = bring(coupling, across, extra)
        outs = pl.pallas_call(
            whole_kernel,
            out_shape=out_shape,
            in_specs=[VMEM] * (len(brought) + 2),
            out_specs=out_specs,
            scratch_shapes=[
                pltpu.VMEM((blocks - 1, total_rows, block_arcs), jnp.bfloat16),
                pltpu.VMEM((blocks, block_arcs, total_rows), jnp.bfloat16),
                pltpu.VMEM((1, arcs), jnp.float32),
                pltpu.VMEM((1, arcs), jnp.float32),
                pltpu.VMEM((1, arcs), jnp.float32),
                pltpu.VMEM((scenarios, total_rows), jnp.float32),
                pltpu.VMEM((scenarios, total_rows), jnp.float32),
                pltpu.VMEM((scenarios, 128), jnp.float32),
                *state,
            ],
            compiler_params=limit(16),
            cost_estimate=cost,
            name="whole",
        )(near, *brought, slots)
    else:
        masked = (
            coupling.reshape(total_rows // TILE, TILE, block_arcs // TILE, TILE)
            * incidence.astype(jnp.bfloat16)[:, None, :, None]
        ).reshape(total_rows, block_arcs)
        masked = lax.all_gather(masked, "arc")
        own_mask = jnp.zeros((block_arcs,), jnp.float32).at[fleet_slots].set(1.0)
        per_arc = lax.all_gather(jnp.stack([arc_cost, capacity, own_mask]), "arc", axis=1, tiled=True)
        shares = jnp.broadcast_to(weights.astype(jnp.float32)[:, None], (1, 128))
        per_scen = lax.all_gather(jnp.concatenate([demand, shares], axis=1), "scen", tiled=True)
        outs = pl.pallas_call(
            plain_kernel,
            out_shape=out_shape,
            in_specs=[VMEM] * 7,
            out_specs=out_specs,
            scratch_shapes=state,
            compiler_params=limit(48),
            cost_estimate=cost,
            name="whole",
        )(masked, per_arc[0:1], per_arc[1:2], per_arc[2:3], per_scen[:, :total_rows],
          per_scen[:, total_rows:], slots)
    flows, duals, multipliers, consensus, spread = outs
    return flows, duals, multipliers, consensus.reshape(-1), spread


def solution(mesh):
    in_specs = (
        P(None, "arc"),
        P(None, "arc"),
        P("arc"),
        P("arc"),
        P("scen", None),
        P("scen"),
        P("arc"),
    )
    out_specs = (P("scen", "arc"), P("scen", "arc"), P("scen", "arc"), P("arc"), P())
    return jax.shard_map(body, mesh=mesh, in_specs=in_specs, out_specs=out_specs, check_vma=False)
```

```python
import functools

import jax
import jax.numpy as jnp
from jax import lax
from jax.experimental import pallas as pl
from jax.experimental.pallas import tpu as pltpu
from jax.sharding import PartitionSpec as P

TILE = 128
ITERS = 4
ROUNDS = 2
EXTRA = 16
GROUPS = ((0, 3, 4, 5), (1, 2))

primal_step = 0.9
dual_step = 0.9
penalty = 1.0

VMEM = pl.BlockSpec(memory_space=pltpu.VMEM)
SMEM = pl.BlockSpec(memory_space=pltpu.SMEM)
ANY = pl.BlockSpec(memory_space=pl.ANY)


def pieces(value):
    high = value.astype(jnp.bfloat16)
    rest = value - high.astype(jnp.float32)
    middle = rest.astype(jnp.bfloat16)
    low = (rest - middle.astype(jnp.float32)).astype(jnp.bfloat16)
    return high, middle, low


def one_hot(slots, block_arcs):
    arcs = lax.broadcasted_iota(jnp.int32, (block_arcs, slots.shape[1]), 0)
    return jnp.where(arcs == slots, 1.0, 0.0).astype(jnp.bfloat16)


def fleet_mask(slots, block_arcs):
    ones = jnp.ones((8, slots.shape[1]), jnp.bfloat16)
    hits = lax.dot_general(ones, one_hot(slots, block_arcs), (((1,), (1,)), ((), ())),
                           preferred_element_type=jnp.float32)
    return hits[:1]


def own_row(value, scen):
    rows = lax.broadcasted_iota(jnp.int32, value.shape, 0)
    return jnp.sum(jnp.where(rows == scen, value, 0.0), axis=0, keepdims=True)


def pack_kernel(coupling, incidence, arc_cost, capacity, demand, weights, slots,
                near, across, extra, rows_in, sems):
    total_rows, block_arcs = rows_in.shape
    chip = lax.axis_index("scen") // 2
    chips = total_rows // TILE
    copies = []
    for part in range(chips):
        first = pl.multiple_of(jnp.bitwise_xor(chip, part) * TILE, TILE)
        copies.append(pltpu.make_async_copy(
            coupling.at[pl.ds(first, TILE)], rows_in.at[pl.ds(part * TILE, TILE)], sems.at[part]))
    for copy in copies:
        copy.start()
    share = jnp.broadcast_to(weights[...].astype(jnp.float32), (1, 128))
    share = jnp.concatenate([*pieces(share), jnp.zeros((1, 128), jnp.bfloat16)], axis=1)
    mask = fleet_mask(slots[...], block_arcs)
    touch = []
    for part in range(chips):
        owner = jnp.bitwise_xor(chip, part)
        touch.append(jnp.concatenate(
            [jnp.full((1, TILE), incidence[owner, tile].astype(jnp.float32))
             for tile in range(block_arcs // TILE)], axis=1))
    lines = [*pieces(arc_cost[...]), *pieces(capacity[...]), mask, *pieces(demand[...]), share, *touch]
    lines = [line.astype(jnp.float32) for line in lines]
    lines += [jnp.zeros((1, block_arcs), jnp.float32)] * (EXTRA - len(lines))
    lines = jnp.concatenate(lines, axis=0).astype(jnp.bfloat16)
    extra[...] = lines
    across[TILE:, :] = lines
    for part in range(chips):
        copies[part].wait()
        rows = slice(part * TILE, (part + 1) * TILE)
        near[rows, :] = rows_in[rows, :] * touch[part].astype(jnp.bfloat16)
    across[:TILE, :] = near[(chips - 1) * TILE:, :]


def rounds(masked, turned, blocks, cost, cap, mask, demand, share, fleet_count, spread_out,
           flows, duals, prices, centre, shifted):
    scenarios, total_rows = demand.shape
    block_arcs = cost.shape[1] // blocks
    weight_sum = jnp.sum(share[:, :1])
    for round_index in range(ROUNDS):
        for step_index in range(ITERS):
            first = round_index == 0 and step_index == 0
            load = jnp.zeros((scenarios, total_rows), jnp.float32)
            if not first:
                duals_low = duals[...].astype(jnp.bfloat16)
            for block in range(blocks):
                cols = slice(block * block_arcs, (block + 1) * block_arcs)
                if first:
                    gradient = jnp.broadcast_to(cost[:, cols], (scenarios, block_arcs))
                    old = jnp.zeros((scenarios, block_arcs), jnp.float32)
                else:
                    old = flows[:, cols]
                    pull = jnp.dot(duals_low, masked(block), preferred_element_type=jnp.float32)
                    push = penalty * mask[:, cols] * old
                    if round_index > 0:
                        push = push + shifted[:, cols]
                    gradient = cost[:, cols] + pull + push
                new = jnp.clip(old - primal_step * gradient, 0.0, cap[:, cols])
                flows[:, cols] = new
                bar = (2.0 * new - old).astype(jnp.bfloat16)
                load = load + jnp.dot(bar, turned(block), preferred_element_type=jnp.float32)
            step = dual_step * (load - demand[...])
            duals[...] = jnp.maximum(step if first else duals[...] + step, 0.0)
        squares = jnp.float32(0.0)
        for block in range(blocks):
            cols = slice(block * block_arcs, (block + 1) * block_arcs)
            fleet = flows[:, cols] * mask[:, cols]
            share_col = share[:, :1]
            mean = jnp.sum(share_col * fleet, axis=0, keepdims=True) / weight_sum
            gap = fleet - mean
            squares = squares + jnp.sum(share_col * gap * gap)
            total = penalty * gap if round_index == 0 else prices[:, cols] + penalty * gap
            prices[:, cols] = total
            centre[:, cols] = mean
            shifted[:, cols] = total - penalty * mean
        spread_out[round_index] = jnp.sqrt(squares / (weight_sum * fleet_count) + 1e-06)


def pick_fleet(price, mean, slots):
    picked = [line.astype(jnp.float32) for line in (*pieces(price), *pieces(mean))]
    picked += [jnp.zeros_like(price)] * 2
    picked = jnp.dot(jnp.concatenate(picked, axis=0).astype(jnp.bfloat16),
                     one_hot(slots, price.shape[1]), preferred_element_type=jnp.float32)
    return picked[0:1] + picked[1:2] + picked[2:3], picked[3:4] + picked[4:5] + picked[5:6]


def plain_kernel(masked, cost, cap, mask, demand, share, slots, flows_out, duals_out, mult_out, cons_out,
                 spread_out, flows, duals, prices, centre, shifted):
    blocks, total_rows, block_arcs = masked.shape
    rounds(lambda block: masked[block], lambda block: masked[block].T, blocks, cost, cap, mask, demand, share, slots.shape[1] * blocks,
           spread_out, flows, duals, prices, centre, shifted)
    scen, arc = lax.axis_index("scen"), lax.axis_index("arc")
    own = pl.ds(pl.multiple_of(arc * block_arcs, block_arcs), block_arcs)
    share_rows = total_rows // blocks
    own_rows = pl.ds(pl.multiple_of(arc * share_rows, share_rows), share_rows)
    flows_out[...] = own_row(flows[:, own], scen)
    duals_out[...] = own_row(duals[:, own_rows], scen)
    mult_out[...], cons_out[...] = pick_fleet(own_row(prices[:, own], scen), centre[:, own], slots[...])


def ready_kernel(near, line, side, front, across, near_turned, mine, mine_turned):
    total_rows, block_arcs = near.shape
    chips = total_rows // TILE
    near_turned[...] = near[...].T
    touch = across[TILE:, :].astype(jnp.float32)[11:11 + chips].astype(jnp.bfloat16)
    for part, source in enumerate((line, side, front, across)):
        rows = slice(part * TILE, (part + 1) * TILE)
        wide = source[:TILE, :]
        mine[rows, :] = wide if part == chips - 1 else wide * touch[part:part + 1]
    mine_turned[...] = mine[...].T


def whole_kernel(near, near_turned, mine, mine_turned, *refs):
    lines, others = refs[:6], [None] * 6
    for group, joined in zip(GROUPS, refs[6:]):
        first = 0
        for part in group:
            rows = lines[part].shape[0]
            others[part] = joined.at[pl.ds(first, rows)]
            first += rows
    (slots, flows_out, duals_out, mult_out, cons_out, spread_out,
     blocks_in, turned, cost, cap, mask, demand_in, demand, share, flows, duals, prices, centre, shifted) = refs[6 + len(GROUPS):]
    total_rows, block_arcs = near.shape
    scen, arc = lax.axis_index("scen"), lax.axis_index("arc")
    chip, core = scen // 2, lax.rem(scen, 2)
    chips = total_rows // TILE
    half = TILE // 2
    tails = [lines[0][TILE + half:, :], lines[3][TILE:, :], others[3][TILE:, :], refs[5][...]]
    touch = []
    for block, tail in enumerate(tails):
        cols = slice(block * block_arcs, (block + 1) * block_arcs)
        tail = tail.astype(jnp.float32)
        cost[:, cols] = tail[0:1] + tail[1:2] + tail[2:3]
        cap[:, cols] = tail[3:4] + tail[4:5] + tail[5:6]
        mask[:, cols] = tail[6:7]
        touch.append(tail[11:11 + chips].astype(jnp.bfloat16))
    for row in range(2 * chips):
        part, source = row // 2, others if row % 2 else lines
        tail = source[part][TILE + half:, :] if part < chips - 1 else source[4][half:, :]
        tail = tail.astype(jnp.float32)
        demand_in[row:row + 1, :] = tail[7:8] + tail[8:9] + tail[9:10]
        share[row:row + 1, :] = tail[10:11, :128] + tail[10:11, 128:256] + tail[10:11, 256:384]
    for part in range(chips):
        owner = jnp.bitwise_xor(chip, part)
        rows = slice(part * TILE, (part + 1) * TILE)
        demand[:, rows] = demand_in[:, pl.ds(pl.multiple_of(owner * TILE, TILE), TILE)]
        wide = others[part][:TILE, :]
        blocks_in[0, rows, :] = wide if part == chips - 1 else wide * touch[2][part:part + 1]
        for side, source in enumerate((lines, others)):
            narrow = source[part][TILE:TILE + half, :] if part < chips - 1 else source[4][:half, :]
            place = jnp.where(core == side, 0, half)
            place = pl.ds(pl.multiple_of(part * TILE + place, half), half)
            blocks_in[1, place, :] = narrow * touch[3][part:part + 1]
    for block in range(2):
        turned[block] = blocks_in[block].T

    def masked(block):
        return (near, mine)[block][...] if block < 2 else blocks_in[block - 2]

    def masked_turned(block):
        return (near_turned, mine_turned)[block][...] if block < 2 else turned[block - 2]

    rounds(masked, masked_turned, len(tails), cost, cap, mask, demand, share, slots.shape[1] * len(tails),
           spread_out, flows, duals, prices, centre, shifted)
    flows_out[...] = flows[0:1, :block_arcs]
    first = pl.multiple_of(jnp.bitwise_xor(chip, arc) * TILE, TILE)
    duals_out[...] = duals[:, pl.ds(first, TILE)][0:1]
    mult_out[...], cons_out[...] = pick_fleet(prices[0:1, :block_arcs], centre[:, :block_arcs], slots[...])


def swap(value, partner):
    scenarios, blocks = lax.axis_size("scen"), lax.axis_size("arc")
    pairs = []
    for scen in range(scenarios):
        for arc in range(blocks):
            other_scen, other_arc = partner(scen, arc)
            pairs.append((scen * blocks + arc, other_scen * blocks + other_arc))
    return lax.ppermute(value, ("scen", "arc"), pairs)


def bring(coupling, across, extra):
    scen = lax.axis_index("scen")
    half = TILE // 2
    wide = lax.dynamic_slice_in_dim(coupling, lax.shift_right_logical(scen, 1) * TILE, TILE, 0)
    wide = lax.optimization_barrier(wide)
    narrow = lax.dynamic_slice_in_dim(wide, (scen & 1) * half, half, 0)
    wide = swap(wide, lambda scen, arc: (scen, arc ^ (1 + scen % 2)))
    narrow = swap(narrow, lambda scen, arc: (scen, arc ^ 3))
    line = jnp.concatenate([wide, narrow, extra], axis=0)
    line, across = lax.optimization_barrier((line, across))
    side = swap(line, lambda scen, arc: (scen ^ 2, arc))
    front = swap(line, lambda scen, arc: (scen ^ 4, arc))
    across = swap(across, lambda scen, arc: (scen, arc ^ (1 + scen % 2)))
    beyond = swap(jnp.concatenate([narrow, extra], axis=0), lambda scen, arc: (scen ^ 6, arc))
    extra = swap(extra, lambda scen, arc: (scen, arc ^ 3))
    brought = [line, side, front, across, beyond, extra]
    joined = [jnp.concatenate([brought[part] for part in group], axis=0) for group in GROUPS]
    return brought + [swap(parts, lambda scen, arc: (scen ^ 1, arc)) for parts in joined]


def body(coupling, incidence, arc_cost, capacity, demand, weights, fleet_slots):
    total_rows, block_arcs = coupling.shape
    scenarios, blocks = lax.axis_size("scen"), lax.axis_size("arc")
    arcs = blocks * block_arcs
    fleet_block = fleet_slots.shape[0]
    row = lambda value: value.reshape(1, -1)
    slots = row(fleet_slots)
    out_shape = (
        jax.ShapeDtypeStruct((1, block_arcs), jnp.float32),
        jax.ShapeDtypeStruct((1, total_rows // blocks), jnp.float32),
        jax.ShapeDtypeStruct((1, fleet_block), jnp.float32),
        jax.ShapeDtypeStruct((1, fleet_block), jnp.float32),
        jax.ShapeDtypeStruct((ROUNDS,), jnp.float32),
    )
    out_specs = (VMEM, VMEM, VMEM, VMEM, SMEM)
    state = [
        pltpu.VMEM((scenarios, arcs), jnp.float32),
        pltpu.VMEM((scenarios, total_rows), jnp.float32),
        pltpu.VMEM((scenarios, arcs), jnp.float32),
        pltpu.VMEM((1, arcs), jnp.float32),
        pltpu.VMEM((scenarios, arcs), jnp.float32),
    ]
    limit = lambda mib: pltpu.CompilerParams(vmem_limit_bytes=mib * 1024 * 1024)
    cost = pl.CostEstimate(
        flops=4 * ROUNDS * ITERS * scenarios * total_rows * arcs,
        bytes_accessed=2 * total_rows * arcs,
        transcendentals=0,
    )
    fits = (scenarios, blocks) == (8, 4)
    if fits and total_rows == TILE * 4:
        like = lambda rows: jax.ShapeDtypeStruct((rows, block_arcs), jnp.bfloat16)
        near, across, extra = pl.pallas_call(
            pack_kernel,
            out_shape=(like(total_rows), like(TILE + EXTRA), like(EXTRA)),
            in_specs=[ANY, SMEM, VMEM, VMEM, VMEM, VMEM, VMEM],
            out_specs=(VMEM,) * 3,
            scratch_shapes=[
                pltpu.VMEM((total_rows, block_arcs), jnp.bfloat16),
                pltpu.SemaphoreType.DMA((total_rows // TILE,)),
            ],
            compiler_params=limit(8),
            name="pack",
        )(coupling, incidence, row(arc_cost), row(capacity), demand, weights.reshape(1, 1), slots)
        brought = bring(coupling, across, extra)
        square = jax.ShapeDtypeStruct((block_arcs, total_rows), jnp.bfloat16)
        ready = pl.pallas_call(
            ready_kernel,
            out_shape=(square, like(total_rows), square),
            in_specs=[VMEM] * 5,
            out_specs=(VMEM,) * 3,
            compiler_params=limit(8),
            name="ready",
        )(near, *brought[:4])
        outs = pl.pallas_call(
            whole_kernel,
            out_shape=out_shape,
            in_specs=[VMEM] * (len(brought) + 5),
            out_specs=out_specs,
            scratch_shapes=[
                pltpu.VMEM((blocks - 2, total_rows, block_arcs), jnp.bfloat16),
                pltpu.VMEM((blocks - 2, block_arcs, total_rows), jnp.bfloat16),
                pltpu.VMEM((1, arcs), jnp.float32),
                pltpu.VMEM((1, arcs), jnp.float32),
                pltpu.VMEM((1, arcs), jnp.float32),
                pltpu.VMEM((scenarios, total_rows), jnp.float32),
                pltpu.VMEM((scenarios, total_rows), jnp.float32),
                pltpu.VMEM((scenarios, 128), jnp.float32),
                *state,
            ],
            compiler_params=limit(16),
            cost_estimate=cost,
            name="whole",
        )(near, *ready, *brought, slots)
    else:
        masked = (
            coupling.reshape(total_rows // TILE, TILE, block_arcs // TILE, TILE)
            * incidence.astype(jnp.bfloat16)[:, None, :, None]
        ).reshape(total_rows, block_arcs)
        masked = lax.all_gather(masked, "arc")
        own_mask = jnp.zeros((block_arcs,), jnp.float32).at[fleet_slots].set(1.0)
        per_arc = lax.all_gather(jnp.stack([arc_cost, capacity, own_mask]), "arc", axis=1, tiled=True)
        shares = jnp.broadcast_to(weights.astype(jnp.float32)[:, None], (1, 128))
        per_scen = lax.all_gather(jnp.concatenate([demand, shares], axis=1), "scen", tiled=True)
        outs = pl.pallas_call(
            plain_kernel,
            out_shape=out_shape,
            in_specs=[VMEM] * 7,
            out_specs=out_specs,
            scratch_shapes=state,
            compiler_params=limit(48),
            cost_estimate=cost,
            name="whole",
        )(masked, per_arc[0:1], per_arc[1:2], per_arc[2:3], per_scen[:, :total_rows],
          per_scen[:, total_rows:], slots)
    flows, duals, multipliers, consensus, spread = outs
    return flows, duals, multipliers, consensus.reshape(-1), spread


def solution(mesh):
    in_specs = (
        P(None, "arc"),
        P(None, "arc"),
        P("arc"),
        P("arc"),
        P("scen", None),
        P("scen"),
        P("arc"),
    )
    out_specs = (P("scen", "arc"), P("scen", "arc"), P("scen", "arc"), P("arc"), P())
    return jax.shard_map(body, mesh=mesh, in_specs=in_specs, out_specs=out_specs, check_vma=False)
```

```python
import functools

import jax
import jax.numpy as jnp
from jax import lax
from jax.experimental import pallas as pl
from jax.experimental.pallas import tpu as pltpu
from jax.sharding import PartitionSpec as P

TILE = 128
ITERS = 4
ROUNDS = 2
EXTRA = 16
GROUPS = ((0, 3, 4, 5), (1, 2))

primal_step = 0.9
dual_step = 0.9
penalty = 1.0

VMEM = pl.BlockSpec(memory_space=pltpu.VMEM)
SMEM = pl.BlockSpec(memory_space=pltpu.SMEM)
ANY = pl.BlockSpec(memory_space=pl.ANY)


def pieces(value):
    high = value.astype(jnp.bfloat16)
    rest = value - high.astype(jnp.float32)
    middle = rest.astype(jnp.bfloat16)
    low = (rest - middle.astype(jnp.float32)).astype(jnp.bfloat16)
    return high, middle, low


def one_hot(slots, block_arcs):
    arcs = lax.broadcasted_iota(jnp.int32, (block_arcs, slots.shape[1]), 0)
    return jnp.where(arcs == slots, 1.0, 0.0).astype(jnp.bfloat16)


def fleet_mask(slots, block_arcs):
    ones = jnp.ones((8, slots.shape[1]), jnp.bfloat16)
    hits = lax.dot_general(ones, one_hot(slots, block_arcs), (((1,), (1,)), ((), ())),
                           preferred_element_type=jnp.float32)
    return hits[:1]


def own_row(value, scen):
    rows = lax.broadcasted_iota(jnp.int32, value.shape, 0)
    return jnp.sum(jnp.where(rows == scen, value, 0.0), axis=0, keepdims=True)


def pack_kernel(coupling, incidence, arc_cost, capacity, demand, weights, slots,
                near, across, extra, rows_in, sems):
    total_rows, block_arcs = rows_in.shape
    chip = lax.axis_index("scen") // 2
    chips = total_rows // TILE
    copies = []
    for part in range(chips):
        first = pl.multiple_of(jnp.bitwise_xor(chip, part) * TILE, TILE)
        copies.append(pltpu.make_async_copy(
            coupling.at[pl.ds(first, TILE)], rows_in.at[pl.ds(part * TILE, TILE)], sems.at[part]))
    for copy in copies:
        copy.start()
    share = jnp.broadcast_to(weights[...].astype(jnp.float32), (1, 128))
    share = jnp.concatenate([*pieces(share), jnp.zeros((1, 128), jnp.bfloat16)], axis=1)
    mask = fleet_mask(slots[...], block_arcs)
    touch = []
    for part in range(chips):
        owner = jnp.bitwise_xor(chip, part)
        touch.append(jnp.concatenate(
            [jnp.full((1, TILE), incidence[owner, tile].astype(jnp.float32))
             for tile in range(block_arcs // TILE)], axis=1))
    lines = [*pieces(arc_cost[...]), *pieces(capacity[...]), mask, *pieces(demand[...]), share, *touch]
    lines = [line.astype(jnp.float32) for line in lines]
    lines += [jnp.zeros((1, block_arcs), jnp.float32)] * (EXTRA - len(lines))
    lines = jnp.concatenate(lines, axis=0).astype(jnp.bfloat16)
    extra[...] = lines
    across[TILE:, :] = lines
    for part in range(chips):
        copies[part].wait()
        rows = slice(part * TILE, (part + 1) * TILE)
        near[rows, :] = rows_in[rows, :] * touch[part].astype(jnp.bfloat16)
    across[:TILE, :] = near[(chips - 1) * TILE:, :]


def rounds(masked, turned, blocks, joined, cost, cap, mask, demand, share, fleet_count, spread_out,
           flows, duals, prices, centre, shifted):
    scenarios, total_rows = demand.shape
    block_arcs = cost.shape[1] // blocks
    weight_sum = jnp.sum(share[:, :1])
    for round_index in range(ROUNDS):
        for step_index in range(ITERS):
            first = round_index == 0 and step_index == 0
            load = jnp.zeros((scenarios, total_rows), jnp.float32)
            if not first:
                duals_low = duals[...].astype(jnp.bfloat16)
            for start in range(0, blocks, joined):
                group = range(start, start + joined)
                if not first:
                    weights = jnp.concatenate([masked(block) for block in group], axis=1)
                    pulls = jnp.dot(duals_low, weights, preferred_element_type=jnp.float32)
                bars = []
                for block in group:
                    cols = slice(block * block_arcs, (block + 1) * block_arcs)
                    if first:
                        gradient = jnp.broadcast_to(cost[:, cols], (scenarios, block_arcs))
                        old = jnp.zeros((scenarios, block_arcs), jnp.float32)
                    else:
                        old = flows[:, cols]
                        pull = pulls[:, (block - start) * block_arcs:(block - start + 1) * block_arcs]
                        push = penalty * mask[:, cols] * old
                        if round_index > 0:
                            push = push + shifted[:, cols]
                        gradient = cost[:, cols] + pull + push
                    new = jnp.clip(old - primal_step * gradient, 0.0, cap[:, cols])
                    flows[:, cols] = new
                    bars.append((2.0 * new - old).astype(jnp.bfloat16))
                weights = jnp.concatenate([turned(block) for block in group], axis=0)
                load = load + jnp.dot(jnp.concatenate(bars, axis=1), weights, preferred_element_type=jnp.float32)
            step = dual_step * (load - demand[...])
            duals[...] = jnp.maximum(step if first else duals[...] + step, 0.0)
        squares = jnp.float32(0.0)
        for block in range(blocks):
            cols = slice(block * block_arcs, (block + 1) * block_arcs)
            fleet = flows[:, cols] * mask[:, cols]
            share_col = share[:, :1]
            mean = jnp.sum(share_col * fleet, axis=0, keepdims=True) / weight_sum
            gap = fleet - mean
            squares = squares + jnp.sum(share_col * gap * gap)
            total = penalty * gap if round_index == 0 else prices[:, cols] + penalty * gap
            prices[:, cols] = total
            centre[:, cols] = mean
            shifted[:, cols] = total - penalty * mean
        spread_out[round_index] = jnp.sqrt(squares / (weight_sum * fleet_count) + 1e-06)


def pick_fleet(price, mean, slots):
    picked = [line.astype(jnp.float32) for line in (*pieces(price), *pieces(mean))]
    picked += [jnp.zeros_like(price)] * 2
    picked = jnp.dot(jnp.concatenate(picked, axis=0).astype(jnp.bfloat16),
                     one_hot(slots, price.shape[1]), preferred_element_type=jnp.float32)
    return picked[0:1] + picked[1:2] + picked[2:3], picked[3:4] + picked[4:5] + picked[5:6]


def plain_kernel(masked, cost, cap, mask, demand, share, slots, flows_out, duals_out, mult_out, cons_out,
                 spread_out, flows, duals, prices, centre, shifted):
    blocks, total_rows, block_arcs = masked.shape
    rounds(lambda block: masked[block], lambda block: masked[block].T, blocks, 1, cost, cap, mask, demand, share, slots.shape[1] * blocks,
           spread_out, flows, duals, prices, centre, shifted)
    scen, arc = lax.axis_index("scen"), lax.axis_index("arc")
    own = pl.ds(pl.multiple_of(arc * block_arcs, block_arcs), block_arcs)
    share_rows = total_rows // blocks
    own_rows = pl.ds(pl.multiple_of(arc * share_rows, share_rows), share_rows)
    flows_out[...] = own_row(flows[:, own], scen)
    duals_out[...] = own_row(duals[:, own_rows], scen)
    mult_out[...], cons_out[...] = pick_fleet(own_row(prices[:, own], scen), centre[:, own], slots[...])


def ready_kernel(near, line, side, front, across, near_turned, mine, mine_turned):
    total_rows, block_arcs = near.shape
    chips = total_rows // TILE
    near_turned[...] = near[...].T
    touch = across[TILE:, :].astype(jnp.float32)[11:11 + chips].astype(jnp.bfloat16)
    for part, source in enumerate((line, side, front, across)):
        rows = slice(part * TILE, (part + 1) * TILE)
        wide = source[:TILE, :]
        mine[rows, :] = wide if part == chips - 1 else wide * touch[part:part + 1]
    mine_turned[...] = mine[...].T


def whole_kernel(near, near_turned, mine, mine_turned, *refs):
    lines, others = refs[:6], [None] * 6
    for group, joined in zip(GROUPS, refs[6:]):
        first = 0
        for part in group:
            rows = lines[part].shape[0]
            others[part] = joined.at[pl.ds(first, rows)]
            first += rows
    (slots, flows_out, duals_out, mult_out, cons_out, spread_out,
     blocks_in, turned, cost, cap, mask, demand_in, demand, share, flows, duals, prices, centre, shifted) = refs[6 + len(GROUPS):]
    total_rows, block_arcs = near.shape
    scen, arc = lax.axis_index("scen"), lax.axis_index("arc")
    chip, core = scen // 2, lax.rem(scen, 2)
    chips = total_rows // TILE
    half = TILE // 2
    tails = [lines[0][TILE + half:, :], lines[3][TILE:, :], others[3][TILE:, :], refs[5][...]]
    touch = []
    for block, tail in enumerate(tails):
        cols = slice(block * block_arcs, (block + 1) * block_arcs)
        tail = tail.astype(jnp.float32)
        cost[:, cols] = tail[0:1] + tail[1:2] + tail[2:3]
        cap[:, cols] = tail[3:4] + tail[4:5] + tail[5:6]
        mask[:, cols] = tail[6:7]
        touch.append(tail[11:11 + chips].astype(jnp.bfloat16))
    for row in range(2 * chips):
        part, source = row // 2, others if row % 2 else lines
        tail = source[part][TILE + half:, :] if part < chips - 1 else source[4][half:, :]
        tail = tail.astype(jnp.float32)
        demand_in[row:row + 1, :] = tail[7:8] + tail[8:9] + tail[9:10]
        share[row:row + 1, :] = tail[10:11, :128] + tail[10:11, 128:256] + tail[10:11, 256:384]
    for part in range(chips):
        owner = jnp.bitwise_xor(chip, part)
        rows = slice(part * TILE, (part + 1) * TILE)
        demand[:, rows] = demand_in[:, pl.ds(pl.multiple_of(owner * TILE, TILE), TILE)]
        wide = others[part][:TILE, :]
        blocks_in[0, rows, :] = wide if part == chips - 1 else wide * touch[2][part:part + 1]
        for side, source in enumerate((lines, others)):
            narrow = source[part][TILE:TILE + half, :] if part < chips - 1 else source[4][:half, :]
            place = jnp.where(core == side, 0, half)
            place = pl.ds(pl.multiple_of(part * TILE + place, half), half)
            blocks_in[1, place, :] = narrow * touch[3][part:part + 1]
    for block in range(2):
        turned[block] = blocks_in[block].T

    def masked(block):
        return (near, mine)[block][...] if block < 2 else blocks_in[block - 2]

    def masked_turned(block):
        return (near_turned, mine_turned)[block][...] if block < 2 else turned[block - 2]

    rounds(masked, masked_turned, len(tails), len(tails), cost, cap, mask, demand, share, slots.shape[1] * len(tails),
           spread_out, flows, duals, prices, centre, shifted)
    flows_out[...] = flows[0:1, :block_arcs]
    first = pl.multiple_of(jnp.bitwise_xor(chip, arc) * TILE, TILE)
    duals_out[...] = duals[:, pl.ds(first, TILE)][0:1]
    mult_out[...], cons_out[...] = pick_fleet(prices[0:1, :block_arcs], centre[:, :block_arcs], slots[...])


def swap(value, partner):
    scenarios, blocks = lax.axis_size("scen"), lax.axis_size("arc")
    pairs = []
    for scen in range(scenarios):
        for arc in range(blocks):
            other_scen, other_arc = partner(scen, arc)
            pairs.append((scen * blocks + arc, other_scen * blocks + other_arc))
    return lax.ppermute(value, ("scen", "arc"), pairs)


def bring(coupling, across, extra):
    scen = lax.axis_index("scen")
    half = TILE // 2
    wide = lax.dynamic_slice_in_dim(coupling, lax.shift_right_logical(scen, 1) * TILE, TILE, 0)
    wide = lax.optimization_barrier(wide)
    narrow = lax.dynamic_slice_in_dim(wide, (scen & 1) * half, half, 0)
    wide = swap(wide, lambda scen, arc: (scen, arc ^ (1 + scen % 2)))
    narrow = swap(narrow, lambda scen, arc: (scen, arc ^ 3))
    line = jnp.concatenate([wide, narrow, extra], axis=0)
    line, across = lax.optimization_barrier((line, across))
    side = swap(line, lambda scen, arc: (scen ^ 2, arc))
    front = swap(line, lambda scen, arc: (scen ^ 4, arc))
    across = swap(across, lambda scen, arc: (scen, arc ^ (1 + scen % 2)))
    beyond = swap(jnp.concatenate([narrow, extra], axis=0), lambda scen, arc: (scen ^ 6, arc))
    extra = swap(extra, lambda scen, arc: (scen, arc ^ 3))
    brought = [line, side, front, across, beyond, extra]
    joined = [jnp.concatenate([brought[part] for part in group], axis=0) for group in GROUPS]
    return brought + [swap(parts, lambda scen, arc: (scen ^ 1, arc)) for parts in joined]


def body(coupling, incidence, arc_cost, capacity, demand, weights, fleet_slots):
    total_rows, block_arcs = coupling.shape
    scenarios, blocks = lax.axis_size("scen"), lax.axis_size("arc")
    arcs = blocks * block_arcs
    fleet_block = fleet_slots.shape[0]
    row = lambda value: value.reshape(1, -1)
    slots = row(fleet_slots)
    out_shape = (
        jax.ShapeDtypeStruct((1, block_arcs), jnp.float32),
        jax.ShapeDtypeStruct((1, total_rows // blocks), jnp.float32),
        jax.ShapeDtypeStruct((1, fleet_block), jnp.float32),
        jax.ShapeDtypeStruct((1, fleet_block), jnp.float32),
        jax.ShapeDtypeStruct((ROUNDS,), jnp.float32),
    )
    out_specs = (VMEM, VMEM, VMEM, VMEM, SMEM)
    state = [
        pltpu.VMEM((scenarios, arcs), jnp.float32),
        pltpu.VMEM((scenarios, total_rows), jnp.float32),
        pltpu.VMEM((scenarios, arcs), jnp.float32),
        pltpu.VMEM((1, arcs), jnp.float32),
        pltpu.VMEM((scenarios, arcs), jnp.float32),
    ]
    limit = lambda mib: pltpu.CompilerParams(vmem_limit_bytes=mib * 1024 * 1024)
    cost = pl.CostEstimate(
        flops=4 * ROUNDS * ITERS * scenarios * total_rows * arcs,
        bytes_accessed=2 * total_rows * arcs,
        transcendentals=0,
    )
    fits = (scenarios, blocks) == (8, 4)
    if fits and total_rows == TILE * 4:
        like = lambda rows: jax.ShapeDtypeStruct((rows, block_arcs), jnp.bfloat16)
        near, across, extra = pl.pallas_call(
            pack_kernel,
            out_shape=(like(total_rows), like(TILE + EXTRA), like(EXTRA)),
            in_specs=[ANY, SMEM, VMEM, VMEM, VMEM, VMEM, VMEM],
            out_specs=(VMEM,) * 3,
            scratch_shapes=[
                pltpu.VMEM((total_rows, block_arcs), jnp.bfloat16),
                pltpu.SemaphoreType.DMA((total_rows // TILE,)),
            ],
            compiler_params=limit(8),
            name="pack",
        )(coupling, incidence, row(arc_cost), row(capacity), demand, weights.reshape(1, 1), slots)
        brought = bring(coupling, across, extra)
        square = jax.ShapeDtypeStruct((block_arcs, total_rows), jnp.bfloat16)
        ready = pl.pallas_call(
            ready_kernel,
            out_shape=(square, like(total_rows), square),
            in_specs=[VMEM] * 5,
            out_specs=(VMEM,) * 3,
            compiler_params=limit(8),
            name="ready",
        )(near, *brought[:4])
        outs = pl.pallas_call(
            whole_kernel,
            out_shape=out_shape,
            in_specs=[VMEM] * (len(brought) + 5),
            out_specs=out_specs,
            scratch_shapes=[
                pltpu.VMEM((blocks - 2, total_rows, block_arcs), jnp.bfloat16),
                pltpu.VMEM((blocks - 2, block_arcs, total_rows), jnp.bfloat16),
                pltpu.VMEM((1, arcs), jnp.float32),
                pltpu.VMEM((1, arcs), jnp.float32),
                pltpu.VMEM((1, arcs), jnp.float32),
                pltpu.VMEM((scenarios, total_rows), jnp.float32),
                pltpu.VMEM((scenarios, total_rows), jnp.float32),
                pltpu.VMEM((scenarios, 128), jnp.float32),
                *state,
            ],
            compiler_params=limit(16),
            cost_estimate=cost,
            name="whole",
        )(near, *ready, *brought, slots)
    else:
        masked = (
            coupling.reshape(total_rows // TILE, TILE, block_arcs // TILE, TILE)
            * incidence.astype(jnp.bfloat16)[:, None, :, None]
        ).reshape(total_rows, block_arcs)
        masked = lax.all_gather(masked, "arc")
        own_mask = jnp.zeros((block_arcs,), jnp.float32).at[fleet_slots].set(1.0)
        per_arc = lax.all_gather(jnp.stack([arc_cost, capacity, own_mask]), "arc", axis=1, tiled=True)
        shares = jnp.broadcast_to(weights.astype(jnp.float32)[:, None], (1, 128))
        per_scen = lax.all_gather(jnp.concatenate([demand, shares], axis=1), "scen", tiled=True)
        outs = pl.pallas_call(
            plain_kernel,
            out_shape=out_shape,
            in_specs=[VMEM] * 7,
            out_specs=out_specs,
            scratch_shapes=state,
            compiler_params=limit(48),
            cost_estimate=cost,
            name="whole",
        )(masked, per_arc[0:1], per_arc[1:2], per_arc[2:3], per_scen[:, :total_rows],
          per_scen[:, total_rows:], slots)
    flows, duals, multipliers, consensus, spread = outs
    return flows, duals, multipliers, consensus.reshape(-1), spread


def solution(mesh):
    in_specs = (
        P(None, "arc"),
        P(None, "arc"),
        P("arc"),
        P("arc"),
        P("scen", None),
        P("scen"),
        P("arc"),
    )
    out_specs = (P("scen", "arc"), P("scen", "arc"), P("scen", "arc"), P("arc"), P())
    return jax.shard_map(body, mesh=mesh, in_specs=in_specs, out_specs=out_specs, check_vma=False)
```

```python
import functools

import jax
import jax.numpy as jnp
from jax import lax
from jax.experimental import pallas as pl
from jax.experimental.pallas import tpu as pltpu
from jax.sharding import PartitionSpec as P

TILE = 128
ITERS = 4
ROUNDS = 2
EXTRA = 16
GROUPS = ((0, 3, 5), (1, 2, 4))

primal_step = 0.9
dual_step = 0.9
penalty = 1.0

VMEM = pl.BlockSpec(memory_space=pltpu.VMEM)
SMEM = pl.BlockSpec(memory_space=pltpu.SMEM)
ANY = pl.BlockSpec(memory_space=pl.ANY)


def pieces(value):
    high = value.astype(jnp.bfloat16)
    rest = value - high.astype(jnp.float32)
    middle = rest.astype(jnp.bfloat16)
    low = (rest - middle.astype(jnp.float32)).astype(jnp.bfloat16)
    return high, middle, low


def one_hot(slots, block_arcs):
    arcs = lax.broadcasted_iota(jnp.int32, (block_arcs, slots.shape[1]), 0)
    return jnp.where(arcs == slots, 1.0, 0.0).astype(jnp.bfloat16)


def fleet_mask(slots, block_arcs):
    ones = jnp.ones((8, slots.shape[1]), jnp.bfloat16)
    hits = lax.dot_general(ones, one_hot(slots, block_arcs), (((1,), (1,)), ((), ())),
                           preferred_element_type=jnp.float32)
    return hits[:1]


def own_row(value, scen):
    rows = lax.broadcasted_iota(jnp.int32, value.shape, 0)
    return jnp.sum(jnp.where(rows == scen, value, 0.0), axis=0, keepdims=True)


def pack_kernel(coupling, incidence, arc_cost, capacity, demand, weights, slots,
                near, across, extra, rows_in, sems):
    total_rows, block_arcs = rows_in.shape
    chip = lax.axis_index("scen") // 2
    chips = total_rows // TILE
    copies = []
    for part in range(chips):
        first = pl.multiple_of(jnp.bitwise_xor(chip, part) * TILE, TILE)
        copies.append(pltpu.make_async_copy(
            coupling.at[pl.ds(first, TILE)], rows_in.at[pl.ds(part * TILE, TILE)], sems.at[part]))
    for copy in copies:
        copy.start()
    share = jnp.broadcast_to(weights[...].astype(jnp.float32), (1, 128))
    share = jnp.concatenate([*pieces(share), jnp.zeros((1, 128), jnp.bfloat16)], axis=1)
    mask = fleet_mask(slots[...], block_arcs)
    touch = []
    for part in range(chips):
        owner = jnp.bitwise_xor(chip, part)
        touch.append(jnp.concatenate(
            [jnp.full((1, TILE), incidence[owner, tile].astype(jnp.float32))
             for tile in range(block_arcs // TILE)], axis=1))
    lines = [*pieces(arc_cost[...]), *pieces(capacity[...]), mask, *pieces(demand[...]), share, *touch]
    lines = [line.astype(jnp.float32) for line in lines]
    lines += [jnp.zeros((1, block_arcs), jnp.float32)] * (EXTRA - len(lines))
    lines = jnp.concatenate(lines, axis=0).astype(jnp.bfloat16)
    extra[...] = lines
    across[TILE:, :] = lines
    for part in range(chips):
        copies[part].wait()
        rows = slice(part * TILE, (part + 1) * TILE)
        near[rows, :] = rows_in[rows, :] * touch[part].astype(jnp.bfloat16)
    across[:TILE, :] = near[(chips - 1) * TILE:, :]


def rounds(masked, turned, blocks, joined, cost, cap, mask, demand, share, fleet_count, spread_out,
           flows, duals, prices, centre, shifted):
    scenarios, total_rows = demand.shape
    block_arcs = cost.shape[1] // blocks
    weight_sum = jnp.sum(share[:, :1])
    for round_index in range(ROUNDS):
        for step_index in range(ITERS):
            first = round_index == 0 and step_index == 0
            load = jnp.zeros((scenarios, total_rows), jnp.float32)
            if not first:
                duals_low = duals[...].astype(jnp.bfloat16)
            for start in range(0, blocks, joined):
                group = range(start, start + joined)
                if not first:
                    weights = jnp.concatenate([masked(block) for block in group], axis=1)
                    pulls = jnp.dot(duals_low, weights, preferred_element_type=jnp.float32)
                bars = []
                for block in group:
                    cols = slice(block * block_arcs, (block + 1) * block_arcs)
                    if first:
                        gradient = jnp.broadcast_to(cost[:, cols], (scenarios, block_arcs))
                        old = jnp.zeros((scenarios, block_arcs), jnp.float32)
                    else:
                        old = flows[:, cols]
                        pull = pulls[:, (block - start) * block_arcs:(block - start + 1) * block_arcs]
                        push = penalty * mask[:, cols] * old
                        if round_index > 0:
                            push = push + shifted[:, cols]
                        gradient = cost[:, cols] + pull + push
                    new = jnp.clip(old - primal_step * gradient, 0.0, cap[:, cols])
                    flows[:, cols] = new
                    bars.append((2.0 * new - old).astype(jnp.bfloat16))
                weights = jnp.concatenate([turned(block) for block in group], axis=0)
                load = load + jnp.dot(jnp.concatenate(bars, axis=1), weights, preferred_element_type=jnp.float32)
            step = dual_step * (load - demand[...])
            duals[...] = jnp.maximum(step if first else duals[...] + step, 0.0)
        squares = jnp.float32(0.0)
        for block in range(blocks):
            cols = slice(block * block_arcs, (block + 1) * block_arcs)
            fleet = flows[:, cols] * mask[:, cols]
            share_col = share[:, :1]
            mean = jnp.sum(share_col * fleet, axis=0, keepdims=True) / weight_sum
            gap = fleet - mean
            squares = squares + jnp.sum(share_col * gap * gap)
            total = penalty * gap if round_index == 0 else prices[:, cols] + penalty * gap
            prices[:, cols] = total
            centre[:, cols] = mean
            shifted[:, cols] = total - penalty * mean
        spread_out[round_index] = jnp.sqrt(squares / (weight_sum * fleet_count) + 1e-06)


def pick_fleet(price, mean, slots):
    picked = [line.astype(jnp.float32) for line in (*pieces(price), *pieces(mean))]
    picked += [jnp.zeros_like(price)] * 2
    picked = jnp.dot(jnp.concatenate(picked, axis=0).astype(jnp.bfloat16),
                     one_hot(slots, price.shape[1]), preferred_element_type=jnp.float32)
    return picked[0:1] + picked[1:2] + picked[2:3], picked[3:4] + picked[4:5] + picked[5:6]


def plain_kernel(masked, cost, cap, mask, demand, share, slots, flows_out, duals_out, mult_out, cons_out,
                 spread_out, flows, duals, prices, centre, shifted):
    blocks, total_rows, block_arcs = masked.shape
    rounds(lambda block: masked[block], lambda block: masked[block].T, blocks, 1, cost, cap, mask, demand, share, slots.shape[1] * blocks,
           spread_out, flows, duals, prices, centre, shifted)
    scen, arc = lax.axis_index("scen"), lax.axis_index("arc")
    own = pl.ds(pl.multiple_of(arc * block_arcs, block_arcs), block_arcs)
    share_rows = total_rows // blocks
    own_rows = pl.ds(pl.multiple_of(arc * share_rows, share_rows), share_rows)
    flows_out[...] = own_row(flows[:, own], scen)
    duals_out[...] = own_row(duals[:, own_rows], scen)
    mult_out[...], cons_out[...] = pick_fleet(own_row(prices[:, own], scen), centre[:, own], slots[...])


def ready_kernel(near, line, side, front, across, near_turned, mine, mine_turned):
    total_rows, block_arcs = near.shape
    chips = total_rows // TILE
    near_turned[...] = near[...].T
    touch = across[TILE:, :].astype(jnp.float32)[11:11 + chips].astype(jnp.bfloat16)
    for part, source in enumerate((line, side, front, across)):
        rows = slice(part * TILE, (part + 1) * TILE)
        wide = source[:TILE, :]
        mine[rows, :] = wide if part == chips - 1 else wide * touch[part:part + 1]
    mine_turned[...] = mine[...].T


def whole_kernel(near, near_turned, mine, mine_turned, *refs):
    lines, others = refs[:6], [None] * 6
    for group, joined in zip(GROUPS, refs[6:]):
        first = 0
        for part in group:
            rows = lines[part].shape[0]
            others[part] = joined.at[pl.ds(first, rows)]
            first += rows
    (slots, flows_out, duals_out, mult_out, cons_out, spread_out,
     blocks_in, turned, cost, cap, mask, demand_in, demand, share, flows, duals, prices, centre, shifted) = refs[6 + len(GROUPS):]
    total_rows, block_arcs = near.shape
    scen, arc = lax.axis_index("scen"), lax.axis_index("arc")
    chip, core = scen // 2, lax.rem(scen, 2)
    chips = total_rows // TILE
    half = TILE // 2
    tails = [lines[0][TILE + half:, :], lines[3][TILE:, :], others[3][TILE:, :], refs[5][...]]
    touch = []
    for block, tail in enumerate(tails):
        cols = slice(block * block_arcs, (block + 1) * block_arcs)
        tail = tail.astype(jnp.float32)
        cost[:, cols] = tail[0:1] + tail[1:2] + tail[2:3]
        cap[:, cols] = tail[3:4] + tail[4:5] + tail[5:6]
        mask[:, cols] = tail[6:7]
        touch.append(tail[11:11 + chips].astype(jnp.bfloat16))
    for row in range(2 * chips):
        part, source = row // 2, others if row % 2 else lines
        tail = source[part][TILE + half:, :] if part < chips - 1 else source[4][half:, :]
        tail = tail.astype(jnp.float32)
        demand_in[row:row + 1, :] = tail[7:8] + tail[8:9] + tail[9:10]
        share[row:row + 1, :] = tail[10:11, :128] + tail[10:11, 128:256] + tail[10:11, 256:384]
    for part in range(chips):
        owner = jnp.bitwise_xor(chip, part)
        rows = slice(part * TILE, (part + 1) * TILE)
        demand[:, rows] = demand_in[:, pl.ds(pl.multiple_of(owner * TILE, TILE), TILE)]
        wide = others[part][:TILE, :]
        blocks_in[0, rows, :] = wide if part == chips - 1 else wide * touch[2][part:part + 1]
        for side, source in enumerate((lines, others)):
            narrow = source[part][TILE:TILE + half, :] if part < chips - 1 else source[4][:half, :]
            place = jnp.where(core == side, 0, half)
            place = pl.ds(pl.multiple_of(part * TILE + place, half), half)
            blocks_in[1, place, :] = narrow * touch[3][part:part + 1]
    for block in range(2):
        turned[block] = blocks_in[block].T

    def masked(block):
        return (near, mine)[block][...] if block < 2 else blocks_in[block - 2]

    def masked_turned(block):
        return (near_turned, mine_turned)[block][...] if block < 2 else turned[block - 2]

    rounds(masked, masked_turned, len(tails), len(tails), cost, cap, mask, demand, share, slots.shape[1] * len(tails),
           spread_out, flows, duals, prices, centre, shifted)
    flows_out[...] = flows[0:1, :block_arcs]
    first = pl.multiple_of(jnp.bitwise_xor(chip, arc) * TILE, TILE)
    duals_out[...] = duals[:, pl.ds(first, TILE)][0:1]
    mult_out[...], cons_out[...] = pick_fleet(prices[0:1, :block_arcs], centre[:, :block_arcs], slots[...])


def swap(value, partner):
    scenarios, blocks = lax.axis_size("scen"), lax.axis_size("arc")
    pairs = []
    for scen in range(scenarios):
        for arc in range(blocks):
            other_scen, other_arc = partner(scen, arc)
            pairs.append((scen * blocks + arc, other_scen * blocks + other_arc))
    return lax.ppermute(value, ("scen", "arc"), pairs)


def bring(coupling, across, extra):
    scen = lax.axis_index("scen")
    half = TILE // 2
    wide = lax.dynamic_slice_in_dim(coupling, lax.shift_right_logical(scen, 1) * TILE, TILE, 0)
    wide = lax.optimization_barrier(wide)
    narrow = lax.dynamic_slice_in_dim(wide, (scen & 1) * half, half, 0)
    wide = swap(wide, lambda scen, arc: (scen, arc ^ (1 + scen % 2)))
    narrow = swap(narrow, lambda scen, arc: (scen, arc ^ 3))
    line = jnp.concatenate([wide, narrow, extra], axis=0)
    line, across = lax.optimization_barrier((line, across))
    side = swap(line, lambda scen, arc: (scen ^ 2, arc))
    front = swap(line, lambda scen, arc: (scen ^ 4, arc))
    across = swap(across, lambda scen, arc: (scen, arc ^ (1 + scen % 2)))
    beyond = swap(jnp.concatenate([narrow, extra], axis=0), lambda scen, arc: (scen ^ 6, arc))
    extra = swap(extra, lambda scen, arc: (scen, arc ^ 3))
    brought = [line, side, front, across, beyond, extra]
    joined = [jnp.concatenate([brought[part] for part in group], axis=0) for group in GROUPS]
    return brought + [swap(parts, lambda scen, arc: (scen ^ 1, arc)) for parts in joined]


def body(coupling, incidence, arc_cost, capacity, demand, weights, fleet_slots):
    total_rows, block_arcs = coupling.shape
    scenarios, blocks = lax.axis_size("scen"), lax.axis_size("arc")
    arcs = blocks * block_arcs
    fleet_block = fleet_slots.shape[0]
    row = lambda value: value.reshape(1, -1)
    slots = row(fleet_slots)
    out_shape = (
        jax.ShapeDtypeStruct((1, block_arcs), jnp.float32),
        jax.ShapeDtypeStruct((1, total_rows // blocks), jnp.float32),
        jax.ShapeDtypeStruct((1, fleet_block), jnp.float32),
        jax.ShapeDtypeStruct((1, fleet_block), jnp.float32),
        jax.ShapeDtypeStruct((ROUNDS,), jnp.float32),
    )
    out_specs = (VMEM, VMEM, VMEM, VMEM, SMEM)
    state = [
        pltpu.VMEM((scenarios, arcs), jnp.float32),
        pltpu.VMEM((scenarios, total_rows), jnp.float32),
        pltpu.VMEM((scenarios, arcs), jnp.float32),
        pltpu.VMEM((1, arcs), jnp.float32),
        pltpu.VMEM((scenarios, arcs), jnp.float32),
    ]
    limit = lambda mib: pltpu.CompilerParams(vmem_limit_bytes=mib * 1024 * 1024)
    cost = pl.CostEstimate(
        flops=4 * ROUNDS * ITERS * scenarios * total_rows * arcs,
        bytes_accessed=2 * total_rows * arcs,
        transcendentals=0,
    )
    fits = (scenarios, blocks) == (8, 4)
    if fits and total_rows == TILE * 4:
        like = lambda rows: jax.ShapeDtypeStruct((rows, block_arcs), jnp.bfloat16)
        near, across, extra = pl.pallas_call(
            pack_kernel,
            out_shape=(like(total_rows), like(TILE + EXTRA), like(EXTRA)),
            in_specs=[ANY, SMEM, VMEM, VMEM, VMEM, VMEM, VMEM],
            out_specs=(VMEM,) * 3,
            scratch_shapes=[
                pltpu.VMEM((total_rows, block_arcs), jnp.bfloat16),
                pltpu.SemaphoreType.DMA((total_rows // TILE,)),
            ],
            compiler_params=limit(8),
            name="pack",
        )(coupling, incidence, row(arc_cost), row(capacity), demand, weights.reshape(1, 1), slots)
        brought = bring(coupling, across, extra)
        square = jax.ShapeDtypeStruct((block_arcs, total_rows), jnp.bfloat16)
        ready = pl.pallas_call(
            ready_kernel,
            out_shape=(square, like(total_rows), square),
            in_specs=[VMEM] * 5,
            out_specs=(VMEM,) * 3,
            compiler_params=limit(8),
            name="ready",
        )(near, *brought[:4])
        outs = pl.pallas_call(
            whole_kernel,
            out_shape=out_shape,
            in_specs=[VMEM] * (len(brought) + 5),
            out_specs=out_specs,
            scratch_shapes=[
                pltpu.VMEM((blocks - 2, total_rows, block_arcs), jnp.bfloat16),
                pltpu.VMEM((blocks - 2, block_arcs, total_rows), jnp.bfloat16),
                pltpu.VMEM((1, arcs), jnp.float32),
                pltpu.VMEM((1, arcs), jnp.float32),
                pltpu.VMEM((1, arcs), jnp.float32),
                pltpu.VMEM((scenarios, total_rows), jnp.float32),
                pltpu.VMEM((scenarios, total_rows), jnp.float32),
                pltpu.VMEM((scenarios, 128), jnp.float32),
                *state,
            ],
            compiler_params=limit(16),
            cost_estimate=cost,
            name="whole",
        )(near, *ready, *brought, slots)
    else:
        masked = (
            coupling.reshape(total_rows // TILE, TILE, block_arcs // TILE, TILE)
            * incidence.astype(jnp.bfloat16)[:, None, :, None]
        ).reshape(total_rows, block_arcs)
        masked = lax.all_gather(masked, "arc")
        own_mask = jnp.zeros((block_arcs,), jnp.float32).at[fleet_slots].set(1.0)
        per_arc = lax.all_gather(jnp.stack([arc_cost, capacity, own_mask]), "arc", axis=1, tiled=True)
        shares = jnp.broadcast_to(weights.astype(jnp.float32)[:, None], (1, 128))
        per_scen = lax.all_gather(jnp.concatenate([demand, shares], axis=1), "scen", tiled=True)
        outs = pl.pallas_call(
            plain_kernel,
            out_shape=out_shape,
            in_specs=[VMEM] * 7,
            out_specs=out_specs,
            scratch_shapes=state,
            compiler_params=limit(48),
            cost_estimate=cost,
            name="whole",
        )(masked, per_arc[0:1], per_arc[1:2], per_arc[2:3], per_scen[:, :total_rows],
          per_scen[:, total_rows:], slots)
    flows, duals, multipliers, consensus, spread = outs
    return flows, duals, multipliers, consensus.reshape(-1), spread


def solution(mesh):
    in_specs = (
        P(None, "arc"),
        P(None, "arc"),
        P("arc"),
        P("arc"),
        P("scen", None),
        P("scen"),
        P("arc"),
    )
    out_specs = (P("scen", "arc"), P("scen", "arc"), P("scen", "arc"), P("arc"), P())
    return jax.shard_map(body, mesh=mesh, in_specs=in_specs, out_specs=out_specs, check_vma=False)
```

```python
import functools

import jax
import jax.numpy as jnp
from jax import lax
from jax.experimental import pallas as pl
from jax.experimental.pallas import tpu as pltpu
from jax.sharding import PartitionSpec as P

TILE = 128
ITERS = 4
ROUNDS = 2
EXTRA = 16
GROUPS = ((0, 3, 5), (1, 2, 4))

primal_step = 0.9
dual_step = 0.9
penalty = 1.0

VMEM = pl.BlockSpec(memory_space=pltpu.VMEM)
SMEM = pl.BlockSpec(memory_space=pltpu.SMEM)
ANY = pl.BlockSpec(memory_space=pl.ANY)


def pieces(value):
    high = value.astype(jnp.bfloat16)
    rest = value - high.astype(jnp.float32)
    middle = rest.astype(jnp.bfloat16)
    low = (rest - middle.astype(jnp.float32)).astype(jnp.bfloat16)
    return high, middle, low


def one_hot(slots, block_arcs):
    arcs = lax.broadcasted_iota(jnp.int32, (block_arcs, slots.shape[1]), 0)
    return jnp.where(arcs == slots, 1.0, 0.0).astype(jnp.bfloat16)


def fleet_mask(slots, block_arcs):
    ones = jnp.ones((8, slots.shape[1]), jnp.bfloat16)
    hits = lax.dot_general(ones, one_hot(slots, block_arcs), (((1,), (1,)), ((), ())),
                           preferred_element_type=jnp.float32)
    return hits[:1]


def own_row(value, scen):
    rows = lax.broadcasted_iota(jnp.int32, value.shape, 0)
    return jnp.sum(jnp.where(rows == scen, value, 0.0), axis=0, keepdims=True)


def pack_kernel(coupling, incidence, arc_cost, capacity, demand, weights, slots,
                near, across, extra, rows_in, sems):
    total_rows, block_arcs = rows_in.shape
    chip = lax.axis_index("scen") // 2
    chips = total_rows // TILE
    copies = []
    for part in range(chips):
        first = pl.multiple_of(jnp.bitwise_xor(chip, part) * TILE, TILE)
        copies.append(pltpu.make_async_copy(
            coupling.at[pl.ds(first, TILE)], rows_in.at[pl.ds(part * TILE, TILE)], sems.at[part]))
    for copy in copies:
        copy.start()
    share = jnp.broadcast_to(weights[...].astype(jnp.float32), (1, 128))
    share = jnp.concatenate([*pieces(share), jnp.zeros((1, 128), jnp.bfloat16)], axis=1)
    mask = fleet_mask(slots[...], block_arcs)
    touch = []
    for part in range(chips):
        owner = jnp.bitwise_xor(chip, part)
        touch.append(jnp.concatenate(
            [jnp.full((1, TILE), incidence[owner, tile].astype(jnp.float32))
             for tile in range(block_arcs // TILE)], axis=1))
    lines = [*pieces(arc_cost[...]), *pieces(capacity[...]), mask, *pieces(demand[...]), share, *touch]
    lines = [line.astype(jnp.float32) for line in lines]
    lines += [jnp.zeros((1, block_arcs), jnp.float32)] * (EXTRA - len(lines))
    lines = jnp.concatenate(lines, axis=0).astype(jnp.bfloat16)
    extra[...] = lines
    across[TILE:, :] = lines
    for part in range(chips):
        copies[part].wait()
        rows = slice(part * TILE, (part + 1) * TILE)
        near[rows, :] = rows_in[rows, :] * touch[part].astype(jnp.bfloat16)
    across[:TILE, :] = near[(chips - 1) * TILE:, :]


def rounds(masked, turned, blocks, joined, cost, cap, mask, demand, share, fleet_count, spread_out,
           flows, duals, prices, centre, shifted):
    scenarios, total_rows = demand.shape
    block_arcs = cost.shape[1] // blocks
    weight_sum = jnp.sum(share[:, :1], axis=0, keepdims=True)
    spreads = []
    for round_index in range(ROUNDS):
        for step_index in range(ITERS):
            first = round_index == 0 and step_index == 0
            load = jnp.zeros((scenarios, total_rows), jnp.float32)
            if not first:
                duals_low = duals[...].astype(jnp.bfloat16)
            for start in range(0, blocks, joined):
                group = range(start, start + joined)
                if not first:
                    weights = jnp.concatenate([masked(block) for block in group], axis=1)
                    pulls = jnp.dot(duals_low, weights, preferred_element_type=jnp.float32)
                bars = []
                for block in group:
                    cols = slice(block * block_arcs, (block + 1) * block_arcs)
                    if first:
                        gradient = jnp.broadcast_to(cost[:, cols], (scenarios, block_arcs))
                        old = jnp.zeros((scenarios, block_arcs), jnp.float32)
                    else:
                        old = flows[:, cols]
                        pull = pulls[:, (block - start) * block_arcs:(block - start + 1) * block_arcs]
                        push = penalty * mask[:, cols] * old
                        if round_index > 0:
                            push = push + shifted[:, cols]
                        gradient = cost[:, cols] + pull + push
                    new = jnp.clip(old - primal_step * gradient, 0.0, cap[:, cols])
                    flows[:, cols] = new
                    bars.append((2.0 * new - old).astype(jnp.bfloat16))
                weights = jnp.concatenate([turned(block) for block in group], axis=0)
                load = load + jnp.dot(jnp.concatenate(bars, axis=1), weights, preferred_element_type=jnp.float32)
            step = dual_step * (load - demand[...])
            duals[...] = jnp.maximum(step if first else duals[...] + step, 0.0)
        squares = jnp.zeros((1, block_arcs), jnp.float32)
        for block in range(blocks):
            cols = slice(block * block_arcs, (block + 1) * block_arcs)
            fleet = flows[:, cols] * mask[:, cols]
            share_col = share[:, :1]
            mean = jnp.sum(share_col * fleet, axis=0, keepdims=True) / weight_sum
            gap = fleet - mean
            squares = squares + jnp.sum(share_col * gap * gap, axis=0, keepdims=True)
            total = penalty * gap if round_index == 0 else prices[:, cols] + penalty * gap
            prices[:, cols] = total
            centre[:, cols] = mean
            shifted[:, cols] = total - penalty * mean
        squares = jnp.sum(squares, axis=1, keepdims=True)
        spreads.append(jnp.sqrt(squares / (weight_sum * fleet_count) + 1e-06))
    lanes = lax.broadcasted_iota(jnp.int32, spread_out.shape, 1)
    spread = jnp.broadcast_to(spreads[0], spread_out.shape)
    for round_index in range(1, ROUNDS):
        spread = jnp.where(lanes == round_index, spreads[round_index], spread)
    spread_out[...] = spread


def pick_fleet(price, mean, slots):
    picked = [line.astype(jnp.float32) for line in (*pieces(price), *pieces(mean))]
    picked += [jnp.zeros_like(price)] * 2
    picked = jnp.dot(jnp.concatenate(picked, axis=0).astype(jnp.bfloat16),
                     one_hot(slots, price.shape[1]), preferred_element_type=jnp.float32)
    return picked[0:1] + picked[1:2] + picked[2:3], picked[3:4] + picked[4:5] + picked[5:6]


def plain_kernel(masked, cost, cap, mask, demand, share, slots, flows_out, duals_out, mult_out, cons_out,
                 spread_out, flows, duals, prices, centre, shifted):
    blocks, total_rows, block_arcs = masked.shape
    rounds(lambda block: masked[block], lambda block: masked[block].T, blocks, 1, cost, cap, mask, demand, share, slots.shape[1] * blocks,
           spread_out, flows, duals, prices, centre, shifted)
    scen, arc = lax.axis_index("scen"), lax.axis_index("arc")
    own = pl.ds(pl.multiple_of(arc * block_arcs, block_arcs), block_arcs)
    share_rows = total_rows // blocks
    own_rows = pl.ds(pl.multiple_of(arc * share_rows, share_rows), share_rows)
    flows_out[...] = own_row(flows[:, own], scen)
    duals_out[...] = own_row(duals[:, own_rows], scen)
    mult_out[...], cons_out[...] = pick_fleet(own_row(prices[:, own], scen), centre[:, own], slots[...])


def ready_kernel(near, line, side, front, across, near_turned, mine, mine_turned):
    total_rows, block_arcs = near.shape
    chips = total_rows // TILE
    near_turned[...] = near[...].T
    touch = across[TILE:, :].astype(jnp.float32)[11:11 + chips].astype(jnp.bfloat16)
    for part, source in enumerate((line, side, front, across)):
        rows = slice(part * TILE, (part + 1) * TILE)
        wide = source[:TILE, :]
        mine[rows, :] = wide if part == chips - 1 else wide * touch[part:part + 1]
    mine_turned[...] = mine[...].T


def whole_kernel(near, near_turned, mine, mine_turned, *refs):
    lines, others = refs[:6], [None] * 6
    for group, joined in zip(GROUPS, refs[6:]):
        first = 0
        for part in group:
            rows = lines[part].shape[0]
            others[part] = joined.at[pl.ds(first, rows)]
            first += rows
    (slots, flows_out, duals_out, mult_out, cons_out, spread_out,
     blocks_in, turned, cost, cap, mask, demand_in, demand, share, flows, duals, prices, centre, shifted) = refs[6 + len(GROUPS):]
    total_rows, block_arcs = near.shape
    scen, arc = lax.axis_index("scen"), lax.axis_index("arc")
    chip, core = scen // 2, lax.rem(scen, 2)
    chips = total_rows // TILE
    half = TILE // 2
    tails = [lines[0][TILE + half:, :], lines[3][TILE:, :], others[3][TILE:, :], refs[5][...]]
    touch = []
    for block, tail in enumerate(tails):
        cols = slice(block * block_arcs, (block + 1) * block_arcs)
        tail = tail.astype(jnp.float32)
        cost[:, cols] = tail[0:1] + tail[1:2] + tail[2:3]
        cap[:, cols] = tail[3:4] + tail[4:5] + tail[5:6]
        mask[:, cols] = tail[6:7]
        touch.append(tail[11:11 + chips].astype(jnp.bfloat16))
    for row in range(2 * chips):
        part, source = row // 2, others if row % 2 else lines
        tail = source[part][TILE + half:, :] if part < chips - 1 else source[4][half:, :]
        tail = tail.astype(jnp.float32)
        demand_in[row:row + 1, :] = tail[7:8] + tail[8:9] + tail[9:10]
        share[row:row + 1, :] = tail[10:11, :128] + tail[10:11, 128:256] + tail[10:11, 256:384]
    for part in range(chips):
        owner = jnp.bitwise_xor(chip, part)
        rows = slice(part * TILE, (part + 1) * TILE)
        demand[:, rows] = demand_in[:, pl.ds(pl.multiple_of(owner * TILE, TILE), TILE)]
        wide = others[part][:TILE, :]
        blocks_in[0, rows, :] = wide if part == chips - 1 else wide * touch[2][part:part + 1]
        for side, source in enumerate((lines, others)):
            narrow = source[part][TILE:TILE + half, :] if part < chips - 1 else source[4][:half, :]
            place = jnp.where(core == side, 0, half)
            place = pl.ds(pl.multiple_of(part * TILE + place, half), half)
            blocks_in[1, place, :] = narrow * touch[3][part:part + 1]
    for block in range(2):
        turned[block] = blocks_in[block].T

    def masked(block):
        return (near, mine)[block][...] if block < 2 else blocks_in[block - 2]

    def masked_turned(block):
        return (near_turned, mine_turned)[block][...] if block < 2 else turned[block - 2]

    rounds(masked, masked_turned, len(tails), len(tails), cost, cap, mask, demand, share, slots.shape[1] * len(tails),
           spread_out, flows, duals, prices, centre, shifted)
    flows_out[...] = flows[0:1, :block_arcs]
    first = pl.multiple_of(jnp.bitwise_xor(chip, arc) * TILE, TILE)
    duals_out[...] = duals[:, pl.ds(first, TILE)][0:1]
    mult_out[...], cons_out[...] = pick_fleet(prices[0:1, :block_arcs], centre[:, :block_arcs], slots[...])


def swap(value, partner):
    scenarios, blocks = lax.axis_size("scen"), lax.axis_size("arc")
    pairs = []
    for scen in range(scenarios):
        for arc in range(blocks):
            other_scen, other_arc = partner(scen, arc)
            pairs.append((scen * blocks + arc, other_scen * blocks + other_arc))
    return lax.ppermute(value, ("scen", "arc"), pairs)


def bring(coupling, across, extra):
    scen = lax.axis_index("scen")
    half = TILE // 2
    wide = lax.dynamic_slice_in_dim(coupling, lax.shift_right_logical(scen, 1) * TILE, TILE, 0)
    wide = lax.optimization_barrier(wide)
    narrow = lax.dynamic_slice_in_dim(wide, (scen & 1) * half, half, 0)
    wide = swap(wide, lambda scen, arc: (scen, arc ^ (1 + scen % 2)))
    narrow = swap(narrow, lambda scen, arc: (scen, arc ^ 3))
    line = jnp.concatenate([wide, narrow, extra], axis=0)
    line, across = lax.optimization_barrier((line, across))
    side = swap(line, lambda scen, arc: (scen ^ 2, arc))
    front = swap(line, lambda scen, arc: (scen ^ 4, arc))
    across = swap(across, lambda scen, arc: (scen, arc ^ (1 + scen % 2)))
    beyond = swap(jnp.concatenate([narrow, extra], axis=0), lambda scen, arc: (scen ^ 6, arc))
    extra = swap(extra, lambda scen, arc: (scen, arc ^ 3))
    brought = [line, side, front, across, beyond, extra]
    joined = [jnp.concatenate([brought[part] for part in group], axis=0) for group in GROUPS]
    return brought + [swap(parts, lambda scen, arc: (scen ^ 1, arc)) for parts in joined]


def body(coupling, incidence, arc_cost, capacity, demand, weights, fleet_slots):
    total_rows, block_arcs = coupling.shape
    scenarios, blocks = lax.axis_size("scen"), lax.axis_size("arc")
    arcs = blocks * block_arcs
    fleet_block = fleet_slots.shape[0]
    row = lambda value: value.reshape(1, -1)
    slots = row(fleet_slots)
    out_shape = (
        jax.ShapeDtypeStruct((1, block_arcs), jnp.float32),
        jax.ShapeDtypeStruct((1, total_rows // blocks), jnp.float32),
        jax.ShapeDtypeStruct((1, fleet_block), jnp.float32),
        jax.ShapeDtypeStruct((1, fleet_block), jnp.float32),
        jax.ShapeDtypeStruct((1, ROUNDS), jnp.float32),
    )
    out_specs = (VMEM,) * 5
    state = [
        pltpu.VMEM((scenarios, arcs), jnp.float32),
        pltpu.VMEM((scenarios, total_rows), jnp.float32),
        pltpu.VMEM((scenarios, arcs), jnp.float32),
        pltpu.VMEM((1, arcs), jnp.float32),
        pltpu.VMEM((scenarios, arcs), jnp.float32),
    ]
    limit = lambda mib: pltpu.CompilerParams(vmem_limit_bytes=mib * 1024 * 1024)
    cost = pl.CostEstimate(
        flops=4 * ROUNDS * ITERS * scenarios * total_rows * arcs,
        bytes_accessed=2 * total_rows * arcs,
        transcendentals=0,
    )
    fits = (scenarios, blocks) == (8, 4)
    if fits and total_rows == TILE * 4:
        like = lambda rows: jax.ShapeDtypeStruct((rows, block_arcs), jnp.bfloat16)
        near, across, extra = pl.pallas_call(
            pack_kernel,
            out_shape=(like(total_rows), like(TILE + EXTRA), like(EXTRA)),
            in_specs=[ANY, SMEM, VMEM, VMEM, VMEM, VMEM, VMEM],
            out_specs=(VMEM,) * 3,
            scratch_shapes=[
                pltpu.VMEM((total_rows, block_arcs), jnp.bfloat16),
                pltpu.SemaphoreType.DMA((total_rows // TILE,)),
            ],
            compiler_params=limit(8),
            name="pack",
        )(coupling, incidence, row(arc_cost), row(capacity), demand, weights.reshape(1, 1), slots)
        brought = bring(coupling, across, extra)
        square = jax.ShapeDtypeStruct((block_arcs, total_rows), jnp.bfloat16)
        ready = pl.pallas_call(
            ready_kernel,
            out_shape=(square, like(total_rows), square),
            in_specs=[VMEM] * 5,
            out_specs=(VMEM,) * 3,
            compiler_params=limit(8),
            name="ready",
        )(near, *brought[:4])
        outs = pl.pallas_call(
            whole_kernel,
            out_shape=out_shape,
            in_specs=[VMEM] * (len(brought) + 5),
            out_specs=out_specs,
            scratch_shapes=[
                pltpu.VMEM((blocks - 2, total_rows, block_arcs), jnp.bfloat16),
                pltpu.VMEM((blocks - 2, block_arcs, total_rows), jnp.bfloat16),
                pltpu.VMEM((1, arcs), jnp.float32),
                pltpu.VMEM((1, arcs), jnp.float32),
                pltpu.VMEM((1, arcs), jnp.float32),
                pltpu.VMEM((scenarios, total_rows), jnp.float32),
                pltpu.VMEM((scenarios, total_rows), jnp.float32),
                pltpu.VMEM((scenarios, 128), jnp.float32),
                *state,
            ],
            compiler_params=limit(16),
            cost_estimate=cost,
            name="whole",
        )(near, *ready, *brought, slots)
    else:
        masked = (
            coupling.reshape(total_rows // TILE, TILE, block_arcs // TILE, TILE)
            * incidence.astype(jnp.bfloat16)[:, None, :, None]
        ).reshape(total_rows, block_arcs)
        masked = lax.all_gather(masked, "arc")
        own_mask = jnp.zeros((block_arcs,), jnp.float32).at[fleet_slots].set(1.0)
        per_arc = lax.all_gather(jnp.stack([arc_cost, capacity, own_mask]), "arc", axis=1, tiled=True)
        shares = jnp.broadcast_to(weights.astype(jnp.float32)[:, None], (1, 128))
        per_scen = lax.all_gather(jnp.concatenate([demand, shares], axis=1), "scen", tiled=True)
        outs = pl.pallas_call(
            plain_kernel,
            out_shape=out_shape,
            in_specs=[VMEM] * 7,
            out_specs=out_specs,
            scratch_shapes=state,
            compiler_params=limit(48),
            cost_estimate=cost,
            name="whole",
        )(masked, per_arc[0:1], per_arc[1:2], per_arc[2:3], per_scen[:, :total_rows],
          per_scen[:, total_rows:], slots)
    flows, duals, multipliers, consensus, spread = outs
    return flows, duals, multipliers, consensus.reshape(-1), spread.reshape(-1)


def solution(mesh):
    in_specs = (
        P(None, "arc"),
        P(None, "arc"),
        P("arc"),
        P("arc"),
        P("scen", None),
        P("scen"),
        P("arc"),
    )
    out_specs = (P("scen", "arc"), P("scen", "arc"), P("scen", "arc"), P("arc"), P())
    return jax.shard_map(body, mesh=mesh, in_specs=in_specs, out_specs=out_specs, check_vma=False)
```

```python
import functools

import jax
import jax.numpy as jnp
from jax import lax
from jax.experimental import pallas as pl
from jax.experimental.pallas import tpu as pltpu
from jax.sharding import PartitionSpec as P

TILE = 128
ITERS = 4
ROUNDS = 2
EXTRA = 16
GROUPS = ((0, 3, 5), (1, 2, 4))

primal_step = 0.9
dual_step = 0.9
penalty = 1.0

VMEM = pl.BlockSpec(memory_space=pltpu.VMEM)
SMEM = pl.BlockSpec(memory_space=pltpu.SMEM)
ANY = pl.BlockSpec(memory_space=pl.ANY)


def pieces(value):
    high = value.astype(jnp.bfloat16)
    rest = value - high.astype(jnp.float32)
    middle = rest.astype(jnp.bfloat16)
    low = (rest - middle.astype(jnp.float32)).astype(jnp.bfloat16)
    return high, middle, low


def one_hot(slots, block_arcs):
    arcs = lax.broadcasted_iota(jnp.int32, (block_arcs, slots.shape[1]), 0)
    return jnp.where(arcs == slots, 1.0, 0.0).astype(jnp.bfloat16)


def fleet_mask(slots, block_arcs):
    ones = jnp.ones((8, slots.shape[1]), jnp.bfloat16)
    hits = lax.dot_general(ones, one_hot(slots, block_arcs), (((1,), (1,)), ((), ())),
                           preferred_element_type=jnp.float32)
    return hits[:1]


def own_row(value, scen):
    rows = lax.broadcasted_iota(jnp.int32, value.shape, 0)
    return jnp.sum(jnp.where(rows == scen, value, 0.0), axis=0, keepdims=True)


def pack_kernel(coupling, incidence, arc_cost, capacity, demand, weights, slots,
                near, across, extra, rows_in, sems):
    total_rows, block_arcs = rows_in.shape
    chip = lax.axis_index("scen") // 2
    chips = total_rows // TILE
    copies = []
    for part in range(chips):
        first = pl.multiple_of(jnp.bitwise_xor(chip, part) * TILE, TILE)
        copies.append(pltpu.make_async_copy(
            coupling.at[pl.ds(first, TILE)], rows_in.at[pl.ds(part * TILE, TILE)], sems.at[part]))
    for copy in copies:
        copy.start()
    share = jnp.broadcast_to(weights[...].astype(jnp.float32), (1, 128))
    share = jnp.concatenate([*pieces(share), jnp.zeros((1, 128), jnp.bfloat16)], axis=1)
    mask = fleet_mask(slots[...], block_arcs)
    touch = []
    for part in range(chips):
        owner = jnp.bitwise_xor(chip, part)
        touch.append(jnp.concatenate(
            [jnp.full((1, TILE), incidence[owner, tile].astype(jnp.float32))
             for tile in range(block_arcs // TILE)], axis=1))
    lines = [*pieces(arc_cost[...]), *pieces(capacity[...]), mask, *pieces(demand[...]), share, *touch]
    lines = [line.astype(jnp.float32) for line in lines]
    lines += [jnp.zeros((1, block_arcs), jnp.float32)] * (EXTRA - len(lines))
    lines = jnp.concatenate(lines, axis=0).astype(jnp.bfloat16)
    extra[...] = lines
    across[TILE:, :] = lines
    for part in range(chips):
        copies[part].wait()
        rows = slice(part * TILE, (part + 1) * TILE)
        near[rows, :] = rows_in[rows, :] * touch[part].astype(jnp.bfloat16)
    across[:TILE, :] = near[(chips - 1) * TILE:, :]


def rounds(masked, turned, blocks, joined, cost, cap, mask, demand, share, fleet_count, spread_out,
           flows, duals, prices, centre, shifted):
    scenarios, total_rows = demand.shape
    block_arcs = cost.shape[1] // blocks
    weight_sum = jnp.sum(share[:, :1], axis=0, keepdims=True)
    spreads = []
    held = {}

    def load_state(name, ref, cols):
        return held[name, cols.start] if joined > 1 else ref[:, cols]

    def store_state(name, ref, cols, value):
        if joined > 1:
            held[name, cols.start] = value
        else:
            ref[:, cols] = value

    rows = slice(0, total_rows)
    for round_index in range(ROUNDS):
        for step_index in range(ITERS):
            first = round_index == 0 and step_index == 0
            load = jnp.zeros((scenarios, total_rows), jnp.float32)
            if not first:
                duals_low = load_state("duals", duals, rows).astype(jnp.bfloat16)
            for start in range(0, blocks, joined):
                group = range(start, start + joined)
                if not first:
                    weights = jnp.concatenate([masked(block) for block in group], axis=1)
                    pulls = jnp.dot(duals_low, weights, preferred_element_type=jnp.float32)
                bars = []
                for block in group:
                    cols = slice(block * block_arcs, (block + 1) * block_arcs)
                    if first:
                        gradient = jnp.broadcast_to(cost[:, cols], (scenarios, block_arcs))
                        old = jnp.zeros((scenarios, block_arcs), jnp.float32)
                    else:
                        old = load_state("flows", flows, cols)
                        pull = pulls[:, (block - start) * block_arcs:(block - start + 1) * block_arcs]
                        push = penalty * mask[:, cols] * old
                        if round_index > 0:
                            push = push + load_state("shifted", shifted, cols)
                        gradient = cost[:, cols] + pull + push
                    new = jnp.clip(old - primal_step * gradient, 0.0, cap[:, cols])
                    store_state("flows", flows, cols, new)
                    bars.append((2.0 * new - old).astype(jnp.bfloat16))
                weights = jnp.concatenate([turned(block) for block in group], axis=0)
                load = load + jnp.dot(jnp.concatenate(bars, axis=1), weights, preferred_element_type=jnp.float32)
            step = dual_step * (load - demand[...])
            if not first:
                step = load_state("duals", duals, rows) + step
            store_state("duals", duals, rows, jnp.maximum(step, 0.0))
        squares = jnp.zeros((1, block_arcs), jnp.float32)
        for block in range(blocks):
            cols = slice(block * block_arcs, (block + 1) * block_arcs)
            fleet = load_state("flows", flows, cols) * mask[:, cols]
            share_col = share[:, :1]
            mean = jnp.sum(share_col * fleet, axis=0, keepdims=True) / weight_sum
            gap = fleet - mean
            squares = squares + jnp.sum(share_col * gap * gap, axis=0, keepdims=True)
            total = penalty * gap
            if round_index > 0:
                total = load_state("prices", prices, cols) + total
            store_state("prices", prices, cols, total)
            centre[:, cols] = mean
            store_state("shifted", shifted, cols, total - penalty * mean)
        squares = jnp.sum(squares, axis=1, keepdims=True)
        spreads.append(jnp.sqrt(squares / (weight_sum * fleet_count) + 1e-06))
    refs = {"flows": flows, "duals": duals, "prices": prices, "shifted": shifted}
    for (name, start), value in held.items():
        refs[name][:, start:start + value.shape[1]] = value
    lanes = lax.broadcasted_iota(jnp.int32, spread_out.shape, 1)
    spread = jnp.broadcast_to(spreads[0], spread_out.shape)
    for round_index in range(1, ROUNDS):
        spread = jnp.where(lanes == round_index, spreads[round_index], spread)
    spread_out[...] = spread


def pick_fleet(price, mean, slots):
    picked = [line.astype(jnp.float32) for line in (*pieces(price), *pieces(mean))]
    picked += [jnp.zeros_like(price)] * 2
    picked = jnp.dot(jnp.concatenate(picked, axis=0).astype(jnp.bfloat16),
                     one_hot(slots, price.shape[1]), preferred_element_type=jnp.float32)
    return picked[0:1] + picked[1:2] + picked[2:3], picked[3:4] + picked[4:5] + picked[5:6]


def plain_kernel(masked, cost, cap, mask, demand, share, slots, flows_out, duals_out, mult_out, cons_out,
                 spread_out, flows, duals, prices, centre, shifted):
    blocks, total_rows, block_arcs = masked.shape
    rounds(lambda block: masked[block], lambda block: masked[block].T, blocks, 1, cost, cap, mask, demand, share, slots.shape[1] * blocks,
           spread_out, flows, duals, prices, centre, shifted)
    scen, arc = lax.axis_index("scen"), lax.axis_index("arc")
    own = pl.ds(pl.multiple_of(arc * block_arcs, block_arcs), block_arcs)
    share_rows = total_rows // blocks
    own_rows = pl.ds(pl.multiple_of(arc * share_rows, share_rows), share_rows)
    flows_out[...] = own_row(flows[:, own], scen)
    duals_out[...] = own_row(duals[:, own_rows], scen)
    mult_out[...], cons_out[...] = pick_fleet(own_row(prices[:, own], scen), centre[:, own], slots[...])


def ready_kernel(near, line, side, front, across, near_turned, mine, mine_turned):
    total_rows, block_arcs = near.shape
    chips = total_rows // TILE
    near_turned[...] = near[...].T
    touch = across[TILE:, :].astype(jnp.float32)[11:11 + chips].astype(jnp.bfloat16)
    for part, source in enumerate((line, side, front, across)):
        rows = slice(part * TILE, (part + 1) * TILE)
        wide = source[:TILE, :]
        mine[rows, :] = wide if part == chips - 1 else wide * touch[part:part + 1]
    mine_turned[...] = mine[...].T


def whole_kernel(near, near_turned, mine, mine_turned, *refs):
    lines, others = refs[:6], [None] * 6
    for group, joined in zip(GROUPS, refs[6:]):
        first = 0
        for part in group:
            rows = lines[part].shape[0]
            others[part] = joined.at[pl.ds(first, rows)]
            first += rows
    (slots, flows_out, duals_out, mult_out, cons_out, spread_out,
     blocks_in, turned, cost, cap, mask, demand_in, demand, share, flows, duals, prices, centre, shifted) = refs[6 + len(GROUPS):]
    total_rows, block_arcs = near.shape
    scen, arc = lax.axis_index("scen"), lax.axis_index("arc")
    chip, core = scen // 2, lax.rem(scen, 2)
    chips = total_rows // TILE
    half = TILE // 2
    tails = [lines[0][TILE + half:, :], lines[3][TILE:, :], others[3][TILE:, :], refs[5][...]]
    touch = []
    for block, tail in enumerate(tails):
        cols = slice(block * block_arcs, (block + 1) * block_arcs)
        tail = tail.astype(jnp.float32)
        cost[:, cols] = tail[0:1] + tail[1:2] + tail[2:3]
        cap[:, cols] = tail[3:4] + tail[4:5] + tail[5:6]
        mask[:, cols] = tail[6:7]
        touch.append(tail[11:11 + chips].astype(jnp.bfloat16))
    for row in range(2 * chips):
        part, source = row // 2, others if row % 2 else lines
        tail = source[part][TILE + half:, :] if part < chips - 1 else source[4][half:, :]
        tail = tail.astype(jnp.float32)
        demand_in[row:row + 1, :] = tail[7:8] + tail[8:9] + tail[9:10]
        share[row:row + 1, :] = tail[10:11, :128] + tail[10:11, 128:256] + tail[10:11, 256:384]
    for part in range(chips):
        owner = jnp.bitwise_xor(chip, part)
        rows = slice(part * TILE, (part + 1) * TILE)
        demand[:, rows] = demand_in[:, pl.ds(pl.multiple_of(owner * TILE, TILE), TILE)]
        wide = others[part][:TILE, :]
        blocks_in[0, rows, :] = wide if part == chips - 1 else wide * touch[2][part:part + 1]
        for side, source in enumerate((lines, others)):
            narrow = source[part][TILE:TILE + half, :] if part < chips - 1 else source[4][:half, :]
            place = jnp.where(core == side, 0, half)
            place = pl.ds(pl.multiple_of(part * TILE + place, half), half)
            blocks_in[1, place, :] = narrow * touch[3][part:part + 1]
    for block in range(2):
        turned[block] = blocks_in[block].T

    def masked(block):
        return (near, mine)[block][...] if block < 2 else blocks_in[block - 2]

    def masked_turned(block):
        return (near_turned, mine_turned)[block][...] if block < 2 else turned[block - 2]

    rounds(masked, masked_turned, len(tails), len(tails), cost, cap, mask, demand, share, slots.shape[1] * len(tails),
           spread_out, flows, duals, prices, centre, shifted)
    flows_out[...] = flows[0:1, :block_arcs]
    first = pl.multiple_of(jnp.bitwise_xor(chip, arc) * TILE, TILE)
    duals_out[...] = duals[:, pl.ds(first, TILE)][0:1]
    mult_out[...], cons_out[...] = pick_fleet(prices[0:1, :block_arcs], centre[:, :block_arcs], slots[...])


def swap(value, partner):
    scenarios, blocks = lax.axis_size("scen"), lax.axis_size("arc")
    pairs = []
    for scen in range(scenarios):
        for arc in range(blocks):
            other_scen, other_arc = partner(scen, arc)
            pairs.append((scen * blocks + arc, other_scen * blocks + other_arc))
    return lax.ppermute(value, ("scen", "arc"), pairs)


def bring(coupling, across, extra):
    scen = lax.axis_index("scen")
    half = TILE // 2
    wide = lax.dynamic_slice_in_dim(coupling, lax.shift_right_logical(scen, 1) * TILE, TILE, 0)
    wide = lax.optimization_barrier(wide)
    narrow = lax.dynamic_slice_in_dim(wide, (scen & 1) * half, half, 0)
    wide = swap(wide, lambda scen, arc: (scen, arc ^ (1 + scen % 2)))
    narrow = swap(narrow, lambda scen, arc: (scen, arc ^ 3))
    line = jnp.concatenate([wide, narrow, extra], axis=0)
    line, across = lax.optimization_barrier((line, across))
    side = swap(line, lambda scen, arc: (scen ^ 2, arc))
    front = swap(line, lambda scen, arc: (scen ^ 4, arc))
    across = swap(across, lambda scen, arc: (scen, arc ^ (1 + scen % 2)))
    beyond = swap(jnp.concatenate([narrow, extra], axis=0), lambda scen, arc: (scen ^ 6, arc))
    extra = swap(extra, lambda scen, arc: (scen, arc ^ 3))
    brought = [line, side, front, across, beyond, extra]
    joined = [jnp.concatenate([brought[part] for part in group], axis=0) for group in GROUPS]
    return brought + [swap(parts, lambda scen, arc: (scen ^ 1, arc)) for parts in joined]


def body(coupling, incidence, arc_cost, capacity, demand, weights, fleet_slots):
    total_rows, block_arcs = coupling.shape
    scenarios, blocks = lax.axis_size("scen"), lax.axis_size("arc")
    arcs = blocks * block_arcs
    fleet_block = fleet_slots.shape[0]
    row = lambda value: value.reshape(1, -1)
    slots = row(fleet_slots)
    out_shape = (
        jax.ShapeDtypeStruct((1, block_arcs), jnp.float32),
        jax.ShapeDtypeStruct((1, total_rows // blocks), jnp.float32),
        jax.ShapeDtypeStruct((1, fleet_block), jnp.float32),
        jax.ShapeDtypeStruct((1, fleet_block), jnp.float32),
        jax.ShapeDtypeStruct((1, ROUNDS), jnp.float32),
    )
    out_specs = (VMEM,) * 5
    state = [
        pltpu.VMEM((scenarios, arcs), jnp.float32),
        pltpu.VMEM((scenarios, total_rows), jnp.float32),
        pltpu.VMEM((scenarios, arcs), jnp.float32),
        pltpu.VMEM((1, arcs), jnp.float32),
        pltpu.VMEM((scenarios, arcs), jnp.float32),
    ]
    limit = lambda mib: pltpu.CompilerParams(vmem_limit_bytes=mib * 1024 * 1024)
    cost = pl.CostEstimate(
        flops=4 * ROUNDS * ITERS * scenarios * total_rows * arcs,
        bytes_accessed=2 * total_rows * arcs,
        transcendentals=0,
    )
    fits = (scenarios, blocks) == (8, 4)
    if fits and total_rows == TILE * 4:
        like = lambda rows: jax.ShapeDtypeStruct((rows, block_arcs), jnp.bfloat16)
        near, across, extra = pl.pallas_call(
            pack_kernel,
            out_shape=(like(total_rows), like(TILE + EXTRA), like(EXTRA)),
            in_specs=[ANY, SMEM, VMEM, VMEM, VMEM, VMEM, VMEM],
            out_specs=(VMEM,) * 3,
            scratch_shapes=[
                pltpu.VMEM((total_rows, block_arcs), jnp.bfloat16),
                pltpu.SemaphoreType.DMA((total_rows // TILE,)),
            ],
            compiler_params=limit(8),
            name="pack",
        )(coupling, incidence, row(arc_cost), row(capacity), demand, weights.reshape(1, 1), slots)
        brought = bring(coupling, across, extra)
        square = jax.ShapeDtypeStruct((block_arcs, total_rows), jnp.bfloat16)
        ready = pl.pallas_call(
            ready_kernel,
            out_shape=(square, like(total_rows), square),
            in_specs=[VMEM] * 5,
            out_specs=(VMEM,) * 3,
            compiler_params=limit(8),
            name="ready",
        )(near, *brought[:4])
        outs = pl.pallas_call(
            whole_kernel,
            out_shape=out_shape,
            in_specs=[VMEM] * (len(brought) + 5),
            out_specs=out_specs,
            scratch_shapes=[
                pltpu.VMEM((blocks - 2, total_rows, block_arcs), jnp.bfloat16),
                pltpu.VMEM((blocks - 2, block_arcs, total_rows), jnp.bfloat16),
                pltpu.VMEM((1, arcs), jnp.float32),
                pltpu.VMEM((1, arcs), jnp.float32),
                pltpu.VMEM((1, arcs), jnp.float32),
                pltpu.VMEM((scenarios, total_rows), jnp.float32),
                pltpu.VMEM((scenarios, total_rows), jnp.float32),
                pltpu.VMEM((scenarios, 128), jnp.float32),
                *state,
            ],
            compiler_params=limit(16),
            cost_estimate=cost,
            name="whole",
        )(near, *ready, *brought, slots)
    else:
        masked = (
            coupling.reshape(total_rows // TILE, TILE, block_arcs // TILE, TILE)
            * incidence.astype(jnp.bfloat16)[:, None, :, None]
        ).reshape(total_rows, block_arcs)
        masked = lax.all_gather(masked, "arc")
        own_mask = jnp.zeros((block_arcs,), jnp.float32).at[fleet_slots].set(1.0)
        per_arc = lax.all_gather(jnp.stack([arc_cost, capacity, own_mask]), "arc", axis=1, tiled=True)
        shares = jnp.broadcast_to(weights.astype(jnp.float32)[:, None], (1, 128))
        per_scen = lax.all_gather(jnp.concatenate([demand, shares], axis=1), "scen", tiled=True)
        outs = pl.pallas_call(
            plain_kernel,
            out_shape=out_shape,
            in_specs=[VMEM] * 7,
            out_specs=out_specs,
            scratch_shapes=state,
            compiler_params=limit(48),
            cost_estimate=cost,
            name="whole",
        )(masked, per_arc[0:1], per_arc[1:2], per_arc[2:3], per_scen[:, :total_rows],
          per_scen[:, total_rows:], slots)
    flows, duals, multipliers, consensus, spread = outs
    return flows, duals, multipliers, consensus.reshape(-1), spread.reshape(-1)


def solution(mesh):
    in_specs = (
        P(None, "arc"),
        P(None, "arc"),
        P("arc"),
        P("arc"),
        P("scen", None),
        P("scen"),
        P("arc"),
    )
    out_specs = (P("scen", "arc"), P("scen", "arc"), P("scen", "arc"), P("arc"), P())
    return jax.shard_map(body, mesh=mesh, in_specs=in_specs, out_specs=out_specs, check_vma=False)
```
